256 devices in a mesh: grp: 16 (over z_lo, x), tp: 16 (over z_hi, y, core).
Axes of the slice: x: 4, y: 4, z: 8 (z_hi: 2, z_lo: 4; z = z_hi * 4 + z_lo), core: 2. Of those that a mesh axis runs over, the one named last changes fastest.
Arguments:
- inputs: bfloat16 [4, 512, 8192], P(None, 'grp'), may hold values from -6 to 6
- norm_gain: bfloat16 [8192], replicated, may hold values from 0.5 to 1.5
- w_query: bfloat16 [8192, 8, 512], P(None, None, 'tp')
- w_keyval: bfloat16 [8192, 2, 512], P(None, None, 'tp')
- w_out: bfloat16 [8, 512, 8192], P(None, 'tp'), may hold values from -1.5 to 1.5
- kv_cache: bfloat16 [2, 512, 512, 512], P(None, 'grp', 'tp'), may hold values from -127 to 127, as said below
- kv_scales: bfloat16 [2, 512, 16, 512], P(None, 'grp', 'tp'), may hold values from 0.004 to 1.2
- ancestors: int32 [512], replicated, may hold values from 0 to 511, as said below
Outputs:
- attn_out: bfloat16 [4, 512, 8192], P(None, 'grp', 'tp')
The draws below stay inside these ranges and needn't reach their ends.
Inputs may be any that keep to these rules, and one draw needn't show every extreme that they name: Particle p takes over the cache of particle ancestors[p]. Among the 32 particles of one group, at most 4 have ancestors in any one group (their own included), and exactly 4 in some group. `kv_cache`: whole numbers.
All inputs are finite; a program needn't handle non-finite values.
Results may differ from the reference program's by a relative error of at most 0.015.
The reference program's roundings to bfloat16 on the way count: a program that leaves them out, or rounds other values in their place, can miss the bound.
Values may be sent and summed in bfloat16 or wider, within the bound.
A program may use at most 128 MiB of HBM per device.

```python
import jax
import jax.numpy as jnp
from jax import lax

D = 8192
HD = 128
KVH = 4
GQ = 8
S = 4
L = 512
PART = 32
KVW = 512
NB = 16
CAP = 4
PTOT = 512
N_GRP = 16


def projection_base(key):
    keys = jax.random.split(key, 1)
    gauss = jnp.clip(jax.random.normal(keys[0], (D, GQ, KVW), jnp.float32), -5.0, 5.0)
    return gauss * D ** (-0.5)


def draw_w_query(key, part):
    base = projection_base(key)
    return base.astype(jnp.bfloat16)


def draw_w_keyval(key, part):
    base = projection_base(key)
    key = jax.random.fold_in(key, 14)
    keys = jax.random.split(key, 3)
    summed = base[:, 0]
    for head_number in range(1, GQ):
        summed = summed + base[:, head_number]
    key_gauss = jnp.clip(jax.random.normal(keys[0], (D, KVW), jnp.float32), -5.0, 5.0)
    value_gauss = jnp.clip(jax.random.normal(keys[2], (D, KVW), jnp.float32), -5.0, 5.0)
    key_noise = key_gauss * D ** (-0.5)
    value_part = value_gauss * D ** (-0.5)
    key_part = GQ ** (-0.5) * summed + key_noise
    return jnp.stack([key_part, value_part], 1).astype(jnp.bfloat16)


def draw_ancestors(key, part):
    key = jax.random.fold_in(key, 11)
    group_count = PTOT // PART
    keys = jax.random.split(key, 6)
    popular = jax.random.permutation(keys[0], group_count)
    favoured = jnp.zeros((group_count,), jnp.int32).at[popular[0]].set(2).at[popular[1]].set(1)
    entries = group_count * CAP
    source_of = jnp.arange(entries) // CAP
    noise_values = jax.random.randint(keys[1], (group_count, entries), 0, 65536)
    rankings = (favoured[source_of][None, :] * 65536 + noise_values) * entries + jnp.arange(entries)[None, :]
    chosen = lax.top_k(rankings, PART)[1]
    shuffle = jnp.argsort(jax.random.randint(keys[2], (group_count, PART), 0, 65536) * PART + jnp.arange(PART)[None, :], axis=1)
    chosen = jnp.take_along_axis(chosen, shuffle, axis=1)
    sources = source_of[chosen]
    first_pick = jax.random.randint(keys[3], (group_count, PART), 0, PART)
    second_pick = jax.random.randint(keys[4], (group_count, PART), 0, PART)
    shift_by = jax.random.randint(keys[5], (group_count,), 0, PART)
    slot_ids = (first_pick * second_pick // PART + shift_by[sources]) % PART
    return (sources * PART + slot_ids).reshape(-1).astype(jnp.int32)


def draw_kv_cache(key, part):
    key = jax.random.fold_in(key, 12)
    whole = jax.random.randint(key, (2, PTOT, KVW, L), -127, 128)
    return whole.astype(jnp.bfloat16)


def draw_kv_scales(key, part):
    key = jax.random.fold_in(key, 13)
    keys = jax.random.split(key, 1)
    shape_all = (2, PTOT, NB, L)
    spread = jax.random.uniform(keys[0], shape_all, jnp.float32)
    values = 0.0041 * jnp.exp(spread * jnp.log(10.0))
    return values.astype(jnp.bfloat16)


def levels(rng, dims, cuts, smallest, high):
    gain, own = 1.0, jax.random.fold_in(rng, 6)
    for axis_at, shards_of in cuts:
        heights = jnp.exp(jax.random.uniform(jax.random.fold_in(own, axis_at), (shards_of,), jnp.float32, smallest / len(cuts), high / len(cuts)))
        gain = gain * jnp.repeat(heights, dims[axis_at] // shards_of).reshape([-1 if axis == axis_at else 1 for axis in range(len(dims))])
    return gain


def gaussian(stream_key, dims, scale, most, cuts=(), dtype=jnp.bfloat16):
    drawn = jax.random.normal(stream_key, dims, jnp.float32) * scale
    if len(cuts) > 0:
        drawn = levels(stream_key, dims, cuts, -0.22, 0.18) * drawn
    return jnp.clip(drawn, min=-most, max=most).astype(dtype)


def setup_inputs(seed: int = 0) -> dict:
    arg_keys = jax.random.split(jax.random.key(seed), 9)
    inputs = gaussian(arg_keys[0], (S, PTOT, D), 1.0, 6.0, ((1, 16),))
    norm_gain = jnp.clip(1.0 + 0.1 * jax.random.normal(arg_keys[1], (D,), jnp.float32), 0.5, 1.5).astype(jnp.bfloat16)
    w_query = draw_w_query(jax.random.fold_in(arg_keys[8], 71), 0)
    w_keyval = draw_w_keyval(jax.random.fold_in(arg_keys[8], 71), 0)
    w_out = gaussian(arg_keys[4], (GQ, KVW, D), 0.25, 1.5, ((1, 16),))
    kv_cache = draw_kv_cache(jax.random.fold_in(arg_keys[8], 71), 0)
    kv_scales = draw_kv_scales(jax.random.fold_in(arg_keys[8], 71), 0)
    ancestors = draw_ancestors(jax.random.fold_in(arg_keys[8], 71), 0)
    return dict(inputs=inputs, norm_gain=norm_gain, w_query=w_query, w_keyval=w_keyval, w_out=w_out, kv_cache=kv_cache, kv_scales=kv_scales, ancestors=ancestors)


def rotate_pairs(values, offset, step_count, cached):
    length = values.shape[-1]
    blocks = length // 32
    block_ids = offset // 32 + jnp.arange(blocks)
    within = jnp.arange(16)
    pair_index = (block_ids % (HD // 32))[:, None] * 16 + within[None, :]
    frequency = jnp.exp(-(pair_index.astype(jnp.float32) / (HD // 2)) * jnp.log(jnp.float32(500000.0)))
    positions = (cached + jnp.arange(step_count)).astype(jnp.float32)
    angles = positions[:, None, None] * frequency[None]
    ones_shape = (1,) * (values.ndim - 2)
    cosine = jnp.cos(angles).reshape((step_count,) + ones_shape + (blocks, 16))
    sine_part = jnp.sin(angles).reshape((step_count,) + ones_shape + (blocks, 16))
    shaped = values.reshape(values.shape[:-1] + (blocks, 2, 16))
    front_half = shaped[..., 0, :]
    back_half = shaped[..., 1, :]
    new_front = front_half * cosine - back_half * sine_part
    new_back = back_half * cosine + front_half * sine_part
    return jnp.stack([new_front, new_back], -2).reshape(values.shape)

def softmax_parts(cache_scores, new_scores):
    step_count = new_scores.shape[0]
    visible = jnp.arange(step_count)[None, :] <= jnp.arange(step_count)[:, None]
    visible = visible.reshape((step_count,) + (1,) * (new_scores.ndim - 2) + (step_count,))
    masked = jnp.where(visible, new_scores, -jnp.inf)
    highest = jnp.maximum(lax.optimization_barrier(jnp.max(cache_scores, -1, keepdims=True)), lax.optimization_barrier(jnp.max(masked, -1, keepdims=True)))
    cache_exp = jnp.exp(cache_scores - highest)
    new_exp = jnp.exp(masked - highest)
    total = lax.optimization_barrier(jnp.sum(cache_exp, -1, keepdims=True)) + lax.optimization_barrier(jnp.sum(new_exp, -1, keepdims=True))
    return ((cache_exp / total).astype(jnp.bfloat16), (new_exp / total).astype(jnp.bfloat16))

def reference(inputs, norm_gain, w_query, w_keyval, w_out, kv_cache, kv_scales, ancestors):
    floats = inputs.astype(jnp.float32)
    normed = (floats * lax.rsqrt(lax.optimization_barrier(jnp.mean(floats * floats, axis=-1, keepdims=True)) + 1e-05) * norm_gain.astype(jnp.float32)).astype(jnp.bfloat16)
    query = jnp.einsum('spd,dgf->spgf', normed.astype(jnp.float32), w_query.astype(jnp.float32))
    query = (rotate_pairs(query, 0, S, L) * HD ** (-0.5)).astype(jnp.bfloat16)
    keyval = jnp.einsum('spd,dcf->spcf', normed.astype(jnp.float32), w_keyval.astype(jnp.float32))
    new_key = rotate_pairs(keyval[:, :, 0], 0, S, L).astype(jnp.bfloat16)
    new_value = keyval[:, :, 1].astype(jnp.bfloat16)
    cache = jnp.take(kv_cache, ancestors, axis=1)
    scale = jnp.take(kv_scales, ancestors, axis=1)
    out_weight = w_out.astype(jnp.float32)
    per_head = NB // KVH

    def by_group(array, axis_pos):
        shape = array.shape
        split = shape[:axis_pos] + (N_GRP, PART) + shape[axis_pos + 1:]
        return jnp.moveaxis(array.reshape(split), axis_pos, 0)

    def attend(block):
        query_b, key_b, value_b, cache_b, scale_b = block
        key_ints = cache_b[0].astype(jnp.float32).reshape(PART, NB, 32, L)
        q_blocks = query_b.astype(jnp.float32).reshape(S, PART, GQ, NB, 32)
        partial_value = jnp.einsum('spgnf,pnfl->spgnl', q_blocks, key_ints)
        partial_value = partial_value * scale_b[0].astype(jnp.float32)[None, :, None]
        cache_scores = lax.optimization_barrier(jnp.sum(partial_value.reshape(S, PART, GQ, KVH, per_head, L), axis=4))
        q_heads = query_b.astype(jnp.float32).reshape(S, PART, GQ, KVH, HD)
        k_heads = key_b.astype(jnp.float32).reshape(S, PART, KVH, HD)
        new_scores = jnp.einsum('spghf,tphf->spght', q_heads, k_heads)
        cache_probs, new_probs = softmax_parts(cache_scores, new_scores)
        value_scale = scale_b[1].astype(jnp.float32).reshape(1, PART, 1, KVH, per_head, L)
        weighted = (cache_probs.astype(jnp.float32).reshape(S, PART, GQ, KVH, 1, L) * value_scale).astype(jnp.bfloat16)
        value_ints = cache_b[1].astype(jnp.float32).reshape(PART, KVH, per_head, 32, L)
        from_cache = jnp.einsum('spghnl,phnfl->spghnf', weighted.astype(jnp.float32), value_ints)
        from_cache = from_cache.reshape(S, PART, GQ, KVW)
        v_heads = value_b.astype(jnp.float32).reshape(S, PART, KVH, HD)
        from_new = jnp.einsum('spght,tphf->spghf', new_probs.astype(jnp.float32), v_heads).reshape(S, PART, GQ, KVW)
        mixed = (from_cache + from_new).astype(jnp.bfloat16)
        return jnp.einsum('spgf,gfd->spd', mixed.astype(jnp.float32), out_weight).astype(jnp.bfloat16)
    results = lax.map(attend, (by_group(query, 1), by_group(new_key, 1), by_group(new_value, 1), by_group(cache, 1), by_group(scale, 1)))
    return jnp.moveaxis(results, 0, 1).reshape(S, PTOT, D)
```

```python
import functools

import jax
import jax.numpy as jnp
import numpy as np
from jax import lax
from jax.experimental import pallas as pl
from jax.experimental.pallas import tpu as pltpu
from jax.sharding import PartitionSpec as P

HD = 128
CAP = 4
MESH = pl.DeviceIdType.MESH
F32 = jnp.float32
BF16 = jnp.bfloat16
MAX_CHUNKS = 4
BLOCKS = ((0, 2), (1, 2), (0, 1), (1, 3), (0, 3), (1, 1), (0, 0), (1, 0))


def flip(t, bit):
    return t + bit - 2 * bit * ((t // bit) % 2)


def mate(t, offset):
    if offset & 1:
        t = flip(t, 1)
    if offset & 2:
        t = flip(t, 2)
    return t


def nt(a, b):
    return lax.dot_general(a, b, (((1,), (1,)), ((), ())), preferred_element_type=F32)


def nn(a, b):
    return jnp.dot(a, b, preferred_element_type=F32)


def iota(shape, axis):
    return lax.broadcasted_iota(jnp.int32, shape, axis)


def kernel(
    ng, x_hbm, gain_ref, wq_hbm, wkv_hbm, wo_hbm, kv_hbm, sc_hbm, rope_ref, child_ref, col_ref, ids_ref,
    out_ref,
    xv, wv, wov, accq, qt, onehot, spread, sendq, qx, kx, vx, scx, scf, prob, pnew, stat, st_send, st_recv,
    fac, acc, ra, sb, rb, mix, back, fold, ta_send, ta_recv, own, tb_send, tb_recv, fin, tc_send, tc_recv,
    loc_sem, kv_ssem, kv_rsem, qa_ssem, qa_rsem, qg_ssem, qg_rsem, st_ssem, st_rsem, ha_ssem, ha_rsem,
    hb_ssem, hb_rsem, bk_ssem, bk_rsem, ta_ssem, ta_rsem, tb_ssem, tb_rsem, tc_ssem, tc_rsem,
):
    g = lax.axis_index("grp")
    t = lax.axis_index("tp")
    i = t % 4
    core = t % 2
    yb = (t // 2) % 2
    y = (t // 2) % 4
    zh = t // 8
    width = x_hbm.shape[1]
    cb = out_ref.shape[1]
    chunks = min(MAX_CHUNKS, ng)
    per = ng // chunks

    loads = [
        pltpu.make_async_copy(x_hbm, xv, loc_sem.at[0]),
        pltpu.make_async_copy(wq_hbm, wv.at[pl.ds(0, 256)], loc_sem.at[1]),
        pltpu.make_async_copy(wkv_hbm, wv.at[pl.ds(256, 64)], loc_sem.at[2]),
        pltpu.make_async_copy(wo_hbm, wov, loc_sem.at[3]),
    ]
    for copy in loads[:3]:
        copy.start()

    barrier = pltpu.get_barrier_semaphore()
    tp_peers = [mate(t, 1), mate(t, 2), mate(t, 3), t + 2 * ((y + 3 - 2 * (y % 2)) % 4 - y), flip(t, 8)]

    def greet(k, _):
        pl.semaphore_signal(barrier, inc=1, device_id={"grp": lax.rem(g + k, ng)}, device_id_type=MESH)
        return 0

    for peer in tp_peers:
        pl.semaphore_signal(barrier, inc=1, device_id={"tp": peer}, device_id_type=MESH)
    lax.fori_loop(1, ng, greet, 0)
    pl.semaphore_wait(barrier, len(tp_peers) + ng - 1)

    def cache_copies(offset):
        other = mate(t, offset)
        lanes = pl.ds(pl.multiple_of(128 * (other % 4), 128), 128)
        o = offset - 1
        args = dict(device_id={"tp": other}, device_id_type=MESH)
        return [
            pltpu.make_async_remote_copy(
                kv_hbm.at[0, :, :, lanes], kx.at[i], kv_ssem.at[o, 0], kv_rsem.at[o, 0], **args),
            pltpu.make_async_remote_copy(
                sc_hbm.at[:, :, lanes], scx.at[i], kv_ssem.at[o, 1], kv_rsem.at[o, 1], **args),
            pltpu.make_async_remote_copy(
                kv_hbm.at[1, :, :, lanes], vx.at[i], kv_ssem.at[o, 2], kv_rsem.at[o, 2], **args),
        ]

    cache_moves = [cache_copies(o) for o in (1, 2, 3)]
    for kind in range(3):
        for o in (2, 1, 0):
            cache_moves[o][kind].start()
    mine = pl.ds(pl.multiple_of(128 * i, 128), 128)
    own_cache = [
        pltpu.make_async_copy(kv_hbm.at[0, :, :, mine], kx.at[i], loc_sem.at[4]),
        pltpu.make_async_copy(sc_hbm.at[:, :, mine], scx.at[i], loc_sem.at[5]),
        pltpu.make_async_copy(kv_hbm.at[1, :, :, mine], vx.at[i], loc_sem.at[6]),
    ]
    for copy in own_cache:
        copy.start()
    loads[3].start()

    rows = ng * 16
    row = iota((rows, 128), 0)
    lane = iota((rows, 128), 1)
    for c in range(CAP):
        hit = (child_ref[:, c : c + 1] == lane % 32) & (row % 4 == lane // 32)
        for gl in range(4):
            block = jnp.where(hit & ((row // 4) % 4 == gl), 1.0, 0.0).astype(BF16)
            onehot[:, (c * 4 + gl) * 128 : (c * 4 + gl + 1) * 128] = block
    spread[...] = jnp.zeros_like(spread)

    loads[0].wait()
    step = min(1024, width)

    def squares(k, total):
        part = xv[:, pl.ds(pl.multiple_of(k * step, step), step)].astype(F32)
        return total + jnp.sum(part * part, axis=1, keepdims=True)

    total = lax.fori_loop(0, width // step, squares, jnp.zeros((128, 1), F32))
    inv = lax.rsqrt(total / width + 1e-05)
    loads[1].wait()
    loads[2].wait()
    accq[...] = jnp.zeros_like(accq)

    def project(k, _):
        part = pl.ds(pl.multiple_of(k * step, step), step)
        normed = (xv[:, part].astype(F32) * inv * gain_ref[:, part]).astype(BF16)
        accq[...] += nt(wv[:, part], normed)
        return 0

    lax.fori_loop(0, width // step, project, 0)
    cosine = rope_ref[0, i]
    sine = rope_ref[1, i]
    for b in range(9):
        front = accq[32 * b : 32 * b + 16, :]
        rear = accq[32 * b + 16 : 32 * b + 32, :]
        new_front = front * cosine - rear * sine
        new_rear = rear * cosine + front * sine
        if b < 8:
            new_front = new_front * HD ** (-0.5)
            new_rear = new_rear * HD ** (-0.5)
        qt[32 * b : 32 * b + 16, :] = new_front.astype(BF16)
        qt[32 * b + 16 : 32 * b + 32, :] = new_rear.astype(BF16)
    qt[288:320, :] = accq[288:320, :].astype(BF16)

    for third in range(3):
        for c in range(CAP):
            for gl in range(4):
                at = pl.ds((c * 4 + gl) * 128, 128)
                b = third * 4 + gl
                if b < 10:
                    spread[32 * c : 32 * c + 32, at] = qt[32 * b : 32 * b + 32, :]
                else:
                    spread[32 * c : 32 * c + 32, at] = jnp.zeros((32, 128), BF16)
        packed = nt(onehot[...], spread[...]).astype(BF16)
        sendq[:, 16 * third : 16 * third + 16, :] = packed.reshape(ng, 16, 128)

    def q_copy(k):
        there = lax.rem(g + k, ng)
        return pltpu.make_async_remote_copy(
            sendq.at[there], qx.at[i, g], qa_ssem.at[k], qa_rsem.at[k],
            device_id={"grp": there}, device_id_type=MESH)

    def q_start(k, _):
        q_copy(k).start()
        return 0

    def q_wait(k, _):
        q_copy(k).wait_recv()
        return 0

    def q_sent(k, _):
        q_copy(k).wait_send()
        return 0

    lax.fori_loop(1, ng, q_start, 0)
    qx[i, g] = sendq[g]
    lax.fori_loop(1, ng, q_wait, 0)
    q_shares = [
        pltpu.make_async_remote_copy(
            qx.at[i], qx.at[i], qg_ssem.at[o - 1], qg_rsem.at[o - 1],
            device_id={"tp": mate(t, o)}, device_id_type=MESH)
        for o in (1, 2, 3)
    ]
    for o in (2, 1, 0):
        q_shares[o].start()

    fold_row = iota(fold.shape, 0)
    fold_lane = iota(fold.shape, 1)
    fold[...] = jnp.where(
        (fold_row // 128 == fold_lane // 32) & (fold_row % 32 == fold_lane % 32), 1.0, 0.0).astype(BF16)
    row = iota((128, 128), 0)
    lane = iota((128, 128), 1)
    diagonal = jnp.where(row // 32 == lane // 32, 1.0, 0.0).astype(BF16)
    stat[...] = jnp.zeros_like(stat)

    for kind in (0, 1):
        own_cache[kind].wait()
        for o in range(3):
            cache_moves[o][kind].wait_recv()
    scf[...] = scx[...].astype(F32)
    for o in range(3):
        q_shares[o].wait_recv()

    def slots(k):
        there = lax.rem(g + k, ng)
        return there, [ids_ref[there * CAP + c] for c in range(CAP)]

    def scale_rows(n, kind, ids):
        return jnp.concatenate(
            [jnp.broadcast_to(scf[n, kind, pl.ds(ids[c], 1), :], (32, 128)) for c in range(CAP)], axis=0)

    def score(k, _):
        there, ids = slots(k)
        total = jnp.zeros((128, 128), F32)
        for n in range(4):
            q = qx[n, there, 0:32, :]
            left = jnp.concatenate([q] * CAP, axis=0) * diagonal
            keys = jnp.concatenate([kx[n, ids[c]] for c in range(CAP)], axis=0)
            total = total + nn(left, keys) * scale_rows(n, 0, ids)
        pnew[k] = jnp.full((128, 16), -jnp.inf, F32)

        @pl.when(there % 4 == i)
        def _():
            new = jnp.zeros((128, 16), F32)
            for n in range(4):
                q = qx[n, there, 0:32, :]
                left = jnp.concatenate([q] * CAP, axis=0) * diagonal
                new = new + nt(left, qx[n, there, 32:48, :])
            column = iota((128, 16), 1)
            seen = (column <= iota((128, 16), 0) % 4) & (column < 4)
            pnew[k] = jnp.where(seen, new, -jnp.inf)

        new = pnew[k]
        top = jnp.maximum(jnp.max(total, axis=1, keepdims=True), jnp.max(new, axis=1, keepdims=True))
        part = jnp.exp(total - top)
        new = jnp.exp(new - top)
        prob[k] = part
        pnew[k] = new
        mass = jnp.sum(part, axis=1, keepdims=True) + jnp.sum(new, axis=1, keepdims=True)
        stat[...] = jnp.where(lane == k, top, jnp.where(lane == ng + k, mass, stat[...]))
        return 0

    lax.fori_loop(0, ng, score, 0)

    st_send[...] = jnp.transpose(stat[...])[0 : 2 * ng, :]
    st_moves = [
        pltpu.make_async_remote_copy(
            st_send, st_recv.at[o - 1], st_ssem.at[o - 1], st_rsem.at[o - 1],
            device_id={"tp": mate(t, o)}, device_id_type=MESH)
        for o in (1, 2, 3)
    ]
    for o in (2, 1, 0):
        st_moves[o].start()
    for o in range(3):
        st_moves[o].wait_recv()
    tops = [st_send[0:ng, :]] + [st_recv[o, 0:ng, :] for o in range(3)]
    masses = [st_send[ng : 2 * ng, :]] + [st_recv[o, ng : 2 * ng, :] for o in range(3)]
    top = jnp.maximum(jnp.maximum(tops[0], tops[1]), jnp.maximum(tops[2], tops[3]))
    mass = sum(masses[o] * jnp.exp(tops[o] - top) for o in range(4))
    factor = jnp.exp(tops[0] - top) / mass
    fac[...] = jnp.transpose(jnp.concatenate([factor, jnp.zeros((128 - ng, 128), F32)], axis=0))

    own_cache[2].wait()
    for o in range(3):
        cache_moves[o][2].wait_recv()

    def head_first(q):
        at = pl.ds(q * per, per)
        return [
            pltpu.make_async_remote_copy(
                acc.at[1 - core + 2 * b, at], ra.at[b, at], ha_ssem.at[q, b], ha_rsem.at[q, b],
                device_id={"tp": mate(t, 1)}, device_id_type=MESH)
            for b in range(2)
        ]

    def head_second(q):
        at = pl.ds(q * per, per)
        return pltpu.make_async_remote_copy(
            sb.at[at], rb.at[at], hb_ssem.at[q], hb_rsem.at[q],
            device_id={"tp": mate(t, 2)}, device_id_type=MESH)

    def value(k, _):
        there, ids = slots(k)
        column = jnp.sum(jnp.where(lane == k, fac[...], 0.0), axis=1, keepdims=True)
        p = (prob[k] * column).astype(BF16).astype(F32)

        def keep(out):
            kept = jnp.zeros((32, 128), F32)
            for c in range(CAP):
                kept = kept + jnp.where(lane[0:32] // 32 == c, out[32 * c : 32 * c + 32, :], 0.0)
            return kept

        for n in range(4):
            weighted = (p * scale_rows(n, 1, ids)).astype(BF16)
            values = jnp.concatenate([vx[n, ids[c]] for c in range(CAP)], axis=0)
            acc[n, k] = keep(nt(weighted, values))

        @pl.when(there % 4 == i)
        def _():
            pn = (pnew[k] * column).astype(BF16)
            for n in range(4):
                both = qx[n, there, 32:48, :].astype(F32)
                new_values = pltpu.roll(both, 12, 0).astype(BF16)
                acc[n, k] += keep(nn(pn, new_values))

        return 0

    for q in range(chunks):
        lax.fori_loop(q * per, (q + 1) * per, value, 0)
        for copy in head_first(q):
            copy.start()
    for q in range(chunks):
        for copy in head_first(q):
            copy.wait()
        at = pl.ds(q * per, per)
        sb[at] = acc[2 * (1 - yb) + core, at] + ra[1 - yb, at]
        head_second(q).start()

    def back_copy(k):
        there = lax.rem(g + k, ng)
        return pltpu.make_async_remote_copy(
            mix.at[k], back.at[g], bk_ssem.at[k], bk_rsem.at[k],
            device_id={"grp": there}, device_id_type=MESH)

    def back_start(k, _):
        back_copy(k).start()
        return 0

    def back_wait(k, _):
        back_copy(k).wait()
        return 0

    for q in range(chunks):
        head_second(q).wait()
        at = pl.ds(q * per, per)
        mix[at] = (acc[i, at] + ra[yb, at] + rb[at]).astype(BF16)
        lax.fori_loop(max(q * per, 1), (q + 1) * per, back_start, 0)
    back[g] = mix[0]
    lax.fori_loop(1, ng, back_wait, 0)

    wide = 32 * ng
    row = iota((128, wide), 0)
    lane_w = iota((128, wide), 1)
    hit = (lane_w // 32 == col_ref[:, 0:1]) & (lane_w % 4 == row // 32)
    chosen = col_ref[:, 1:2] == lane // 32
    slots_all = back[...].reshape(wide, 128)
    mixed = jnp.zeros((128, 256), F32)
    for b in range(8):
        pick = jnp.where(hit & ((lane_w // 4) % 8 == b), 1.0, 0.0).astype(BF16)
        rows_b = jnp.where(chosen, nn(pick, slots_all), 0.0).astype(BF16)
        mixed = mixed + nn(rows_b, fold[128 * b : 128 * b + 128, :])
    mixed = mixed.astype(BF16)

    loads[3].wait()

    def columns(e, c):
        half, dy = BLOCKS[e]
        block = half * 8 + lax.rem(y + dy, 4) * 2 + c
        return pl.ds(pl.multiple_of(block * cb, 128), cb)

    def ta_copy(e):
        return pltpu.make_async_remote_copy(
            ta_send.at[e], ta_recv.at[e], ta_ssem.at[e], ta_rsem.at[e],
            device_id={"tp": mate(t, 1)}, device_id_type=MESH)

    for e in range(8):
        ta_send[e] = nn(mixed, wov[:, columns(e, 1 - core)]).astype(BF16)
        ta_copy(e).start()
    for e in range(8):
        own[e] = nn(mixed, wov[:, columns(e, core)])

    before = t + 2 * ((y + 3) % 4 - y)
    after = t + 2 * ((y + 1) % 4 - y)
    targets = (before, after, after, before, before, after)

    def tb_copy(e):
        return pltpu.make_async_remote_copy(
            tb_send.at[e], tb_recv.at[e], tb_ssem.at[e], tb_rsem.at[e],
            device_id={"tp": targets[e]}, device_id_type=MESH)

    for e in range(8):
        ta_copy(e).wait()
        summed = own[e] + ta_recv[e].astype(F32)
        if e < 4:
            tb_send[e] = summed.astype(BF16)
            tb_copy(e).start()
        elif e < 6:
            tb_copy(e - 4).wait()
            tb_send[e] = (summed + tb_recv[e - 4].astype(F32)).astype(BF16)
            tb_copy(e).start()
        else:
            fin[e - 6] = summed
    for e in (2, 3, 4, 5):
        tb_copy(e).wait()
    fin[0] = fin[0] + tb_recv[2].astype(F32) + tb_recv[4].astype(F32)
    fin[1] = fin[1] + tb_recv[3].astype(F32) + tb_recv[5].astype(F32)
    tc_send[...] = fin[1 - zh].astype(BF16)
    tc_copy = pltpu.make_async_remote_copy(
        tc_send, tc_recv, tc_ssem.at[0], tc_rsem.at[0], device_id={"tp": flip(t, 8)}, device_id_type=MESH)
    tc_copy.start()
    tc_copy.wait()
    out_ref[...] = (fin[zh] + tc_recv[...].astype(F32)).astype(BF16)

    lax.fori_loop(1, ng, q_sent, 0)
    for o in range(3):
        for kind in range(3):
            cache_moves[o][kind].wait_send()
        q_shares[o].wait_send()
        st_moves[o].wait_send()


def rope_tables(step_count, cached, particles):
    pair = np.arange(64, dtype=np.float32).reshape(4, 16)
    frequency = np.exp(-(pair / np.float32(64)) * np.log(np.float32(500000.0))).astype(np.float32)
    positions = (cached + np.arange(step_count)).astype(np.float32)
    angles = (positions[None, None, :] * frequency[:, :, None]).astype(np.float32)
    tables = np.stack([np.cos(angles), np.sin(angles)]).astype(np.float32)
    return np.repeat(tables, particles, axis=-1)


def shards(ng, inputs, norm_gain, w_query, w_keyval, w_out, kv_cache, kv_scales, ancestors):
    step_count, particles, width = inputs.shape
    cached = kv_cache.shape[3]
    my_group = lax.axis_index("grp")
    parents = ancestors.reshape(ng, particles)
    source = parents // particles
    parent_slot = parents % particles
    p_ids = jnp.arange(particles)
    caps = jnp.arange(CAP)
    wanted = source == my_group
    place = jnp.sum(wanted[:, None, :] & (p_ids[None, None, :] < p_ids[None, :, None]), axis=2)
    at_slot = wanted[:, None, :] & (place[:, None, :] == caps[None, :, None])
    ids = jnp.sum(jnp.where(at_slot, parent_slot[:, None, :], 0), axis=2).reshape(-1)
    mine = lax.dynamic_index_in_dim(source, my_group, 0, keepdims=False)
    rank = jnp.sum((mine[:, None] == mine[None, :]) & (p_ids[None, :] < p_ids[:, None]), axis=1)
    here = (mine[None, None, :] == jnp.arange(ng)[:, None, None]) & (rank[None, None, :] == caps[None, :, None])
    child = jnp.max(jnp.where(here, p_ids[None, None, :], -1), axis=2)
    child = jnp.repeat(child, 16, axis=0)
    col = jnp.tile(jnp.stack([mine, rank], axis=1), (step_count, 1))

    rope = jnp.asarray(rope_tables(step_count, cached, particles))
    rows = step_count * particles
    cb = width // lax.axis_size("tp")
    vmem = pl.BlockSpec(memory_space=pltpu.VMEM)
    smem = pl.BlockSpec(memory_space=pltpu.SMEM)
    hbm = pl.BlockSpec(memory_space=pl.ANY)
    dma = pltpu.SemaphoreType.DMA
    scratch = [
        pltpu.VMEM((rows, width), BF16),
        pltpu.VMEM((320, width), BF16),
        pltpu.VMEM((256, width), BF16),
        pltpu.VMEM((320, 128), F32),
        pltpu.VMEM((320, 128), BF16),
        pltpu.VMEM((ng * 16, 2048), BF16),
        pltpu.VMEM((128, 2048), BF16),
        pltpu.VMEM((ng, 48, 128), BF16),
        pltpu.VMEM((4, ng, 48, 128), BF16),
        pltpu.VMEM((4, particles, 32, 128), BF16),
        pltpu.VMEM((4, particles, 32, 128), BF16),
        pltpu.VMEM((4, 2, particles, 128), BF16),
        pltpu.VMEM((4, 2, particles, 128), F32),
        pltpu.VMEM((ng, 128, 128), F32),
        pltpu.VMEM((ng, 128, 16), F32),
        pltpu.VMEM((128, 128), F32),
        pltpu.VMEM((2 * ng, 128), F32),
        pltpu.VMEM((3, 2 * ng, 128), F32),
        pltpu.VMEM((128, 128), F32),
        pltpu.VMEM((4, ng, 32, 128), F32),
        pltpu.VMEM((2, ng, 32, 128), F32),
        pltpu.VMEM((ng, 32, 128), F32),
        pltpu.VMEM((ng, 32, 128), F32),
        pltpu.VMEM((ng, 32, 128), BF16),
        pltpu.VMEM((ng, 32, 128), BF16),
        pltpu.VMEM((1024, 256), BF16),
        pltpu.VMEM((8, rows, cb), BF16),
        pltpu.VMEM((8, rows, cb), BF16),
        pltpu.VMEM((8, rows, cb), F32),
        pltpu.VMEM((6, rows, cb), BF16),
        pltpu.VMEM((6, rows, cb), BF16),
        pltpu.VMEM((2, rows, cb), F32),
        pltpu.VMEM((rows, cb), BF16),
        pltpu.VMEM((rows, cb), BF16),
        dma((7,)),
        dma((3, 3)), dma((3, 3)),
        dma((ng,)), dma((ng,)),
        dma((3,)), dma((3,)),
        dma((3,)), dma((3,)),
        dma((MAX_CHUNKS, 2)), dma((MAX_CHUNKS, 2)),
        dma((MAX_CHUNKS,)), dma((MAX_CHUNKS,)),
        dma((ng,)), dma((ng,)),
        dma((8,)), dma((8,)),
        dma((6,)), dma((6,)),
        dma((1,)), dma((1,)),
    ]
    out = pl.pallas_call(
        functools.partial(kernel, ng),
        out_shape=jax.ShapeDtypeStruct((rows, cb), BF16),
        in_specs=[hbm, vmem, hbm, hbm, hbm, hbm, hbm, vmem, vmem, vmem, smem],
        out_specs=vmem,
        scratch_shapes=scratch,
        compiler_params=pltpu.CompilerParams(
            collective_id=0, has_side_effects=True, vmem_limit_bytes=52 * 1024 * 1024),
    )(
        inputs.reshape(rows, width),
        norm_gain.astype(F32).reshape(1, width),
        jnp.transpose(w_query, (1, 2, 0)).reshape(256, width),
        jnp.transpose(w_keyval, (1, 2, 0)).reshape(64, width),
        w_out.reshape(256, width),
        kv_cache,
        kv_scales.reshape(2, particles, cached),
        rope,
        child.astype(jnp.int32),
        col.astype(jnp.int32),
        ids.astype(jnp.int32),
    )
    return out.reshape(step_count, particles, cb)


def solution(mesh):
    in_specs = (
        P(None, "grp", None),
        P(),
        P(None, None, "tp"),
        P(None, None, "tp"),
        P(None, "tp", None),
        P(None, "grp", "tp", None),
        P(None, "grp", "tp", None),
        P(),
    )
    out_specs = P(None, "grp", "tp")
    return jax.shard_map(
        functools.partial(shards, mesh.shape["grp"]), mesh=mesh, in_specs=in_specs, out_specs=out_specs,
        check_vma=False)
```

```python
import functools

import jax
import jax.numpy as jnp
import numpy as np
from jax import lax
from jax.experimental import pallas as pl
from jax.experimental.pallas import tpu as pltpu
from jax.sharding import PartitionSpec as P

HD = 128
CAP = 4
MESH = pl.DeviceIdType.MESH
F32 = jnp.float32
BF16 = jnp.bfloat16
MAX_CHUNKS = 4
PIECES = 4
EARLY = 1
BLOCKS = ((0, 2), (1, 2), (0, 1), (1, 3), (0, 3), (1, 1), (0, 0), (1, 0))


def flip(t, bit):
    return t + bit - 2 * bit * ((t // bit) % 2)


def mate(t, offset):
    if offset & 1:
        t = flip(t, 1)
    if offset & 2:
        t = flip(t, 2)
    return t


def nt(a, b):
    return lax.dot_general(a, b, (((1,), (1,)), ((), ())), preferred_element_type=F32)


def nn(a, b):
    return jnp.dot(a, b, preferred_element_type=F32)


def iota(shape, axis):
    return lax.broadcasted_iota(jnp.int32, shape, axis)


def kernel(
    ng, x_hbm, gain_hbm, wq_hbm, wkv_hbm, wo_hbm, kv_hbm, sc_hbm, rope_hbm, anc_hbm,
    out_ref,
    xv, wv, wov, gain_v, gain_f, rope, anc, ids_v, ids_s, src_col, rank_col,
    accq, qt, onehot, spread, sendq, qx, kn, kf, vn, vf, scx, scf, prob, pb, pnew, stat, st_send, st_recv,
    fac, acc, ra, sb, rb, mix, back, fold, ta_send, ta_recv, own, tb_send, tb_recv, fin, tc_send, tc_recv,
    loc_sem, k_ssem, k_rsem, v_ssem, v_rsem, qa_ssem, qa_rsem, qg_ssem, qg_rsem, st_ssem, st_rsem, ha_ssem,
    ha_rsem, hb_ssem, hb_rsem, bk_ssem, bk_rsem, ta_ssem, ta_rsem, tb_ssem, tb_rsem, tc_ssem, tc_rsem,
):
    g = lax.axis_index("grp")
    t = lax.axis_index("tp")
    i = t % 4
    core = t % 2
    y = (t // 2) % 4
    zh = t // 8
    width = x_hbm.shape[1]
    half = out_ref.shape[1] // 2
    chunks = min(MAX_CHUNKS, ng)
    per = ng // chunks
    block_of = [mate(t, o) % 4 for o in range(4)]
    core_of = [core, 1 - core, core, 1 - core]

    loads = [
        pltpu.make_async_copy(x_hbm, xv, loc_sem.at[0]),
        pltpu.make_async_copy(wq_hbm, wv.at[pl.ds(0, 256)], loc_sem.at[1]),
        pltpu.make_async_copy(wkv_hbm, wv.at[pl.ds(256, 64)], loc_sem.at[2]),
        pltpu.make_async_copy(wo_hbm, wov, loc_sem.at[3]),
        pltpu.make_async_copy(anc_hbm, anc.at[pl.ds(0, anc_hbm.shape[0])], loc_sem.at[4]),
        pltpu.make_async_copy(gain_hbm, gain_v, loc_sem.at[5]),
        pltpu.make_async_copy(rope_hbm.at[:, i], rope, loc_sem.at[6]),
    ]
    anc[...] = jnp.full(anc.shape, -1, jnp.int32)
    for n in (4, 0, 5, 6, 1, 2):
        loads[n].start()

    barrier = pltpu.get_barrier_semaphore()
    tp_peers = [mate(t, 1), mate(t, 2), mate(t, 3), t + 2 * ((y + 3 - 2 * (y % 2)) % 4 - y), flip(t, 8)]

    def greet(k, _):
        pl.semaphore_signal(barrier, inc=1, device_id={"grp": lax.rem(g + k, ng)}, device_id_type=MESH)
        return 0

    for peer in tp_peers:
        pl.semaphore_signal(barrier, inc=1, device_id={"tp": peer}, device_id_type=MESH)
    lax.fori_loop(1, ng, greet, 0)
    pl.semaphore_wait(barrier, len(tp_peers) + ng - 1)

    def lanes_of(block):
        return pl.ds(pl.multiple_of(128 * block, 128), 128)

    def key_copies(o):
        args = dict(device_id={"tp": mate(t, o)}, device_id_type=MESH)
        lanes = lanes_of(block_of[o])
        return [
            pltpu.make_async_remote_copy(
                kv_hbm.at[0, :, :, lanes], (kn if o == 1 else kf).at[core], k_ssem.at[o - 1, 0], k_rsem.at[o - 1, 0], **args),
            pltpu.make_async_remote_copy(
                sc_hbm.at[:, :, lanes], scx.at[i], k_ssem.at[o - 1, 1], k_rsem.at[o - 1, 1], **args),
        ]

    piece = kv_hbm.shape[1] // PIECES

    def value_copy(o, j):
        at = pl.ds(j * piece, piece)
        return pltpu.make_async_remote_copy(
            kv_hbm.at[1, at, :, lanes_of(block_of[o])], (vn if o == 1 else vf).at[core, at],
            v_ssem.at[o - 1, j], v_rsem.at[o - 1, j], device_id={"tp": mate(t, o)}, device_id_type=MESH)

    key_moves = {o: key_copies(o) for o in (1, 2, 3)}
    value_moves = [value_copy(o, j) for j in range(PIECES) for o in (2, 3)]
    near_values = [value_copy(1, j) for j in range(PIECES)]
    for o in (2, 3, 1):
        key_moves[o][1].start()
    for o in (2, 3, 1):
        key_moves[o][0].start()
    for move in near_values + value_moves[:EARLY]:
        move.start()
    own_cache = [
        pltpu.make_async_copy(kv_hbm.at[0, :, :, lanes_of(i)], kn.at[core], loc_sem.at[7]),
        pltpu.make_async_copy(sc_hbm.at[:, :, lanes_of(i)], scx.at[i], loc_sem.at[8]),
        pltpu.make_async_copy(kv_hbm.at[1, :, :, lanes_of(i)], vn.at[core], loc_sem.at[9]),
    ]
    for copy in own_cache:
        copy.start()
    loads[3].start()

    row = iota((128, 128), 0)
    lane = iota((128, 128), 1)

    def ones(where):
        return jnp.where(where, 1.0, 0.0).astype(BF16)

    loads[4].wait()
    parents = anc[...]
    source = parents >> 5
    wanted = source == g
    within = iota((8, 128), 1) % 32

    def running(v):
        for shift in (1, 2, 4, 8, 16):
            v = v + jnp.where(within >= shift, pltpu.roll(v, shift, 1), 0)
        return v

    place = running(wanted.astype(jnp.int32))
    ids = jnp.zeros((8, 128), jnp.int32)
    for c in range(CAP):
        at_slot = running(jnp.where(wanted & (place == c + 1), parents & 31, 0))
        ids = jnp.where(within == 32 - CAP + c, pltpu.roll(at_slot, (c + 1 - CAP) % 128, 1), ids)
    ids_v[...] = ids
    to_scalars = pltpu.make_async_copy(ids_v, ids_s, loc_sem.at[10])
    to_scalars.start()
    mine = jnp.sum(jnp.where(iota((8, 128), 0) == g // 4, source.astype(F32), 0.0), axis=0, keepdims=True)
    mine = nn(jnp.broadcast_to(mine, (8, 128)).astype(BF16), ones(row == (g % 4) * 32 + lane % 32))[0:1]
    mine = jnp.broadcast_to(mine, (128, 128))
    mine_col = jnp.transpose(mine)
    src_col[...] = mine_col
    rank = jnp.sum(jnp.where((mine == mine_col) & (row < lane % 32), 1.0, 0.0), axis=0, keepdims=True)
    rank_col[...] = jnp.transpose(jnp.broadcast_to(rank, (128, 128)))

    slot_row = iota((ng * 16, 128), 0)
    slot_lane = iota((ng * 16, 128), 1)
    hit = (mine[0:1] == (slot_row // 16).astype(F32)) & (slot_row % 4 == slot_lane // 32)
    for c in range(CAP):
        hit_c = hit & (rank == c)
        for gl in range(4):
            onehot[:, (c * 4 + gl) * 128 : (c * 4 + gl + 1) * 128] = ones(hit_c & ((slot_row // 4) % 4 == gl))
    spread[...] = jnp.zeros_like(spread)

    loads[5].wait()
    gain_f[...] = gain_v[...].astype(F32)
    loads[0].wait()
    step = min(1024, width)

    def squares(k, total):
        part = xv[:, pl.ds(pl.multiple_of(k * step, step), step)].astype(F32)
        return total + jnp.sum(part * part, axis=1, keepdims=True)

    total = lax.fori_loop(0, width // step, squares, jnp.zeros((128, 1), F32))
    inv = lax.rsqrt(total / width + 1e-05)
    loads[1].wait()
    loads[2].wait()
    accq[...] = jnp.zeros_like(accq)

    def project(k, _):
        part = pl.ds(pl.multiple_of(k * step, step), step)
        gains = gain_f[pl.ds(pl.multiple_of(k * (step // 128), 8), step // 128), :]
        gains = jnp.concatenate([gains[r : r + 1] for r in range(step // 128)], axis=1)
        normed = (xv[:, part].astype(F32) * inv * gains).astype(BF16)
        accq[...] += nt(wv[:, part], normed)
        return 0

    lax.fori_loop(0, width // step, project, 0)
    loads[6].wait()
    cosine = rope[0]
    sine = rope[1]
    for b in range(9):
        front = accq[32 * b : 32 * b + 16, :]
        rear = accq[32 * b + 16 : 32 * b + 32, :]
        new_front = front * cosine - rear * sine
        new_rear = rear * cosine + front * sine
        if b < 8:
            new_front = new_front * HD ** (-0.5)
            new_rear = new_rear * HD ** (-0.5)
        qt[32 * b : 32 * b + 16, :] = new_front.astype(BF16)
        qt[32 * b + 16 : 32 * b + 32, :] = new_rear.astype(BF16)
    qt[288:320, :] = accq[288:320, :].astype(BF16)

    for third in range(3):
        for c in range(CAP):
            for gl in range(4):
                at = pl.ds((c * 4 + gl) * 128, 128)
                b = third * 4 + gl
                if b < 10:
                    spread[32 * c : 32 * c + 32, at] = qt[32 * b : 32 * b + 32, :]
                else:
                    spread[32 * c : 32 * c + 32, at] = jnp.zeros((32, 128), BF16)
        packed = nt(onehot[...], spread[...]).astype(BF16)
        sendq[:, 16 * third : 16 * third + 16, :] = packed.reshape(ng, 16, 128)

    def q_copy(k):
        there = lax.rem(g + k, ng)
        return pltpu.make_async_remote_copy(
            sendq.at[there], qx.at[i, g], qa_ssem.at[k], qa_rsem.at[k],
            device_id={"grp": there}, device_id_type=MESH)

    def q_share(o, k):
        here = lax.rem(g - k + ng, ng)
        return pltpu.make_async_remote_copy(
            qx.at[i, here], qx.at[i, here], qg_ssem.at[o - 1, k], qg_rsem.at[o - 1, k],
            device_id={"tp": mate(t, o)}, device_id_type=MESH)

    def q_arrival(o, k):
        here = lax.rem(g - k + ng, ng)
        return pltpu.make_async_remote_copy(
            qx.at[i, here], qx.at[block_of[o], here], qg_ssem.at[o - 1, k], qg_rsem.at[o - 1, k],
            device_id={"tp": mate(t, o)}, device_id_type=MESH)

    def q_start(k, _):
        q_copy(k).start()
        return 0

    def q_forward(k, _):
        q_copy(k).wait_recv()
        for o in (2, 3, 1):
            q_share(o, k).start()
        return 0

    lax.fori_loop(1, ng, q_start, 0)
    qx[i, g] = sendq[g]
    for o in (2, 3, 1):
        q_share(o, 0).start()
    lax.fori_loop(1, ng, q_forward, 0)
    for move in value_moves[EARLY:]:
        move.start()

    fold_row = iota(fold.shape, 0)
    fold_lane = iota(fold.shape, 1)
    fold[...] = ones((fold_row // 128 == fold_lane // 32) & (fold_row % 32 == fold_lane % 32))
    diagonal = ones(row // 32 == lane // 32)
    stat[...] = jnp.zeros_like(stat)
    to_scalars.wait()

    def slots(k):
        there = lax.rem(g - k + ng, ng)
        return there, [ids_s[there // 4, (there % 4) * 32 + 32 - CAP + c] & 31 for c in range(CAP)]

    def scale_rows(n, kind, ids):
        return jnp.concatenate(
            [jnp.broadcast_to(scf[n, kind, pl.ds(ids[c], 1), :], (32, 128)) for c in range(CAP)], axis=0)

    def queries(n, there):
        return jnp.concatenate([qx[n, there, 0:32, :]] * CAP, axis=0) * diagonal

    def block_scores(o, there, ids):
        n = block_of[o]
        held = kn if o < 2 else kf
        keys = jnp.concatenate([held[core_of[o], ids[c]] for c in range(CAP)], axis=0)
        return nn(queries(n, there), keys) * scale_rows(n, 0, ids)

    own_cache[0].wait()
    own_cache[1].wait()
    for kind in (0, 1):
        key_moves[1][kind].wait_recv()
    key_moves[2][1].wait_recv()
    key_moves[3][1].wait_recv()
    scf[...] = scx[...].astype(F32)

    def score_near(k, _):
        q_arrival(1, k).wait_recv()
        there, ids = slots(k)
        prob[k] = block_scores(0, there, ids) + block_scores(1, there, ids)
        return 0

    lax.fori_loop(0, ng, score_near, 0)
    key_moves[2][0].wait_recv()
    key_moves[3][0].wait_recv()

    def score_far(k, _):
        q_arrival(2, k).wait_recv()
        q_arrival(3, k).wait_recv()
        there, ids = slots(k)
        total = prob[k] + block_scores(2, there, ids) + block_scores(3, there, ids)
        pnew[k] = jnp.full((128, 16), -jnp.inf, F32)

        @pl.when(there % 4 == i)
        def _():
            new = jnp.zeros((128, 16), F32)
            for n in range(4):
                new = new + nt(queries(n, there), qx[n, there, 32:48, :])
            column = iota((128, 16), 1)
            seen = (column <= iota((128, 16), 0) % 4) & (column < 4)
            pnew[k] = jnp.where(seen, new, -jnp.inf)

        new = pnew[k]
        top = jnp.maximum(jnp.max(total, axis=1, keepdims=True), jnp.max(new, axis=1, keepdims=True))
        part = jnp.exp(total - top)
        new = jnp.exp(new - top)
        prob[k] = part
        pnew[k] = new
        mass = jnp.sum(part, axis=1, keepdims=True) + jnp.sum(new, axis=1, keepdims=True)
        stat[...] = jnp.where(lane == k, top, jnp.where(lane == ng + k, mass, stat[...]))
        return 0

    lax.fori_loop(0, ng, score_far, 0)

    st_send[...] = jnp.transpose(stat[...])[0 : 2 * ng, :]
    st_moves = [
        pltpu.make_async_remote_copy(
            st_send, st_recv.at[o - 1], st_ssem.at[o - 1], st_rsem.at[o - 1],
            device_id={"tp": mate(t, o)}, device_id_type=MESH)
        for o in (1, 2, 3)
    ]
    for o in (2, 1, 0):
        st_moves[o].start()
    for o in range(3):
        st_moves[o].wait_recv()
    tops = [st_send[0:ng, :]] + [st_recv[o, 0:ng, :] for o in range(3)]
    masses = [st_send[ng : 2 * ng, :]] + [st_recv[o, ng : 2 * ng, :] for o in range(3)]
    top = jnp.maximum(jnp.maximum(tops[0], tops[1]), jnp.maximum(tops[2], tops[3]))
    mass = sum(masses[o] * jnp.exp(tops[o] - top) for o in range(4))
    factor = jnp.exp(tops[0] - top) / mass
    fac[...] = jnp.transpose(jnp.concatenate([factor, jnp.zeros((128 - ng, 128), F32)], axis=0))

    def keep(out):
        kept = jnp.zeros((32, 128), F32)
        for c in range(CAP):
            kept = kept + jnp.where(lane[0:32] // 32 == c, out[32 * c : 32 * c + 32, :], 0.0)
        return kept

    def value(k, mates, first):
        there, ids = slots(k)
        if first:
            column = jnp.sum(jnp.where(lane == k, fac[...], 0.0), axis=1, keepdims=True)
            pb[k] = (prob[k] * column).astype(BF16)
            pnew[k] = pnew[k] * column
        p = pb[k].astype(F32)
        for o in mates:
            n = block_of[o]
            weighted = (p * scale_rows(n, 1, ids)).astype(BF16)
            held = vn if o < 2 else vf
            values = jnp.concatenate([held[core_of[o], ids[c]] for c in range(CAP)], axis=0)
            acc[n, k] = keep(nt(weighted, values))

        @pl.when(there % 4 == i)
        def _():
            pn = pnew[k].astype(BF16)
            for o in mates:
                n = block_of[o]
                both = qx[n, there, 32:48, :].astype(F32)
                new_values = pltpu.roll(both, 12, 0).astype(BF16)
                acc[n, k] += keep(nn(pn, new_values))

    def value_near(k, _):
        value(k, (0, 1), True)
        return 0

    def value_far(k, _):
        value(k, (2, 3), False)
        return 0

    near_sum = pltpu.make_async_remote_copy(
        acc.at[block_of[1]], ra.at[0], ha_ssem.at[0], ha_rsem.at[0],
        device_id={"tp": mate(t, 1)}, device_id_type=MESH)

    def far_sum(q):
        at = pl.ds(q * per, per)
        return pltpu.make_async_remote_copy(
            acc.at[block_of[3], at], ra.at[1, at], ha_ssem.at[1 + q], ha_rsem.at[1 + q],
            device_id={"tp": mate(t, 1)}, device_id_type=MESH)

    def chip_sum(q):
        at = pl.ds(q * per, per)
        return pltpu.make_async_remote_copy(
            sb.at[at], rb.at[at], hb_ssem.at[q], hb_rsem.at[q],
            device_id={"tp": mate(t, 2)}, device_id_type=MESH)

    def back_copy(k):
        there = lax.rem(g - k + ng, ng)
        return pltpu.make_async_remote_copy(
            mix.at[k], back.at[g], bk_ssem.at[k], bk_rsem.at[k],
            device_id={"grp": there}, device_id_type=MESH)

    def back_start(k, _):
        back_copy(k).start()
        return 0

    def back_wait(k, _):
        back_copy(k).wait()
        return 0

    def send_chip_sum(q):
        at = pl.ds(q * per, per)
        far_sum(q).wait()
        sb[at] = (acc[block_of[2], at] + ra[1, at]).astype(BF16)
        chip_sum(q).start()

    def send_back(q):
        at = pl.ds(q * per, per)
        chip_sum(q).wait()
        mix[at] = (acc[i, at] + ra[0, at] + rb[at].astype(F32)).astype(BF16)
        lax.fori_loop(max(q * per, 1), (q + 1) * per, back_start, 0)

    own_cache[2].wait()
    for move in near_values:
        move.wait_recv()
    lax.fori_loop(0, ng, value_near, 0)
    near_sum.start()
    for move in value_moves:
        move.wait_recv()
    for q in range(chunks):
        lax.fori_loop(q * per, (q + 1) * per, value_far, 0)
        far_sum(q).start()
        if q >= 1:
            send_chip_sum(q - 1)
    near_sum.wait()
    if chunks >= 2:
        send_back(0)
    send_chip_sum(chunks - 1)
    for q in range(1 if chunks >= 2 else 0, chunks):
        send_back(q)
    back[g] = mix[0]
    lax.fori_loop(1, ng, back_wait, 0)

    wide = 32 * ng
    row_w = iota((128, wide), 0)
    lane_w = iota((128, wide), 1)
    hit = ((lane_w // 32).astype(F32) == src_col[:, 0:1]) & (lane_w % 4 == row_w // 32)
    chosen = rank_col[...] == (lane // 32).astype(F32)
    slots_all = back[...].reshape(wide, 128)
    mixed = jnp.zeros((128, 256), F32)
    for b in range(8):
        pick = ones(hit & ((lane_w // 4) % 8 == b))
        rows_b = jnp.where(chosen, nn(pick, slots_all), 0.0).astype(BF16)
        mixed = mixed + nn(rows_b, fold[128 * b : 128 * b + 128, :])
    mixed = mixed.astype(BF16)

    loads[3].wait()

    def columns(h, e, c):
        part, dy = BLOCKS[e]
        block = part * 8 + lax.rem(y + dy, 4) * 2 + c
        return pl.ds(pl.multiple_of((block * 2 + h) * half, 128), half)

    def ta_copy(h, e):
        return pltpu.make_async_remote_copy(
            ta_send.at[h, e], ta_recv.at[h, e], ta_ssem.at[h, e], ta_rsem.at[h, e],
            device_id={"tp": mate(t, 1)}, device_id_type=MESH)

    before = t + 2 * ((y + 3) % 4 - y)
    after = t + 2 * ((y + 1) % 4 - y)
    targets = (before, after, after, before, before, after)

    def tb_copy(h, e):
        return pltpu.make_async_remote_copy(
            tb_send.at[h, e], tb_recv.at[h, e], tb_ssem.at[h, e], tb_rsem.at[h, e],
            device_id={"tp": targets[e]}, device_id_type=MESH)

    def tc_copy(h):
        return pltpu.make_async_remote_copy(
            tc_send.at[h], tc_recv.at[h], tc_ssem.at[h], tc_rsem.at[h],
            device_id={"tp": flip(t, 8)}, device_id_type=MESH)

    def core_sum(h, e):
        ta_copy(h, e).wait()
        return own[h, e] + ta_recv[h, e].astype(F32)

    for h in range(2):
        for e in range(8):
            ta_send[h, e] = nn(mixed, wov[:, columns(h, e, 1 - core)]).astype(BF16)
            ta_copy(h, e).start()
        for e in range(8):
            own[h, e] = nn(mixed, wov[:, columns(h, e, core)])
        for e in range(4):
            tb_send[h, e] = core_sum(h, e).astype(BF16)
            tb_copy(h, e).start()
    for h in range(2):
        for e in (4, 5):
            summed = core_sum(h, e)
            tb_copy(h, e - 4).wait()
            tb_send[h, e] = (summed + tb_recv[h, e - 4].astype(F32)).astype(BF16)
            tb_copy(h, e).start()
        fin[h, 0] = core_sum(h, 6)
        fin[h, 1] = core_sum(h, 7)
    for h in range(2):
        for e in (2, 3, 4, 5):
            tb_copy(h, e).wait()
        fin[h, 0] = fin[h, 0] + tb_recv[h, 2].astype(F32) + tb_recv[h, 4].astype(F32)
        fin[h, 1] = fin[h, 1] + tb_recv[h, 3].astype(F32) + tb_recv[h, 5].astype(F32)
        tc_send[h] = fin[h, 1 - zh].astype(BF16)
        tc_copy(h).start()
    for h in range(2):
        tc_copy(h).wait()
        out_ref[:, h * half : (h + 1) * half] = (fin[h, zh] + tc_recv[h].astype(F32)).astype(BF16)

    def q_sent(k, _):
        q_copy(k).wait_send()
        return 0

    def q_shared(k, _):
        for o in (1, 2, 3):
            q_share(o, k).wait_send()
        return 0

    lax.fori_loop(1, ng, q_sent, 0)
    lax.fori_loop(0, ng, q_shared, 0)
    for o in (1, 2, 3):
        key_moves[o][0].wait_send()
        key_moves[o][1].wait_send()
        st_moves[o - 1].wait_send()
    for move in near_values + value_moves:
        move.wait_send()


def rope_tables(step_count, cached, particles):
    pair = np.arange(64, dtype=np.float32).reshape(4, 16)
    frequency = np.exp(-(pair / np.float32(64)) * np.log(np.float32(500000.0))).astype(np.float32)
    positions = (cached + np.arange(step_count)).astype(np.float32)
    angles = (positions[None, None, :] * frequency[:, :, None]).astype(np.float32)
    tables = np.stack([np.cos(angles), np.sin(angles)]).astype(np.float32)
    return np.repeat(tables, particles, axis=-1)


def shards(ng, inputs, norm_gain, w_query, w_keyval, w_out, kv_cache, kv_scales, ancestors):
    step_count, particles, width = inputs.shape
    cached = kv_cache.shape[3]
    rope = jnp.asarray(rope_tables(step_count, cached, particles))
    missing = -ancestors.shape[0] % 128
    if missing:
        ancestors = jnp.pad(ancestors, (0, missing), constant_values=-1)
    rows = step_count * particles
    cb = width // lax.axis_size("tp")
    half = cb // 2
    vmem = pl.BlockSpec(memory_space=pltpu.VMEM)
    hbm = pl.BlockSpec(memory_space=pltpu.HBM)
    dma = pltpu.SemaphoreType.DMA
    scratch = [
        pltpu.VMEM((rows, width), BF16),
        pltpu.VMEM((320, width), BF16),
        pltpu.VMEM((256, width), BF16),
        pltpu.VMEM((width // 128, 128), BF16),
        pltpu.VMEM((width // 128, 128), F32),
        pltpu.VMEM((2, 16, 128), F32),
        pltpu.VMEM((8, 128), jnp.int32),
        pltpu.VMEM((8, 128), jnp.int32),
        pltpu.SMEM((8, 128), jnp.int32),
        pltpu.VMEM((128, 128), F32),
        pltpu.VMEM((128, 128), F32),
        pltpu.VMEM((320, 128), F32),
        pltpu.VMEM((320, 128), BF16),
        pltpu.VMEM((ng * 16, 2048), BF16),
        pltpu.VMEM((128, 2048), BF16),
        pltpu.VMEM((ng, 48, 128), BF16),
        pltpu.VMEM((4, ng, 48, 128), BF16),
        pltpu.VMEM((2, particles, 32, 128), BF16),
        pltpu.VMEM((2, particles, 32, 128), BF16),
        pltpu.VMEM((2, particles, 32, 128), BF16),
        pltpu.VMEM((2, particles, 32, 128), BF16),
        pltpu.VMEM((4, 2, particles, 128), BF16),
        pltpu.VMEM((4, 2, particles, 128), F32),
        pltpu.VMEM((ng, 128, 128), F32),
        pltpu.VMEM((ng, 128, 128), BF16),
        pltpu.VMEM((ng, 128, 16), F32),
        pltpu.VMEM((128, 128), F32),
        pltpu.VMEM((2 * ng, 128), F32),
        pltpu.VMEM((3, 2 * ng, 128), F32),
        pltpu.VMEM((128, 128), F32),
        pltpu.VMEM((4, ng, 32, 128), F32),
        pltpu.VMEM((2, ng, 32, 128), F32),
        pltpu.VMEM((ng, 32, 128), BF16),
        pltpu.VMEM((ng, 32, 128), BF16),
        pltpu.VMEM((ng, 32, 128), BF16),
        pltpu.VMEM((ng, 32, 128), BF16),
        pltpu.VMEM((1024, 256), BF16),
        pltpu.VMEM((2, 8, rows, half), BF16),
        pltpu.VMEM((2, 8, rows, half), BF16),
        pltpu.VMEM((2, 8, rows, half), F32),
        pltpu.VMEM((2, 6, rows, half), BF16),
        pltpu.VMEM((2, 6, rows, half), BF16),
        pltpu.VMEM((2, 2, rows, half), F32),
        pltpu.VMEM((2, rows, half), BF16),
        pltpu.VMEM((2, rows, half), BF16),
        dma((11,)),
        dma((3, 2)), dma((3, 2)),
        dma((3, PIECES)), dma((3, PIECES)),
        dma((ng,)), dma((ng,)),
        dma((3, ng)), dma((3, ng)),
        dma((3,)), dma((3,)),
        dma((1 + MAX_CHUNKS,)), dma((1 + MAX_CHUNKS,)),
        dma((MAX_CHUNKS,)), dma((MAX_CHUNKS,)),
        dma((ng,)), dma((ng,)),
        dma((2, 8)), dma((2, 8)),
        dma((2, 6)), dma((2, 6)),
        dma((2,)), dma((2,)),
    ]
    out = pl.pallas_call(
        functools.partial(kernel, ng),
        out_shape=jax.ShapeDtypeStruct((rows, cb), BF16),
        in_specs=[hbm] * 9,
        out_specs=vmem,
        scratch_shapes=scratch,
        compiler_params=pltpu.CompilerParams(
            collective_id=0, has_side_effects=True, vmem_limit_bytes=60 * 1024 * 1024),
    )(
        inputs.reshape(rows, width),
        norm_gain.reshape(width // 128, 128),
        jnp.transpose(w_query, (1, 2, 0)).reshape(256, width),
        jnp.transpose(w_keyval, (1, 2, 0)).reshape(64, width),
        w_out.reshape(256, width),
        kv_cache,
        kv_scales.reshape(2, particles, cached),
        rope,
        ancestors.reshape(-1, 128),
    )
    return out.reshape(step_count, particles, cb)


def solution(mesh):
    in_specs = (
        P(None, "grp", None),
        P(),
        P(None, None, "tp"),
        P(None, None, "tp"),
        P(None, "tp", None),
        P(None, "grp", "tp", None),
        P(None, "grp", "tp", None),
        P(),
    )
    out_specs = P(None, "grp", "tp")
    return jax.shard_map(
        functools.partial(shards, mesh.shape["grp"]), mesh=mesh, in_specs=in_specs, out_specs=out_specs,
        check_vma=False)
```

```python
import functools

import jax
import jax.numpy as jnp
import numpy as np
from jax import lax
from jax.experimental import pallas as pl
from jax.experimental.pallas import tpu as pltpu
from jax.sharding import PartitionSpec as P

HD = 128
CAP = 4
MESH = pl.DeviceIdType.MESH
F32 = jnp.float32
BF16 = jnp.bfloat16
MAX_CHUNKS = 4
PIECES = 2
EARLY = 0
BLOCKS = ((0, 2), (1, 2), (0, 1), (1, 3), (0, 3), (1, 1), (0, 0), (1, 0))


def flip(t, bit):
    return t + bit - 2 * bit * ((t // bit) % 2)


def mate(t, offset):
    if offset & 1:
        t = flip(t, 1)
    if offset & 2:
        t = flip(t, 2)
    return t


def nt(a, b):
    return lax.dot_general(a, b, (((1,), (1,)), ((), ())), preferred_element_type=F32)


def nn(a, b):
    return jnp.dot(a, b, preferred_element_type=F32)


def iota(shape, axis):
    return lax.broadcasted_iota(jnp.int32, shape, axis)


def kernel(
    ng, x_hbm, gain_hbm, wq_hbm, wkv_hbm, wo_hbm, kv_hbm, sc_hbm, rope_hbm, anc_hbm,
    out_ref,
    xv, wv, wov, gain_v, gain_f, rope, anc, ids_v, ids_s, src_col, rank_col,
    accq, qt, onehot, spread, sendq, qx, kn, kf, vn, vo, vl, scx, scf, prob, pb, pnew, stat, st_send, st_recv,
    fac, acc, ra, sb, rb, mix, back, fold, ta_send, ta_recv, own, tb_send, tb_recv, fin, tc_send, tc_recv,
    loc_sem, k_ssem, k_rsem, v_ssem, v_rsem, qa_ssem, qa_rsem, qg_ssem, qg_rsem, st_ssem, st_rsem, ha_ssem,
    ha_rsem, hb_ssem, hb_rsem, bk_ssem, bk_rsem, ta_ssem, ta_rsem, tb_ssem, tb_rsem, tc_ssem, tc_rsem,
):
    g = lax.axis_index("grp")
    t = lax.axis_index("tp")
    i = t % 4
    core = t % 2
    y = (t // 2) % 4
    zh = t // 8
    width = x_hbm.shape[1]
    half = out_ref.shape[1] // 2
    chunks = min(MAX_CHUNKS, ng)
    per = ng // chunks
    block_of = [mate(t, o) % 4 for o in range(4)]
    core_of = [core, 1 - core, core, 1 - core]

    loads = [
        pltpu.make_async_copy(x_hbm, xv, loc_sem.at[0]),
        pltpu.make_async_copy(wq_hbm, wv.at[pl.ds(0, 256)], loc_sem.at[1]),
        pltpu.make_async_copy(wkv_hbm, wv.at[pl.ds(256, 64)], loc_sem.at[2]),
        pltpu.make_async_copy(wo_hbm, wov, loc_sem.at[3]),
        pltpu.make_async_copy(anc_hbm, anc.at[pl.ds(0, anc_hbm.shape[0])], loc_sem.at[4]),
        pltpu.make_async_copy(gain_hbm, gain_v, loc_sem.at[5]),
        pltpu.make_async_copy(rope_hbm.at[:, i], rope, loc_sem.at[6]),
    ]
    anc[...] = jnp.full(anc.shape, -1, jnp.int32)
    for n in (4, 0, 5, 6, 1, 2):
        loads[n].start()

    barrier = pltpu.get_barrier_semaphore()
    tp_peers = [mate(t, 1), mate(t, 2), mate(t, 3), t + 2 * ((y + 3 - 2 * (y % 2)) % 4 - y), flip(t, 8)]

    def greet(k, _):
        pl.semaphore_signal(barrier, inc=1, device_id={"grp": lax.rem(g + k, ng)}, device_id_type=MESH)
        return 0

    for peer in tp_peers:
        pl.semaphore_signal(barrier, inc=1, device_id={"tp": peer}, device_id_type=MESH)
    lax.fori_loop(1, ng, greet, 0)
    pl.semaphore_wait(barrier, len(tp_peers) + ng - 1)

    def lanes_of(block):
        return pl.ds(pl.multiple_of(128 * block, 128), 128)

    def key_copies(o):
        args = dict(device_id={"tp": mate(t, o)}, device_id_type=MESH)
        lanes = lanes_of(block_of[o])
        return [
            pltpu.make_async_remote_copy(
                kv_hbm.at[0, :, :, lanes], (kn if o == 1 else kf).at[core], k_ssem.at[o - 1, 0], k_rsem.at[o - 1, 0], **args),
            pltpu.make_async_remote_copy(
                sc_hbm.at[:, :, lanes], scx.at[i], k_ssem.at[o - 1, 1], k_rsem.at[o - 1, 1], **args),
        ]

    piece = kv_hbm.shape[1] // PIECES

    def value_copy(o, j):
        at = pl.ds(j * piece, piece)
        return pltpu.make_async_remote_copy(
            kv_hbm.at[1, at, :, lanes_of(block_of[o])], (vn.at[core, at], vl.at[at], vo.at[at])[o - 1],
            v_ssem.at[o - 1, j], v_rsem.at[o - 1, j], device_id={"tp": mate(t, o)}, device_id_type=MESH)

    key_moves = {o: key_copies(o) for o in (1, 2, 3)}
    value_moves = [value_copy(o, j) for o in (3, 2) for j in range(PIECES)]
    near_values = [value_copy(1, j) for j in range(PIECES)]
    for o in (2, 3, 1):
        key_moves[o][1].start()
    for o in (2, 3, 1):
        key_moves[o][0].start()
    for move in near_values + value_moves[:EARLY]:
        move.start()
    own_cache = [
        pltpu.make_async_copy(kv_hbm.at[0, :, :, lanes_of(i)], kn.at[core], loc_sem.at[7]),
        pltpu.make_async_copy(sc_hbm.at[:, :, lanes_of(i)], scx.at[i], loc_sem.at[8]),
        pltpu.make_async_copy(kv_hbm.at[1, :, :, lanes_of(i)], vn.at[core], loc_sem.at[9]),
    ]
    for copy in own_cache:
        copy.start()
    loads[3].start()

    row = iota((128, 128), 0)
    lane = iota((128, 128), 1)

    def ones(where):
        return jnp.where(where, 1.0, 0.0).astype(BF16)

    loads[4].wait()
    parents = anc[...]
    source = parents >> 5
    wanted = source == g
    within = iota((8, 128), 1) % 32

    def running(v):
        for shift in (1, 2, 4, 8, 16):
            v = v + jnp.where(within >= shift, pltpu.roll(v, shift, 1), 0)
        return v

    place = running(wanted.astype(jnp.int32))
    ids = jnp.zeros((8, 128), jnp.int32)
    for c in range(CAP):
        at_slot = running(jnp.where(wanted & (place == c + 1), parents & 31, 0))
        ids = jnp.where(within == 32 - CAP + c, pltpu.roll(at_slot, (c + 1 - CAP) % 128, 1), ids)
    ids_v[...] = ids
    to_scalars = pltpu.make_async_copy(ids_v, ids_s, loc_sem.at[10])
    to_scalars.start()
    mine = jnp.sum(jnp.where(iota((8, 128), 0) == g // 4, source.astype(F32), 0.0), axis=0, keepdims=True)
    mine = nn(jnp.broadcast_to(mine, (8, 128)).astype(BF16), ones(row == (g % 4) * 32 + lane % 32))[0:1]
    mine = jnp.broadcast_to(mine, (128, 128))
    mine_col = jnp.transpose(mine)
    src_col[...] = mine_col
    rank = jnp.sum(jnp.where((mine == mine_col) & (row < lane % 32), 1.0, 0.0), axis=0, keepdims=True)
    rank_col[...] = jnp.transpose(jnp.broadcast_to(rank, (128, 128)))

    slot_row = iota((ng * 16, 128), 0)
    slot_lane = iota((ng * 16, 128), 1)
    hit = (mine[0:1] == (slot_row // 16).astype(F32)) & (slot_row % 4 == slot_lane // 32)
    for c in range(CAP):
        hit_c = hit & (rank == c)
        for gl in range(4):
            onehot[:, (c * 4 + gl) * 128 : (c * 4 + gl + 1) * 128] = ones(hit_c & ((slot_row // 4) % 4 == gl))
    spread[...] = jnp.zeros_like(spread)

    loads[5].wait()
    gain_f[...] = gain_v[...].astype(F32)
    loads[0].wait()
    step = min(1024, width)

    def squares(k, total):
        part = xv[:, pl.ds(pl.multiple_of(k * step, step), step)].astype(F32)
        return total + jnp.sum(part * part, axis=1, keepdims=True)

    total = lax.fori_loop(0, width // step, squares, jnp.zeros((128, 1), F32))
    inv = lax.rsqrt(total / width + 1e-05)
    loads[1].wait()
    loads[2].wait()
    accq[...] = jnp.zeros_like(accq)

    def project(k, _):
        part = pl.ds(pl.multiple_of(k * step, step), step)
        gains = gain_f[pl.ds(pl.multiple_of(k * (step // 128), 8), step // 128), :]
        gains = jnp.concatenate([gains[r : r + 1] for r in range(step // 128)], axis=1)
        normed = (xv[:, part].astype(F32) * inv * gains).astype(BF16)
        accq[...] += nt(wv[:, part], normed)
        return 0

    lax.fori_loop(0, width // step, project, 0)
    loads[6].wait()
    cosine = rope[0]
    sine = rope[1]
    for b in range(9):
        front = accq[32 * b : 32 * b + 16, :]
        rear = accq[32 * b + 16 : 32 * b + 32, :]
        new_front = front * cosine - rear * sine
        new_rear = rear * cosine + front * sine
        if b < 8:
            new_front = new_front * HD ** (-0.5)
            new_rear = new_rear * HD ** (-0.5)
        qt[32 * b : 32 * b + 16, :] = new_front.astype(BF16)
        qt[32 * b + 16 : 32 * b + 32, :] = new_rear.astype(BF16)
    qt[288:320, :] = accq[288:320, :].astype(BF16)

    for third in range(3):
        for c in range(CAP):
            for gl in range(4):
                at = pl.ds((c * 4 + gl) * 128, 128)
                b = third * 4 + gl
                if b < 10:
                    spread[32 * c : 32 * c + 32, at] = qt[32 * b : 32 * b + 32, :]
                else:
                    spread[32 * c : 32 * c + 32, at] = jnp.zeros((32, 128), BF16)
        packed = nt(onehot[...], spread[...]).astype(BF16)
        sendq[:, 16 * third : 16 * third + 16, :] = packed.reshape(ng, 16, 128)

    def q_copy(k):
        there = lax.rem(g + k, ng)
        return pltpu.make_async_remote_copy(
            sendq.at[there], qx.at[i, g], qa_ssem.at[k], qa_rsem.at[k],
            device_id={"grp": there}, device_id_type=MESH)

    def q_share(o, k):
        here = lax.rem(g - k + ng, ng)
        return pltpu.make_async_remote_copy(
            qx.at[i, here], qx.at[i, here], qg_ssem.at[o - 1, k], qg_rsem.at[o - 1, k],
            device_id={"tp": mate(t, o)}, device_id_type=MESH)

    def q_arrival(o, k):
        here = lax.rem(g - k + ng, ng)
        return pltpu.make_async_remote_copy(
            qx.at[i, here], qx.at[block_of[o], here], qg_ssem.at[o - 1, k], qg_rsem.at[o - 1, k],
            device_id={"tp": mate(t, o)}, device_id_type=MESH)

    def q_start(k, _):
        q_copy(k).start()
        return 0

    def q_forward(k, _):
        q_copy(k).wait_recv()
        for o in (2, 1):
            q_share(o, k).start()
        return 0

    def q_relay(k):
        here = lax.rem(g - k + ng, ng)
        return pltpu.make_async_remote_copy(
            qx.at[block_of[2], here], qx.at[block_of[2], here], qg_ssem.at[2, k], qg_rsem.at[2, k],
            device_id={"tp": mate(t, 1)}, device_id_type=MESH)

    def hand_on(k):
        q_arrival(2, k).wait_recv()
        q_relay(k).start()

    lax.fori_loop(1, ng, q_start, 0)
    qx[i, g] = sendq[g]
    for o in (2, 1):
        q_share(o, 0).start()
    lax.fori_loop(1, ng, q_forward, 0)
    for move in value_moves[EARLY:]:
        move.start()

    fold_row = iota(fold.shape, 0)
    fold_lane = iota(fold.shape, 1)
    fold[...] = ones((fold_row // 128 == fold_lane // 32) & (fold_row % 32 == fold_lane % 32))
    diagonal = ones(row // 32 == lane // 32)
    stat[...] = jnp.zeros_like(stat)
    to_scalars.wait()

    def slots(k):
        there = lax.rem(g - k + ng, ng)
        return there, [ids_s[there // 4, (there % 4) * 32 + 32 - CAP + c] & 31 for c in range(CAP)]

    def scale_rows(n, kind, ids):
        return jnp.concatenate(
            [jnp.broadcast_to(scf[n, kind, pl.ds(ids[c], 1), :], (32, 128)) for c in range(CAP)], axis=0)

    def queries(n, there):
        return jnp.concatenate([qx[n, there, 0:32, :]] * CAP, axis=0) * diagonal

    def block_scores(o, there, ids):
        n = block_of[o]
        held = kn if o < 2 else kf
        keys = jnp.concatenate([held[core_of[o], ids[c]] for c in range(CAP)], axis=0)
        return nn(queries(n, there), keys) * scale_rows(n, 0, ids)

    own_cache[0].wait()
    own_cache[1].wait()
    for kind in (0, 1):
        key_moves[1][kind].wait_recv()
    key_moves[2][1].wait_recv()
    key_moves[3][1].wait_recv()
    scf[...] = scx[...].astype(F32)

    def score_near(k, _):
        q_arrival(1, k).wait_recv()
        there, ids = slots(k)
        prob[k] = block_scores(0, there, ids) + block_scores(1, there, ids)
        return 0

    lax.fori_loop(0, ng, score_near, 0)
    key_moves[2][0].wait_recv()
    key_moves[3][0].wait_recv()

    ahead = min(3, ng)
    for k in range(ahead):
        hand_on(k)

    def score_far(k, _):
        @pl.when(k + ahead < ng)
        def _():
            hand_on(k + ahead)

        q_arrival(3, k).wait_recv()
        there, ids = slots(k)
        total = prob[k] + block_scores(2, there, ids) + block_scores(3, there, ids)
        pnew[k] = jnp.full((128, 16), -jnp.inf, F32)

        @pl.when(there % 4 == i)
        def _():
            new = jnp.zeros((128, 16), F32)
            for n in range(4):
                new = new + nt(queries(n, there), qx[n, there, 32:48, :])
            column = iota((128, 16), 1)
            seen = (column <= iota((128, 16), 0) % 4) & (column < 4)
            pnew[k] = jnp.where(seen, new, -jnp.inf)

        new = pnew[k]
        top = jnp.maximum(jnp.max(total, axis=1, keepdims=True), jnp.max(new, axis=1, keepdims=True))
        part = jnp.exp(total - top)
        new = jnp.exp(new - top)
        prob[k] = part
        pnew[k] = new
        mass = jnp.sum(part, axis=1, keepdims=True) + jnp.sum(new, axis=1, keepdims=True)
        stat[...] = jnp.where(lane == k, top, jnp.where(lane == ng + k, mass, stat[...]))
        return 0

    lax.fori_loop(0, ng, score_far, 0)

    st_send[...] = jnp.transpose(stat[...])[0 : 2 * ng, :]
    st_moves = [
        pltpu.make_async_remote_copy(
            st_send, st_recv.at[o - 1], st_ssem.at[o - 1], st_rsem.at[o - 1],
            device_id={"tp": mate(t, o)}, device_id_type=MESH)
        for o in (1, 2, 3)
    ]
    for o in (2, 1, 0):
        st_moves[o].start()
    for o in range(3):
        st_moves[o].wait_recv()
    tops = [st_send[0:ng, :]] + [st_recv[o, 0:ng, :] for o in range(3)]
    masses = [st_send[ng : 2 * ng, :]] + [st_recv[o, ng : 2 * ng, :] for o in range(3)]
    top = jnp.maximum(jnp.maximum(tops[0], tops[1]), jnp.maximum(tops[2], tops[3]))
    mass = sum(masses[o] * jnp.exp(tops[o] - top) for o in range(4))
    factor = jnp.exp(tops[0] - top) / mass
    fac[...] = jnp.transpose(jnp.concatenate([factor, jnp.zeros((128 - ng, 128), F32)], axis=0))

    def keep(out):
        kept = jnp.zeros((32, 128), F32)
        for c in range(CAP):
            kept = kept + jnp.where(lane[0:32] // 32 == c, out[32 * c : 32 * c + 32, :], 0.0)
        return kept

    def value(k, mates, first):
        there, ids = slots(k)
        if first:
            column = jnp.sum(jnp.where(lane == k, fac[...], 0.0), axis=1, keepdims=True)
            pb[k] = (prob[k] * column).astype(BF16)
            pnew[k] = pnew[k] * column
        p = pb[k].astype(F32)
        for o in mates:
            n = block_of[o]
            weighted = (p * scale_rows(n, 1, ids)).astype(BF16)
            held = [vn.at[core], vn.at[1 - core], vl, vo][o]
            values = jnp.concatenate([held[ids[c]] for c in range(CAP)], axis=0)
            acc[n, k] = keep(nt(weighted, values))

        @pl.when(there % 4 == i)
        def _():
            pn = pnew[k].astype(BF16)
            for o in mates:
                n = block_of[o]
                both = qx[n, there, 32:48, :].astype(F32)
                new_values = pltpu.roll(both, 12, 0).astype(BF16)
                acc[n, k] += keep(nn(pn, new_values))

    def value_near(k, _):
        value(k, (0, 1), True)
        return 0

    def value_other(k, _):
        value(k, (3,), False)
        return 0

    def value_last(k, _):
        value(k, (2,), False)
        return 0

    near_sum = pltpu.make_async_remote_copy(
        acc.at[block_of[1]], ra.at[0], ha_ssem.at[0], ha_rsem.at[0],
        device_id={"tp": mate(t, 1)}, device_id_type=MESH)

    def far_sum(q):
        at = pl.ds(q * per, per)
        return pltpu.make_async_remote_copy(
            acc.at[block_of[3], at], ra.at[1, at], ha_ssem.at[1 + q], ha_rsem.at[1 + q],
            device_id={"tp": mate(t, 1)}, device_id_type=MESH)

    def chip_sum(q):
        at = pl.ds(q * per, per)
        return pltpu.make_async_remote_copy(
            sb.at[at], rb.at[at], hb_ssem.at[q], hb_rsem.at[q],
            device_id={"tp": mate(t, 2)}, device_id_type=MESH)

    def back_copy(k):
        there = lax.rem(g - k + ng, ng)
        return pltpu.make_async_remote_copy(
            mix.at[k], back.at[g], bk_ssem.at[k], bk_rsem.at[k],
            device_id={"grp": there}, device_id_type=MESH)

    def back_start(k, _):
        back_copy(k).start()
        return 0

    def back_wait(k, _):
        back_copy(k).wait()
        return 0

    def send_chip_sum(q):
        at = pl.ds(q * per, per)
        far_sum(q).wait()
        sb[at] = (acc[block_of[2], at] + ra[1, at]).astype(BF16)
        chip_sum(q).start()

    def send_back(q):
        at = pl.ds(q * per, per)
        chip_sum(q).wait()
        mix[at] = (acc[i, at] + ra[0, at] + rb[at].astype(F32)).astype(BF16)
        lax.fori_loop(max(q * per, 1), (q + 1) * per, back_start, 0)

    own_cache[2].wait()
    for move in near_values:
        move.wait_recv()
    lax.fori_loop(0, ng, value_near, 0)
    near_sum.start()
    for move in value_moves[:PIECES]:
        move.wait_recv()
    for q in range(chunks):
        lax.fori_loop(q * per, (q + 1) * per, value_other, 0)
        far_sum(q).start()
    for move in value_moves[PIECES:]:
        move.wait_recv()
    for q in range(chunks):
        lax.fori_loop(q * per, (q + 1) * per, value_last, 0)
        send_chip_sum(q)
        if q == 0:
            near_sum.wait()
        else:
            send_back(q - 1)
    send_back(chunks - 1)
    back[g] = mix[0]
    lax.fori_loop(1, ng, back_wait, 0)

    wide = 32 * ng
    row_w = iota((128, wide), 0)
    lane_w = iota((128, wide), 1)
    hit = ((lane_w // 32).astype(F32) == src_col[:, 0:1]) & (lane_w % 4 == row_w // 32)
    chosen = rank_col[...] == (lane // 32).astype(F32)
    slots_all = back[...].reshape(wide, 128)
    mixed = jnp.zeros((128, 256), F32)
    for b in range(8):
        pick = ones(hit & ((lane_w // 4) % 8 == b))
        rows_b = jnp.where(chosen, nn(pick, slots_all), 0.0).astype(BF16)
        mixed = mixed + nn(rows_b, fold[128 * b : 128 * b + 128, :])
    mixed = mixed.astype(BF16)

    loads[3].wait()

    def columns(h, e, c):
        part, dy = BLOCKS[e]
        block = part * 8 + lax.rem(y + dy, 4) * 2 + c
        return pl.ds(pl.multiple_of((block * 2 + h) * half, 128), half)

    def ta_copy(h, e):
        return pltpu.make_async_remote_copy(
            ta_send.at[h, e], ta_recv.at[h, e], ta_ssem.at[h, e], ta_rsem.at[h, e],
            device_id={"tp": mate(t, 1)}, device_id_type=MESH)

    before = t + 2 * ((y + 3) % 4 - y)
    after = t + 2 * ((y + 1) % 4 - y)
    targets = (before, after, after, before, before, after)

    def tb_copy(h, e):
        return pltpu.make_async_remote_copy(
            tb_send.at[h, e], tb_recv.at[h, e], tb_ssem.at[h, e], tb_rsem.at[h, e],
            device_id={"tp": targets[e]}, device_id_type=MESH)

    def tc_copy(h):
        return pltpu.make_async_remote_copy(
            tc_send.at[h], tc_recv.at[h], tc_ssem.at[h], tc_rsem.at[h],
            device_id={"tp": flip(t, 8)}, device_id_type=MESH)

    def core_sum(h, e):
        ta_copy(h, e).wait()
        return own[h, e] + ta_recv[h, e].astype(F32)

    def first_step(h, pair):
        for e in pair:
            ta_send[h, e] = nn(mixed, wov[:, columns(h, e, 1 - core)]).astype(BF16)
            ta_copy(h, e).start()
        for e in pair:
            own[h, e] = nn(mixed, wov[:, columns(h, e, core)])

    def second_step(h, pair):
        for e in pair:
            summed = core_sum(h, e)
            if e in (4, 5):
                tb_copy(h, e - 4).wait()
                summed = summed + tb_recv[h, e - 4].astype(F32)
            if e < 6:
                tb_send[h, e] = summed.astype(BF16)
                tb_copy(h, e).start()
            else:
                fin[h, e - 6] = summed

    order = [(0, (0, 1)), (0, (2, 3)), (1, (0, 1)), (0, (4, 5)), (1, (2, 3)), (1, (4, 5)), (0, (6, 7)), (1, (6, 7))]
    for at, step_at in enumerate(order):
        first_step(*step_at)
        if at:
            second_step(*order[at - 1])
    second_step(*order[-1])
    for h in range(2):
        for e in (2, 3, 4, 5):
            tb_copy(h, e).wait()
        fin[h, 0] = fin[h, 0] + tb_recv[h, 2].astype(F32) + tb_recv[h, 4].astype(F32)
        fin[h, 1] = fin[h, 1] + tb_recv[h, 3].astype(F32) + tb_recv[h, 5].astype(F32)
        tc_send[h] = fin[h, 1 - zh].astype(BF16)
        tc_copy(h).start()
    for h in range(2):
        tc_copy(h).wait()
        out_ref[:, h * half : (h + 1) * half] = (fin[h, zh] + tc_recv[h].astype(F32)).astype(BF16)

    def q_sent(k, _):
        q_copy(k).wait_send()
        return 0

    def q_shared(k, _):
        for o in (1, 2):
            q_share(o, k).wait_send()
        q_relay(k).wait_send()
        return 0

    lax.fori_loop(1, ng, q_sent, 0)
    lax.fori_loop(0, ng, q_shared, 0)
    for o in (1, 2, 3):
        key_moves[o][0].wait_send()
        key_moves[o][1].wait_send()
        st_moves[o - 1].wait_send()
    for move in near_values + value_moves:
        move.wait_send()


def rope_tables(step_count, cached, particles):
    pair = np.arange(64, dtype=np.float32).reshape(4, 16)
    frequency = np.exp(-(pair / np.float32(64)) * np.log(np.float32(500000.0))).astype(np.float32)
    positions = (cached + np.arange(step_count)).astype(np.float32)
    angles = (positions[None, None, :] * frequency[:, :, None]).astype(np.float32)
    tables = np.stack([np.cos(angles), np.sin(angles)]).astype(np.float32)
    return np.repeat(tables, particles, axis=-1)


def shards(ng, inputs, norm_gain, w_query, w_keyval, w_out, kv_cache, kv_scales, ancestors):
    step_count, particles, width = inputs.shape
    cached = kv_cache.shape[3]
    rope = jnp.asarray(rope_tables(step_count, cached, particles))
    missing = -ancestors.shape[0] % 128
    if missing:
        ancestors = jnp.pad(ancestors, (0, missing), constant_values=-1)
    rows = step_count * particles
    cb = width // lax.axis_size("tp")
    half = cb // 2
    vmem = pl.BlockSpec(memory_space=pltpu.VMEM)
    hbm = pl.BlockSpec(memory_space=pltpu.HBM)
    dma = pltpu.SemaphoreType.DMA
    scratch = [
        pltpu.VMEM((rows, width), BF16),
        pltpu.VMEM((320, width), BF16),
        pltpu.VMEM((256, width), BF16),
        pltpu.VMEM((width // 128, 128), BF16),
        pltpu.VMEM((width // 128, 128), F32),
        pltpu.VMEM((2, 16, 128), F32),
        pltpu.VMEM((8, 128), jnp.int32),
        pltpu.VMEM((8, 128), jnp.int32),
        pltpu.SMEM((8, 128), jnp.int32),
        pltpu.VMEM((128, 128), F32),
        pltpu.VMEM((128, 128), F32),
        pltpu.VMEM((320, 128), F32),
        pltpu.VMEM((320, 128), BF16),
        pltpu.VMEM((ng * 16, 2048), BF16),
        pltpu.VMEM((128, 2048), BF16),
        pltpu.VMEM((ng, 48, 128), BF16),
        pltpu.VMEM((4, ng, 48, 128), BF16),
        pltpu.VMEM((2, particles, 32, 128), BF16),
        pltpu.VMEM((2, particles, 32, 128), BF16),
        pltpu.VMEM((2, particles, 32, 128), BF16),
        pltpu.VMEM((particles, 32, 128), BF16),
        pltpu.VMEM((particles, 32, 128), BF16),
        pltpu.VMEM((4, 2, particles, 128), BF16),
        pltpu.VMEM((4, 2, particles, 128), F32),
        pltpu.VMEM((ng, 128, 128), F32),
        pltpu.VMEM((ng, 128, 128), BF16),
        pltpu.VMEM((ng, 128, 16), F32),
        pltpu.VMEM((128, 128), F32),
        pltpu.VMEM((2 * ng, 128), F32),
        pltpu.VMEM((3, 2 * ng, 128), F32),
        pltpu.VMEM((128, 128), F32),
        pltpu.VMEM((4, ng, 32, 128), F32),
        pltpu.VMEM((2, ng, 32, 128), F32),
        pltpu.VMEM((ng, 32, 128), BF16),
        pltpu.VMEM((ng, 32, 128), BF16),
        pltpu.VMEM((ng, 32, 128), BF16),
        pltpu.VMEM((ng, 32, 128), BF16),
        pltpu.VMEM((1024, 256), BF16),
        pltpu.VMEM((2, 8, rows, half), BF16),
        pltpu.VMEM((2, 8, rows, half), BF16),
        pltpu.VMEM((2, 8, rows, half), F32),
        pltpu.VMEM((2, 6, rows, half), BF16),
        pltpu.VMEM((2, 6, rows, half), BF16),
        pltpu.VMEM((2, 2, rows, half), F32),
        pltpu.VMEM((2, rows, half), BF16),
        pltpu.VMEM((2, rows, half), BF16),
        dma((11,)),
        dma((3, 2)), dma((3, 2)),
        dma((3, PIECES)), dma((3, PIECES)),
        dma((ng,)), dma((ng,)),
        dma((3, ng)), dma((3, ng)),
        dma((3,)), dma((3,)),
        dma((1 + MAX_CHUNKS,)), dma((1 + MAX_CHUNKS,)),
        dma((MAX_CHUNKS,)), dma((MAX_CHUNKS,)),
        dma((ng,)), dma((ng,)),
        dma((2, 8)), dma((2, 8)),
        dma((2, 6)), dma((2, 6)),
        dma((2,)), dma((2,)),
    ]
    out = pl.pallas_call(
        functools.partial(kernel, ng),
        out_shape=jax.ShapeDtypeStruct((rows, cb), BF16),
        in_specs=[hbm] * 9,
        out_specs=vmem,
        scratch_shapes=scratch,
        compiler_params=pltpu.CompilerParams(
            collective_id=0, has_side_effects=True, vmem_limit_bytes=60 * 1024 * 1024),
    )(
        inputs.reshape(rows, width),
        norm_gain.reshape(width // 128, 128),
        jnp.transpose(w_query, (1, 2, 0)).reshape(256, width),
        jnp.transpose(w_keyval, (1, 2, 0)).reshape(64, width),
        w_out.reshape(256, width),
        kv_cache,
        kv_scales.reshape(2, particles, cached),
        rope,
        ancestors.reshape(-1, 128),
    )
    return out.reshape(step_count, particles, cb)


def solution(mesh):
    in_specs = (
        P(None, "grp", None),
        P(),
        P(None, None, "tp"),
        P(None, None, "tp"),
        P(None, "tp", None),
        P(None, "grp", "tp", None),
        P(None, "grp", "tp", None),
        P(),
    )
    out_specs = P(None, "grp", "tp")
    return jax.shard_map(
        functools.partial(shards, mesh.shape["grp"]), mesh=mesh, in_specs=in_specs, out_specs=out_specs,
        check_vma=False)
```

```python
import functools

import jax
import jax.numpy as jnp
import numpy as np
from jax import lax
from jax.experimental import pallas as pl
from jax.experimental.pallas import tpu as pltpu
from jax.sharding import PartitionSpec as P

HD = 128
CAP = 4
MESH = pl.DeviceIdType.MESH
F32 = jnp.float32
BF16 = jnp.bfloat16
MAX_CHUNKS = 4
PIECES = 2
EARLY = 1
BLOCKS = ((0, 2), (1, 2), (0, 1), (1, 3), (0, 3), (1, 1), (0, 0), (1, 0))


def flip(t, bit):
    return t + bit - 2 * bit * ((t // bit) % 2)


def mate(t, offset):
    if offset & 1:
        t = flip(t, 1)
    if offset & 2:
        t = flip(t, 2)
    return t


def nt(a, b):
    return lax.dot_general(a, b, (((1,), (1,)), ((), ())), preferred_element_type=F32)


def nn(a, b):
    return jnp.dot(a, b, preferred_element_type=F32)


def iota(shape, axis):
    return lax.broadcasted_iota(jnp.int32, shape, axis)


def kernel(
    ng, x_hbm, gain_hbm, wq_hbm, wkv_hbm, wo_hbm, kv_hbm, sc_hbm, rope_hbm, anc_hbm,
    out_ref,
    xv, wv, wov, gain_v, gain_f, rope, anc, ids_v, ids_s, src_col, rank_col,
    accq, qt, onehot, spread, sendq, qx, kn, kf, vn, vo, vl, scx, scf, prob, pb, pnew, stat, st_send, st_recv,
    fac, acc, ra, sb, rb, mix, back, fold, ta_send, ta_recv, own, tb_send, tb_recv, fin, tc_send, tc_recv,
    loc_sem, k_ssem, k_rsem, v_ssem, v_rsem, qa_ssem, qa_rsem, qg_ssem, qg_rsem, st_ssem, st_rsem, ha_ssem,
    ha_rsem, hb_ssem, hb_rsem, bk_ssem, bk_rsem, ta_ssem, ta_rsem, tb_ssem, tb_rsem, tc_ssem, tc_rsem,
):
    g = lax.axis_index("grp")
    t = lax.axis_index("tp")
    i = t % 4
    core = t % 2
    y = (t // 2) % 4
    zh = t // 8
    width = x_hbm.shape[1]
    half = out_ref.shape[1] // 2
    chunks = min(MAX_CHUNKS, ng)
    per = ng // chunks
    block_of = [mate(t, o) % 4 for o in range(4)]
    core_of = [core, 1 - core, core, 1 - core]

    loads = [
        pltpu.make_async_copy(x_hbm, xv, loc_sem.at[0]),
        pltpu.make_async_copy(wq_hbm, wv.at[pl.ds(0, 256)], loc_sem.at[1]),
        pltpu.make_async_copy(wkv_hbm, wv.at[pl.ds(256, 64)], loc_sem.at[2]),
        pltpu.make_async_copy(wo_hbm, wov, loc_sem.at[3]),
        pltpu.make_async_copy(anc_hbm, anc.at[pl.ds(0, anc_hbm.shape[0])], loc_sem.at[4]),
        pltpu.make_async_copy(gain_hbm, gain_v, loc_sem.at[5]),
        pltpu.make_async_copy(rope_hbm.at[:, i], rope, loc_sem.at[6]),
    ]
    anc[...] = jnp.full(anc.shape, -1, jnp.int32)
    for n in (4, 0, 5, 6, 1, 2):
        loads[n].start()

    barrier = pltpu.get_barrier_semaphore()
    tp_peers = [mate(t, 1), mate(t, 2), mate(t, 3), t + 2 * ((y + 3 - 2 * (y % 2)) % 4 - y), flip(t, 8)]

    def greet(k, _):
        pl.semaphore_signal(barrier, inc=1, device_id={"grp": lax.rem(g + k, ng)}, device_id_type=MESH)
        return 0

    for peer in tp_peers:
        pl.semaphore_signal(barrier, inc=1, device_id={"tp": peer}, device_id_type=MESH)
    lax.fori_loop(1, ng, greet, 0)
    pl.semaphore_wait(barrier, len(tp_peers) + ng - 1)

    def lanes_of(block):
        return pl.ds(pl.multiple_of(128 * block, 128), 128)

    def key_copies(o):
        args = dict(device_id={"tp": mate(t, o)}, device_id_type=MESH)
        lanes = lanes_of(block_of[o])
        return [
            pltpu.make_async_remote_copy(
                kv_hbm.at[0, :, :, lanes], (kn if o == 1 else kf).at[core], k_ssem.at[o - 1, 0], k_rsem.at[o - 1, 0], **args),
            pltpu.make_async_remote_copy(
                sc_hbm.at[:, :, lanes], scx.at[i], k_ssem.at[o - 1, 1], k_rsem.at[o - 1, 1], **args),
        ]

    piece = kv_hbm.shape[1] // PIECES

    def value_copy(o, j):
        at = pl.ds(j * piece, piece)
        return pltpu.make_async_remote_copy(
            kv_hbm.at[1, at, :, lanes_of(block_of[o])], (vn.at[core, at], vl.at[at], vo.at[at])[o - 1],
            v_ssem.at[o - 1, j], v_rsem.at[o - 1, j], device_id={"tp": mate(t, o)}, device_id_type=MESH)

    key_moves = {o: key_copies(o) for o in (1, 2, 3)}
    value_moves = [value_copy(o, j) for o in (3, 2) for j in range(PIECES)]
    near_values = [value_copy(1, j) for j in range(PIECES)]
    for o in (2, 3, 1):
        key_moves[o][1].start()
    for o in (2, 3, 1):
        key_moves[o][0].start()
    for move in near_values:
        move.start()
    own_cache = [
        pltpu.make_async_copy(kv_hbm.at[0, :, :, lanes_of(i)], kn.at[core], loc_sem.at[7]),
        pltpu.make_async_copy(sc_hbm.at[:, :, lanes_of(i)], scx.at[i], loc_sem.at[8]),
        pltpu.make_async_copy(kv_hbm.at[1, :, :, lanes_of(i)], vn.at[core], loc_sem.at[9]),
    ]
    for copy in own_cache:
        copy.start()
    loads[3].start()

    row = iota((128, 128), 0)
    lane = iota((128, 128), 1)

    def ones(where):
        return jnp.where(where, 1.0, 0.0).astype(BF16)

    loads[4].wait()
    parents = anc[...]
    source = parents >> 5
    wanted = source == g
    within = iota((8, 128), 1) % 32

    def running(v):
        for shift in (1, 2, 4, 8, 16):
            v = v + jnp.where(within >= shift, pltpu.roll(v, shift, 1), 0)
        return v

    place = running(wanted.astype(jnp.int32))
    ids = jnp.zeros((8, 128), jnp.int32)
    for c in range(CAP):
        at_slot = running(jnp.where(wanted & (place == c + 1), parents & 31, 0))
        ids = jnp.where(within == 32 - CAP + c, pltpu.roll(at_slot, (c + 1 - CAP) % 128, 1), ids)
    ids_v[...] = ids
    to_scalars = pltpu.make_async_copy(ids_v, ids_s, loc_sem.at[10])
    to_scalars.start()
    mine = jnp.sum(jnp.where(iota((8, 128), 0) == g // 4, source.astype(F32), 0.0), axis=0, keepdims=True)
    mine = nn(jnp.broadcast_to(mine, (8, 128)).astype(BF16), ones(row == (g % 4) * 32 + lane % 32))[0:1]
    mine = jnp.broadcast_to(mine, (128, 128))
    mine_col = jnp.transpose(mine)
    src_col[...] = mine_col
    rank = jnp.sum(jnp.where((mine == mine_col) & (row < lane % 32), 1.0, 0.0), axis=0, keepdims=True)
    rank_col[...] = jnp.transpose(jnp.broadcast_to(rank, (128, 128)))

    slot_row = iota((ng * 16, 128), 0)
    slot_lane = iota((ng * 16, 128), 1)
    hit = (mine[0:1] == (slot_row // 16).astype(F32)) & (slot_row % 4 == slot_lane // 32)
    for c in range(CAP):
        hit_c = hit & (rank == c)
        for gl in range(4):
            onehot[:, (c * 4 + gl) * 128 : (c * 4 + gl + 1) * 128] = ones(hit_c & ((slot_row // 4) % 4 == gl))
    spread[...] = jnp.zeros_like(spread)

    loads[5].wait()
    gain_f[...] = gain_v[...].astype(F32)
    loads[0].wait()
    step = min(1024, width)

    def squares(k, total):
        part = xv[:, pl.ds(pl.multiple_of(k * step, step), step)].astype(F32)
        return total + jnp.sum(part * part, axis=1, keepdims=True)

    total = lax.fori_loop(0, width // step, squares, jnp.zeros((128, 1), F32))
    inv = lax.rsqrt(total / width + 1e-05)
    loads[1].wait()
    loads[2].wait()
    accq[...] = jnp.zeros_like(accq)

    def project(k, _):
        part = pl.ds(pl.multiple_of(k * step, step), step)
        gains = gain_f[pl.ds(pl.multiple_of(k * (step // 128), 8), step // 128), :]
        gains = jnp.concatenate([gains[r : r + 1] for r in range(step // 128)], axis=1)
        normed = (xv[:, part].astype(F32) * inv * gains).astype(BF16)
        accq[...] += nt(wv[:, part], normed)
        return 0

    lax.fori_loop(0, width // step, project, 0)
    loads[6].wait()
    cosine = rope[0]
    sine = rope[1]
    for b in range(9):
        front = accq[32 * b : 32 * b + 16, :]
        rear = accq[32 * b + 16 : 32 * b + 32, :]
        new_front = front * cosine - rear * sine
        new_rear = rear * cosine + front * sine
        if b < 8:
            new_front = new_front * HD ** (-0.5)
            new_rear = new_rear * HD ** (-0.5)
        qt[32 * b : 32 * b + 16, :] = new_front.astype(BF16)
        qt[32 * b + 16 : 32 * b + 32, :] = new_rear.astype(BF16)
    qt[288:320, :] = accq[288:320, :].astype(BF16)

    for third in range(3):
        for c in range(CAP):
            for gl in range(4):
                at = pl.ds((c * 4 + gl) * 128, 128)
                b = third * 4 + gl
                if b < 10:
                    spread[32 * c : 32 * c + 32, at] = qt[32 * b : 32 * b + 32, :]
                else:
                    spread[32 * c : 32 * c + 32, at] = jnp.zeros((32, 128), BF16)
        packed = nt(onehot[...], spread[...]).astype(BF16)
        sendq[:, 16 * third : 16 * third + 16, :] = packed.reshape(ng, 16, 128)

    def q_copy(k):
        there = lax.rem(g + k, ng)
        return pltpu.make_async_remote_copy(
            sendq.at[there], qx.at[i, g], qa_ssem.at[k], qa_rsem.at[k],
            device_id={"grp": there}, device_id_type=MESH)

    def q_share(o, k):
        here = lax.rem(g - k + ng, ng)
        return pltpu.make_async_remote_copy(
            qx.at[i, here], qx.at[i, here], qg_ssem.at[o - 1, k], qg_rsem.at[o - 1, k],
            device_id={"tp": mate(t, o)}, device_id_type=MESH)

    def q_arrival(o, k):
        here = lax.rem(g - k + ng, ng)
        return pltpu.make_async_remote_copy(
            qx.at[i, here], qx.at[block_of[o], here], qg_ssem.at[o - 1, k], qg_rsem.at[o - 1, k],
            device_id={"tp": mate(t, o)}, device_id_type=MESH)

    def q_start(k, _):
        q_copy(k).start()
        return 0

    def q_forward(k, _):
        q_copy(k).wait_recv()
        for o in (2, 1):
            q_share(o, k).start()
        return 0

    def q_relay(k):
        here = lax.rem(g - k + ng, ng)
        return pltpu.make_async_remote_copy(
            qx.at[block_of[2], here], qx.at[block_of[2], here], qg_ssem.at[2, k], qg_rsem.at[2, k],
            device_id={"tp": mate(t, 1)}, device_id_type=MESH)

    def hand_on(k):
        q_arrival(2, k).wait_recv()
        q_relay(k).start()

    lax.fori_loop(1, ng, q_start, 0)
    qx[i, g] = sendq[g]
    for o in (2, 1):
        q_share(o, 0).start()
    lax.fori_loop(1, ng, q_forward, 0)
    for move in value_moves[:EARLY]:
        move.start()

    fold_row = iota(fold.shape, 0)
    fold_lane = iota(fold.shape, 1)
    fold[...] = ones((fold_row // 128 == fold_lane // 32) & (fold_row % 32 == fold_lane % 32))
    diagonal = ones(row // 32 == lane // 32)
    stat[...] = jnp.zeros_like(stat)
    to_scalars.wait()

    def slots(k):
        there = lax.rem(g - k + ng, ng)
        return there, [ids_s[there // 4, (there % 4) * 32 + 32 - CAP + c] & 31 for c in range(CAP)]

    def scale_rows(n, kind, ids):
        return jnp.concatenate(
            [jnp.broadcast_to(scf[n, kind, pl.ds(ids[c], 1), :], (32, 128)) for c in range(CAP)], axis=0)

    def queries(n, there):
        return jnp.concatenate([qx[n, there, 0:32, :]] * CAP, axis=0) * diagonal

    def block_scores(o, there, ids):
        n = block_of[o]
        held = kn if o < 2 else kf
        keys = jnp.concatenate([held[core_of[o], ids[c]] for c in range(CAP)], axis=0)
        return nn(queries(n, there), keys) * scale_rows(n, 0, ids)

    own_cache[0].wait()
    own_cache[1].wait()
    for kind in (0, 1):
        key_moves[1][kind].wait_recv()
    key_moves[2][1].wait_recv()
    key_moves[3][1].wait_recv()
    scf[...] = scx[...].astype(F32)

    def each(first, last, width, body):
        width = min(width, last - first)

        def run(j, _):
            body([first + j * width + d for d in range(width)])
            return 0

        lax.fori_loop(0, (last - first) // width, run, 0)

    def score_near(ks):
        for k in ks:
            q_arrival(1, k).wait_recv()
        totals = []
        for k in ks:
            there, ids = slots(k)
            totals.append(block_scores(0, there, ids) + block_scores(1, there, ids))
        for k, total in zip(ks, totals):
            prob[k] = total

    each(0, ng, 2, score_near)

    def hand_all(k, _):
        hand_on(k)
        return 0

    lax.fori_loop(0, ng, hand_all, 0)
    key_moves[2][0].wait_recv()
    key_moves[3][0].wait_recv()
    pnew[...] = jnp.full(pnew.shape, -jnp.inf, F32)

    def far_arrival(k, _):
        q_arrival(3, k).wait_recv()
        return 0

    lax.fori_loop(0, ng, far_arrival, 0)
    first_new = (g - i + 4 * ng) % 4
    share = max(ng // 4, 1)

    def score_new(j, _):
        k = lax.rem(first_new + 4 * j, ng)
        there, _ = slots(k)
        new = jnp.zeros((128, 16), F32)
        for n in range(4):
            new = new + nt(queries(n, there), qx[n, there, 32:48, :])
        column = iota((128, 16), 1)
        seen = (column <= iota((128, 16), 0) % 4) & (column < 4)
        if ng < 4:
            seen = seen & (there == i)
        pnew[k] = jnp.where(seen, new, -jnp.inf)
        return 0

    lax.fori_loop(0, share, score_new, 0)

    def score_far(ks):
        done = []
        for k in ks:
            there, ids = slots(k)
            total = prob[k] + block_scores(2, there, ids) + block_scores(3, there, ids)
            new = pnew[k]
            top = jnp.maximum(jnp.max(total, axis=1, keepdims=True), jnp.max(new, axis=1, keepdims=True))
            part = jnp.exp(total - top)
            new = jnp.exp(new - top)
            mass = jnp.sum(part, axis=1, keepdims=True) + jnp.sum(new, axis=1, keepdims=True)
            done.append((part, new, top, mass))
        both = stat[...]
        for k, (part, new, top, mass) in zip(ks, done):
            prob[k] = part
            pnew[k] = new
            both = jnp.where(lane == k, top, jnp.where(lane == ng + k, mass, both))
        stat[...] = both

    each(0, ng, 2, score_far)

    st_send[...] = jnp.transpose(stat[...])[0 : 2 * ng, :]
    st_moves = [
        pltpu.make_async_remote_copy(
            st_send, st_recv.at[o - 1], st_ssem.at[o - 1], st_rsem.at[o - 1],
            device_id={"tp": mate(t, o)}, device_id_type=MESH)
        for o in (1, 2, 3)
    ]
    for o in (2, 1, 0):
        st_moves[o].start()
    for move in value_moves[EARLY:]:
        move.start()
    for o in range(3):
        st_moves[o].wait_recv()
    tops = [st_send[0:ng, :]] + [st_recv[o, 0:ng, :] for o in range(3)]
    masses = [st_send[ng : 2 * ng, :]] + [st_recv[o, ng : 2 * ng, :] for o in range(3)]
    top = jnp.maximum(jnp.maximum(tops[0], tops[1]), jnp.maximum(tops[2], tops[3]))
    mass = sum(masses[o] * jnp.exp(tops[o] - top) for o in range(4))
    factor = jnp.exp(tops[0] - top) / mass
    fac[...] = jnp.transpose(jnp.concatenate([factor, jnp.zeros((128 - ng, 128), F32)], axis=0))

    def keep(out):
        kept = jnp.zeros((32, 128), F32)
        for c in range(CAP):
            kept = kept + jnp.where(lane[0:32] // 32 == c, out[32 * c : 32 * c + 32, :], 0.0)
        return kept

    def value(ks, mates, first):
        if first:
            for k in ks:
                column = jnp.sum(jnp.where(lane == k, fac[...], 0.0), axis=1, keepdims=True)
                pb[k] = (prob[k] * column).astype(BF16)
        kept = []
        for k in ks:
            there, ids = slots(k)
            p = pb[k].astype(F32)
            for o in mates:
                weighted = (p * scale_rows(block_of[o], 1, ids)).astype(BF16)
                held = [vn.at[core], vn.at[1 - core], vl, vo][o]
                values = jnp.concatenate([held[ids[c]] for c in range(CAP)], axis=0)
                kept.append((block_of[o], k, keep(nt(weighted, values))))
        for n, k, out in kept:
            acc[n, k] = acc[n, k] + out

    def value_new(j, _):
        k = lax.rem(first_new + 4 * j, ng)
        there, _ = slots(k)
        pn = pnew[k].astype(BF16)
        for n in range(4):
            both = qx[n, there, 32:48, :].astype(F32)
            new_values = pltpu.roll(both, 12, 0).astype(BF16)
            acc[n, k] = keep(nn(pn, new_values))
        return 0

    def scale_new(j, _):
        k = lax.rem(first_new + 4 * j, ng)
        column = jnp.sum(jnp.where(lane == k, fac[...], 0.0), axis=1, keepdims=True)
        pnew[k] = pnew[k] * column
        return 0

    near_sum = pltpu.make_async_remote_copy(
        acc.at[block_of[1]], ra.at[0], ha_ssem.at[0], ha_rsem.at[0],
        device_id={"tp": mate(t, 1)}, device_id_type=MESH)

    def far_sum(q):
        at = pl.ds(q * per, per)
        return pltpu.make_async_remote_copy(
            acc.at[block_of[3], at], ra.at[1, at], ha_ssem.at[1 + q], ha_rsem.at[1 + q],
            device_id={"tp": mate(t, 1)}, device_id_type=MESH)

    def chip_sum(q):
        at = pl.ds(q * per, per)
        return pltpu.make_async_remote_copy(
            sb.at[at], rb.at[at], hb_ssem.at[q], hb_rsem.at[q],
            device_id={"tp": mate(t, 2)}, device_id_type=MESH)

    def back_copy(k):
        there = lax.rem(g - k + ng, ng)
        return pltpu.make_async_remote_copy(
            mix.at[k], back.at[g], bk_ssem.at[k], bk_rsem.at[k],
            device_id={"grp": there}, device_id_type=MESH)

    def back_start(k, _):
        back_copy(k).start()
        return 0

    def back_wait(k, _):
        back_copy(k).wait()
        return 0

    def send_chip_sum(q):
        at = pl.ds(q * per, per)
        far_sum(q).wait()
        sb[at] = (acc[block_of[2], at] + ra[1, at]).astype(BF16)
        chip_sum(q).start()

    def send_back(q):
        at = pl.ds(q * per, per)
        chip_sum(q).wait()
        mix[at] = (acc[i, at] + ra[0, at] + rb[at].astype(F32)).astype(BF16)
        lax.fori_loop(max(q * per, 1), (q + 1) * per, back_start, 0)

    acc[...] = jnp.zeros_like(acc)
    lax.fori_loop(0, share, scale_new, 0)
    lax.fori_loop(0, share, value_new, 0)
    own_cache[2].wait()
    for move in near_values:
        move.wait_recv()
    each(0, ng, 2, lambda ks: value(ks, (0, 1), True))
    near_sum.start()
    for move in value_moves[:PIECES]:
        move.wait_recv()
    for q in range(chunks):
        each(q * per, (q + 1) * per, 4, lambda ks: value(ks, (3,), False))
        far_sum(q).start()
    for move in value_moves[PIECES:]:
        move.wait_recv()
    for q in range(chunks):
        each(q * per, (q + 1) * per, 4, lambda ks: value(ks, (2,), False))
        send_chip_sum(q)
        if q == 0:
            near_sum.wait()
        else:
            send_back(q - 1)
    send_back(chunks - 1)
    back[g] = mix[0]
    lax.fori_loop(1, ng, back_wait, 0)

    wide = 32 * ng
    row_w = iota((128, wide), 0)
    lane_w = iota((128, wide), 1)
    hit = ((lane_w // 32).astype(F32) == src_col[:, 0:1]) & (lane_w % 4 == row_w // 32)
    chosen = rank_col[...] == (lane // 32).astype(F32)
    slots_all = back[...].reshape(wide, 128)
    mixed = jnp.zeros((128, 256), F32)
    for b in range(8):
        pick = ones(hit & ((lane_w // 4) % 8 == b))
        rows_b = jnp.where(chosen, nn(pick, slots_all), 0.0).astype(BF16)
        mixed = mixed + nn(rows_b, fold[128 * b : 128 * b + 128, :])
    mixed = mixed.astype(BF16)

    loads[3].wait()

    def columns(h, e, c):
        part, dy = BLOCKS[e]
        block = part * 8 + lax.rem(y + dy, 4) * 2 + c
        return pl.ds(pl.multiple_of((block * 2 + h) * half, 128), half)

    def ta_copy(h, e):
        return pltpu.make_async_remote_copy(
            ta_send.at[h, e], ta_recv.at[h, e], ta_ssem.at[h, e], ta_rsem.at[h, e],
            device_id={"tp": mate(t, 1)}, device_id_type=MESH)

    before = t + 2 * ((y + 3) % 4 - y)
    after = t + 2 * ((y + 1) % 4 - y)
    targets = (before, after, after, before, before, after)

    def tb_copy(h, e):
        return pltpu.make_async_remote_copy(
            tb_send.at[h, e], tb_recv.at[h, e], tb_ssem.at[h, e], tb_rsem.at[h, e],
            device_id={"tp": targets[e]}, device_id_type=MESH)

    def tc_copy(h):
        return pltpu.make_async_remote_copy(
            tc_send.at[h], tc_recv.at[h], tc_ssem.at[h], tc_rsem.at[h],
            device_id={"tp": flip(t, 8)}, device_id_type=MESH)

    def core_sum(h, e):
        ta_copy(h, e).wait()
        return own[h, e] + ta_recv[h, e].astype(F32)

    def first_step(h, pair):
        for e in pair:
            ta_send[h, e] = nn(mixed, wov[:, columns(h, e, 1 - core)]).astype(BF16)
            ta_copy(h, e).start()
        for e in pair:
            own[h, e] = nn(mixed, wov[:, columns(h, e, core)])

    def second_step(h, pair):
        for e in pair:
            summed = core_sum(h, e)
            if e in (4, 5):
                tb_copy(h, e - 4).wait()
                summed = summed + tb_recv[h, e - 4].astype(F32)
            if e < 6:
                tb_send[h, e] = summed.astype(BF16)
                tb_copy(h, e).start()
            else:
                fin[h, e - 6] = summed

    def last_step(h):
        for e in (2, 3, 4, 5):
            tb_copy(h, e).wait()
        fin[h, 0] = fin[h, 0] + tb_recv[h, 2].astype(F32) + tb_recv[h, 4].astype(F32)
        fin[h, 1] = fin[h, 1] + tb_recv[h, 3].astype(F32) + tb_recv[h, 5].astype(F32)
        tc_send[h] = fin[h, 1 - zh].astype(BF16)
        tc_copy(h).start()

    opposite, direct, joined, kept = (0, 1), (2, 3), (4, 5), (6, 7)
    first_step(0, opposite)
    first_step(0, direct)
    second_step(0, opposite)
    first_step(1, opposite)
    second_step(0, direct)
    first_step(0, joined)
    second_step(1, opposite)
    first_step(1, direct)
    second_step(0, joined)
    first_step(1, joined)
    second_step(1, direct)
    first_step(0, kept)
    first_step(1, kept)
    second_step(0, kept)
    second_step(1, joined)
    last_step(0)
    second_step(1, kept)
    last_step(1)
    for h in range(2):
        tc_copy(h).wait()
        out_ref[:, h * half : (h + 1) * half] = (fin[h, zh] + tc_recv[h].astype(F32)).astype(BF16)

    def q_sent(k, _):
        q_copy(k).wait_send()
        return 0

    def q_shared(k, _):
        for o in (1, 2):
            q_share(o, k).wait_send()
        q_relay(k).wait_send()
        return 0

    lax.fori_loop(1, ng, q_sent, 0)
    lax.fori_loop(0, ng, q_shared, 0)
    for o in (1, 2, 3):
        key_moves[o][0].wait_send()
        key_moves[o][1].wait_send()
        st_moves[o - 1].wait_send()
    for move in near_values + value_moves:
        move.wait_send()


def rope_tables(step_count, cached, particles):
    pair = np.arange(64, dtype=np.float32).reshape(4, 16)
    frequency = np.exp(-(pair / np.float32(64)) * np.log(np.float32(500000.0))).astype(np.float32)
    positions = (cached + np.arange(step_count)).astype(np.float32)
    angles = (positions[None, None, :] * frequency[:, :, None]).astype(np.float32)
    tables = np.stack([np.cos(angles), np.sin(angles)]).astype(np.float32)
    return np.repeat(tables, particles, axis=-1)


def shards(ng, inputs, norm_gain, w_query, w_keyval, w_out, kv_cache, kv_scales, ancestors):
    step_count, particles, width = inputs.shape
    cached = kv_cache.shape[3]
    rope = jnp.asarray(rope_tables(step_count, cached, particles))
    missing = -ancestors.shape[0] % 128
    if missing:
        ancestors = jnp.pad(ancestors, (0, missing), constant_values=-1)
    rows = step_count * particles
    cb = width // lax.axis_size("tp")
    half = cb // 2
    vmem = pl.BlockSpec(memory_space=pltpu.VMEM)
    hbm = pl.BlockSpec(memory_space=pltpu.HBM)
    dma = pltpu.SemaphoreType.DMA
    scratch = [
        pltpu.VMEM((rows, width), BF16),
        pltpu.VMEM((320, width), BF16),
        pltpu.VMEM((256, width), BF16),
        pltpu.VMEM((width // 128, 128), BF16),
        pltpu.VMEM((width // 128, 128), F32),
        pltpu.VMEM((2, 16, 128), F32),
        pltpu.VMEM((8, 128), jnp.int32),
        pltpu.VMEM((8, 128), jnp.int32),
        pltpu.SMEM((8, 128), jnp.int32),
        pltpu.VMEM((128, 128), F32),
        pltpu.VMEM((128, 128), F32),
        pltpu.VMEM((320, 128), F32),
        pltpu.VMEM((320, 128), BF16),
        pltpu.VMEM((ng * 16, 2048), BF16),
        pltpu.VMEM((128, 2048), BF16),
        pltpu.VMEM((ng, 48, 128), BF16),
        pltpu.VMEM((4, ng, 48, 128), BF16),
        pltpu.VMEM((2, particles, 32, 128), BF16),
        pltpu.VMEM((2, particles, 32, 128), BF16),
        pltpu.VMEM((2, particles, 32, 128), BF16),
        pltpu.VMEM((particles, 32, 128), BF16),
        pltpu.VMEM((particles, 32, 128), BF16),
        pltpu.VMEM((4, 2, particles, 128), BF16),
        pltpu.VMEM((4, 2, particles, 128), F32),
        pltpu.VMEM((ng, 128, 128), F32),
        pltpu.VMEM((ng, 128, 128), BF16),
        pltpu.VMEM((ng, 128, 16), F32),
        pltpu.VMEM((128, 128), F32),
        pltpu.VMEM((2 * ng, 128), F32),
        pltpu.VMEM((3, 2 * ng, 128), F32),
        pltpu.VMEM((128, 128), F32),
        pltpu.VMEM((4, ng, 32, 128), F32),
        pltpu.VMEM((2, ng, 32, 128), F32),
        pltpu.VMEM((ng, 32, 128), BF16),
        pltpu.VMEM((ng, 32, 128), BF16),
        pltpu.VMEM((ng, 32, 128), BF16),
        pltpu.VMEM((ng, 32, 128), BF16),
        pltpu.VMEM((1024, 256), BF16),
        pltpu.VMEM((2, 8, rows, half), BF16),
        pltpu.VMEM((2, 8, rows, half), BF16),
        pltpu.VMEM((2, 8, rows, half), F32),
        pltpu.VMEM((2, 6, rows, half), BF16),
        pltpu.VMEM((2, 6, rows, half), BF16),
        pltpu.VMEM((2, 2, rows, half), F32),
        pltpu.VMEM((2, rows, half), BF16),
        pltpu.VMEM((2, rows, half), BF16),
        dma((11,)),
        dma((3, 2)), dma((3, 2)),
        dma((3, PIECES)), dma((3, PIECES)),
        dma((ng,)), dma((ng,)),
        dma((3, ng)), dma((3, ng)),
        dma((3,)), dma((3,)),
        dma((1 + MAX_CHUNKS,)), dma((1 + MAX_CHUNKS,)),
        dma((MAX_CHUNKS,)), dma((MAX_CHUNKS,)),
        dma((ng,)), dma((ng,)),
        dma((2, 8)), dma((2, 8)),
        dma((2, 6)), dma((2, 6)),
        dma((2,)), dma((2,)),
    ]
    out = pl.pallas_call(
        functools.partial(kernel, ng),
        out_shape=jax.ShapeDtypeStruct((rows, cb), BF16),
        in_specs=[hbm] * 9,
        out_specs=vmem,
        scratch_shapes=scratch,
        compiler_params=pltpu.CompilerParams(
            collective_id=0, has_side_effects=True, vmem_limit_bytes=60 * 1024 * 1024),
    )(
        inputs.reshape(rows, width),
        norm_gain.reshape(width // 128, 128),
        jnp.transpose(w_query, (1, 2, 0)).reshape(256, width),
        jnp.transpose(w_keyval, (1, 2, 0)).reshape(64, width),
        w_out.reshape(256, width),
        kv_cache,
        kv_scales.reshape(2, particles, cached),
        rope,
        ancestors.reshape(-1, 128),
    )
    return out.reshape(step_count, particles, cb)


def solution(mesh):
    in_specs = (
        P(None, "grp", None),
        P(),
        P(None, None, "tp"),
        P(None, None, "tp"),
        P(None, "tp", None),
        P(None, "grp", "tp", None),
        P(None, "grp", "tp", None),
        P(),
    )
    out_specs = P(None, "grp", "tp")
    return jax.shard_map(
        functools.partial(shards, mesh.shape["grp"]), mesh=mesh, in_specs=in_specs, out_specs=out_specs,
        check_vma=False)
```

```python
import functools

import jax
import jax.numpy as jnp
import numpy as np
from jax import lax
from jax.experimental import pallas as pl
from jax.experimental.pallas import tpu as pltpu
from jax.sharding import PartitionSpec as P

HD = 128
CAP = 4
MESH = pl.DeviceIdType.MESH
F32 = jnp.float32
BF16 = jnp.bfloat16
MAX_CHUNKS = 4
PIECES = 4
EARLY = 5
BLOCKS = ((0, 2), (1, 2), (0, 1), (1, 3), (0, 3), (1, 1), (0, 0), (1, 0))


def flip(t, bit):
    return t + bit - 2 * bit * ((t // bit) % 2)


def mate(t, offset):
    if offset & 1:
        t = flip(t, 1)
    if offset & 2:
        t = flip(t, 2)
    return t


def nt(a, b):
    return lax.dot_general(a, b, (((1,), (1,)), ((), ())), preferred_element_type=F32)


def nn(a, b):
    return jnp.dot(a, b, preferred_element_type=F32)


def iota(shape, axis):
    return lax.broadcasted_iota(jnp.int32, shape, axis)


def kernel(
    ng, x_hbm, gain_hbm, wq_hbm, wkv_hbm, wo_hbm, kv_hbm, sc_hbm, rope_hbm, anc_hbm,
    out_ref,
    xv, wv, wov, gain_v, gain_f, rope, anc, ids_v, ids_s, src_col, rank_col,
    accq, qt, onehot, spread, sendq, qx, kn, kf, vn, vo, vl, scx, scf, prob, pb, pnew, stat, st_send, st_recv,
    fac, acc, ra, sb, rb, mix, back, fold, ta_send, ta_recv, own, tb_send, tb_recv, fin, tc_send, tc_recv,
    loc_sem, k_ssem, k_rsem, v_ssem, v_rsem, qa_ssem, qa_rsem, qg_ssem, qg_rsem, st_ssem, st_rsem, ha_ssem,
    ha_rsem, hb_ssem, hb_rsem, bk_ssem, bk_rsem, ta_ssem, ta_rsem, tb_ssem, tb_rsem, tc_ssem, tc_rsem,
):
    g = lax.axis_index("grp")
    t = lax.axis_index("tp")
    i = t % 4
    core = t % 2
    y = (t // 2) % 4
    zh = t // 8
    width = x_hbm.shape[1]
    half = out_ref.shape[1] // 2
    chunks = min(MAX_CHUNKS, ng)
    per = ng // chunks
    block_of = [mate(t, o) % 4 for o in range(4)]
    core_of = [core, 1 - core, core, 1 - core]

    loads = [
        pltpu.make_async_copy(x_hbm, xv, loc_sem.at[0]),
        pltpu.make_async_copy(wq_hbm, wv.at[pl.ds(0, 256)], loc_sem.at[1]),
        pltpu.make_async_copy(wkv_hbm, wv.at[pl.ds(256, 64)], loc_sem.at[2]),
        pltpu.make_async_copy(wo_hbm, wov, loc_sem.at[3]),
        pltpu.make_async_copy(anc_hbm, anc.at[pl.ds(0, anc_hbm.shape[0])], loc_sem.at[4]),
        pltpu.make_async_copy(gain_hbm, gain_v, loc_sem.at[5]),
        pltpu.make_async_copy(rope_hbm.at[:, i], rope, loc_sem.at[6]),
    ]
    anc[...] = jnp.full(anc.shape, -1, jnp.int32)
    for n in (4, 0, 5, 6, 1, 2):
        loads[n].start()

    barrier = pltpu.get_barrier_semaphore()
    tp_peers = [mate(t, 1), mate(t, 2), mate(t, 3), t + 2 * ((y + 3 - 2 * (y % 2)) % 4 - y), flip(t, 8)]

    def greet(k, _):
        pl.semaphore_signal(barrier, inc=1, device_id={"grp": lax.rem(g + k, ng)}, device_id_type=MESH)
        return 0

    for peer in tp_peers:
        pl.semaphore_signal(barrier, inc=1, device_id={"tp": peer}, device_id_type=MESH)
    lax.fori_loop(1, ng, greet, 0)
    pl.semaphore_wait(barrier, len(tp_peers) + ng - 1)

    def lanes_of(block):
        return pl.ds(pl.multiple_of(128 * block, 128), 128)

    def key_copies(o):
        args = dict(device_id={"tp": mate(t, o)}, device_id_type=MESH)
        lanes = lanes_of(block_of[o])
        return [
            pltpu.make_async_remote_copy(
                kv_hbm.at[0, :, :, lanes], (kn if o == 1 else kf).at[core], k_ssem.at[o - 1, 0], k_rsem.at[o - 1, 0], **args),
            pltpu.make_async_remote_copy(
                sc_hbm.at[:, :, lanes], scx.at[i], k_ssem.at[o - 1, 1], k_rsem.at[o - 1, 1], **args),
        ]

    piece = kv_hbm.shape[1] // PIECES

    def value_copy(o, j):
        at = pl.ds(j * piece, piece)
        return pltpu.make_async_remote_copy(
            kv_hbm.at[1, at, :, lanes_of(block_of[o])], (vn.at[core, at], vl.at[at], vo.at[at])[o - 1],
            v_ssem.at[o - 1, j], v_rsem.at[o - 1, j], device_id={"tp": mate(t, o)}, device_id_type=MESH)

    key_moves = {o: key_copies(o) for o in (1, 2, 3)}
    value_moves = [value_copy(o, j) for o in (3, 2) for j in range(PIECES)]
    near_values = [value_copy(1, j) for j in range(PIECES)]
    for o in (2, 3, 1):
        key_moves[o][1].start()
    for o in (2, 3, 1):
        key_moves[o][0].start()
    for move in near_values:
        move.start()
    own_cache = [
        pltpu.make_async_copy(kv_hbm.at[0, :, :, lanes_of(i)], kn.at[core], loc_sem.at[7]),
        pltpu.make_async_copy(sc_hbm.at[:, :, lanes_of(i)], scx.at[i], loc_sem.at[8]),
        pltpu.make_async_copy(kv_hbm.at[1, :, :, lanes_of(i)], vn.at[core], loc_sem.at[9]),
    ]
    for copy in own_cache:
        copy.start()
    loads[3].start()

    row = iota((128, 128), 0)
    lane = iota((128, 128), 1)

    def ones(where):
        return jnp.where(where, 1.0, 0.0).astype(BF16)

    loads[4].wait()
    parents = anc[...]
    source = parents >> 5
    wanted = source == g
    within = iota((8, 128), 1) % 32

    def running(v):
        for shift in (1, 2, 4, 8, 16):
            v = v + jnp.where(within >= shift, pltpu.roll(v, shift, 1), 0)
        return v

    place = running(wanted.astype(jnp.int32))
    ids = jnp.zeros((8, 128), jnp.int32)
    for c in range(CAP):
        at_slot = running(jnp.where(wanted & (place == c + 1), parents & 31, 0))
        ids = jnp.where(within == 32 - CAP + c, pltpu.roll(at_slot, (c + 1 - CAP) % 128, 1), ids)
    ids_v[...] = ids
    to_scalars = pltpu.make_async_copy(ids_v, ids_s, loc_sem.at[10])
    to_scalars.start()
    mine = jnp.sum(jnp.where(iota((8, 128), 0) == g // 4, source.astype(F32), 0.0), axis=0, keepdims=True)
    mine = nn(jnp.broadcast_to(mine, (8, 128)).astype(BF16), ones(row == (g % 4) * 32 + lane % 32))[0:1]
    mine = jnp.broadcast_to(mine, (128, 128))
    mine_col = jnp.transpose(mine)
    src_col[...] = mine_col
    rank = jnp.sum(jnp.where((mine == mine_col) & (row < lane % 32), 1.0, 0.0), axis=0, keepdims=True)
    rank_col[...] = jnp.transpose(jnp.broadcast_to(rank, (128, 128)))

    slot_row = iota((ng * 16, 128), 0)
    slot_lane = iota((ng * 16, 128), 1)
    hit = (mine[0:1] == (slot_row // 16).astype(F32)) & (slot_row % 4 == slot_lane // 32)
    for c in range(CAP):
        hit_c = hit & (rank == c)
        for gl in range(4):
            onehot[:, (c * 4 + gl) * 128 : (c * 4 + gl + 1) * 128] = ones(hit_c & ((slot_row // 4) % 4 == gl))
    spread[...] = jnp.zeros_like(spread)

    loads[5].wait()
    gain_f[...] = gain_v[...].astype(F32)
    loads[0].wait()
    step = min(1024, width)

    def squares(k, total):
        part = xv[:, pl.ds(pl.multiple_of(k * step, step), step)].astype(F32)
        return total + jnp.sum(part * part, axis=1, keepdims=True)

    total = lax.fori_loop(0, width // step, squares, jnp.zeros((128, 1), F32))
    inv = lax.rsqrt(total / width + 1e-05)
    loads[1].wait()
    loads[2].wait()
    accq[...] = jnp.zeros_like(accq)

    def project(k, _):
        part = pl.ds(pl.multiple_of(k * step, step), step)
        gains = gain_f[pl.ds(pl.multiple_of(k * (step // 128), 8), step // 128), :]
        gains = jnp.concatenate([gains[r : r + 1] for r in range(step // 128)], axis=1)
        normed = (xv[:, part].astype(F32) * inv * gains).astype(BF16)
        accq[...] += nt(wv[:, part], normed)
        return 0

    lax.fori_loop(0, width // step, project, 0)
    loads[6].wait()
    cosine = rope[0]
    sine = rope[1]
    for b in range(9):
        front = accq[32 * b : 32 * b + 16, :]
        rear = accq[32 * b + 16 : 32 * b + 32, :]
        new_front = front * cosine - rear * sine
        new_rear = rear * cosine + front * sine
        if b < 8:
            new_front = new_front * HD ** (-0.5)
            new_rear = new_rear * HD ** (-0.5)
        qt[32 * b : 32 * b + 16, :] = new_front.astype(BF16)
        qt[32 * b + 16 : 32 * b + 32, :] = new_rear.astype(BF16)
    qt[288:320, :] = accq[288:320, :].astype(BF16)

    for third in range(3):
        for c in range(CAP):
            for gl in range(4):
                at = pl.ds((c * 4 + gl) * 128, 128)
                b = third * 4 + gl
                if b < 10:
                    spread[32 * c : 32 * c + 32, at] = qt[32 * b : 32 * b + 32, :]
                else:
                    spread[32 * c : 32 * c + 32, at] = jnp.zeros((32, 128), BF16)
        packed = nt(onehot[...], spread[...]).astype(BF16)
        sendq[:, 16 * third : 16 * third + 16, :] = packed.reshape(ng, 16, 128)

    def q_copy(k):
        there = lax.rem(g + k, ng)
        return pltpu.make_async_remote_copy(
            sendq.at[there], qx.at[i, g], qa_ssem.at[k], qa_rsem.at[k],
            device_id={"grp": there}, device_id_type=MESH)

    def q_share(o, k):
        here = lax.rem(g - k + ng, ng)
        return pltpu.make_async_remote_copy(
            qx.at[i, here], qx.at[i, here], qg_ssem.at[o - 1, k], qg_rsem.at[o - 1, k],
            device_id={"tp": mate(t, o)}, device_id_type=MESH)

    def q_arrival(o, k):
        here = lax.rem(g - k + ng, ng)
        return pltpu.make_async_remote_copy(
            qx.at[i, here], qx.at[block_of[o], here], qg_ssem.at[o - 1, k], qg_rsem.at[o - 1, k],
            device_id={"tp": mate(t, o)}, device_id_type=MESH)

    def q_start(k, _):
        q_copy(k).start()
        return 0

    def q_forward(k, _):
        q_copy(k).wait_recv()
        for o in (2, 1):
            q_share(o, k).start()
        return 0

    def q_relay(k):
        here = lax.rem(g - k + ng, ng)
        return pltpu.make_async_remote_copy(
            qx.at[block_of[2], here], qx.at[block_of[2], here], qg_ssem.at[2, k], qg_rsem.at[2, k],
            device_id={"tp": mate(t, 1)}, device_id_type=MESH)

    def hand_on(k):
        q_arrival(2, k).wait_recv()
        q_relay(k).start()

    lax.fori_loop(1, ng, q_start, 0)
    qx[i, g] = sendq[g]
    for o in (2, 1):
        q_share(o, 0).start()
    lax.fori_loop(1, ng, q_forward, 0)
    for move in value_moves[:EARLY]:
        move.start()

    fold_row = iota(fold.shape, 0)
    fold_lane = iota(fold.shape, 1)
    fold[...] = ones((fold_row // 128 == fold_lane // 32) & (fold_row % 32 == fold_lane % 32))
    diagonal = ones(row // 32 == lane // 32)
    stat[...] = jnp.zeros_like(stat)
    to_scalars.wait()

    def slots(k):
        there = lax.rem(g - k + ng, ng)
        return there, [ids_s[there // 4, (there % 4) * 32 + 32 - CAP + c] & 31 for c in range(CAP)]

    def scale_rows(n, kind, ids):
        return jnp.concatenate(
            [jnp.broadcast_to(scf[n, kind, pl.ds(ids[c], 1), :], (32, 128)) for c in range(CAP)], axis=0)

    def queries(n, there):
        return jnp.concatenate([qx[n, there, 0:32, :]] * CAP, axis=0) * diagonal

    def block_scores(o, there, ids):
        n = block_of[o]
        held = kn if o < 2 else kf
        keys = jnp.concatenate([held[core_of[o], ids[c]] for c in range(CAP)], axis=0)
        return nn(queries(n, there), keys) * scale_rows(n, 0, ids)

    own_cache[0].wait()
    own_cache[1].wait()
    for kind in (0, 1):
        key_moves[1][kind].wait_recv()
    key_moves[2][1].wait_recv()
    key_moves[3][1].wait_recv()
    scf[...] = scx[...].astype(F32)

    def each(first, last, width, body):
        width = min(width, last - first)

        def run(j, _):
            body([first + j * width + d for d in range(width)])
            return 0

        lax.fori_loop(0, (last - first) // width, run, 0)

    def score_near(ks):
        for k in ks:
            q_arrival(1, k).wait_recv()
        totals = []
        for k in ks:
            there, ids = slots(k)
            totals.append(block_scores(0, there, ids) + block_scores(1, there, ids))
        for k, total in zip(ks, totals):
            prob[k] = total

    each(0, ng, 2, score_near)

    def hand_all(k, _):
        hand_on(k)
        return 0

    lax.fori_loop(0, ng, hand_all, 0)
    key_moves[2][0].wait_recv()
    key_moves[3][0].wait_recv()
    pnew[...] = jnp.full(pnew.shape, -jnp.inf, F32)

    def far_arrival(k, _):
        q_arrival(3, k).wait_recv()
        return 0

    lax.fori_loop(0, ng, far_arrival, 0)
    first_new = (g - i + 4 * ng) % 4
    share = max(ng // 4, 1)

    def score_new(j, _):
        k = lax.rem(first_new + 4 * j, ng)
        there, _ = slots(k)
        new = jnp.zeros((128, 16), F32)
        for n in range(4):
            new = new + nt(queries(n, there), qx[n, there, 32:48, :])
        column = iota((128, 16), 1)
        seen = (column <= iota((128, 16), 0) % 4) & (column < 4)
        if ng < 4:
            seen = seen & (there == i)
        pnew[k] = jnp.where(seen, new, -jnp.inf)
        return 0

    lax.fori_loop(0, share, score_new, 0)

    def score_far(ks):
        done = []
        for k in ks:
            there, ids = slots(k)
            total = prob[k] + block_scores(2, there, ids) + block_scores(3, there, ids)
            new = pnew[k]
            top = jnp.maximum(jnp.max(total, axis=1, keepdims=True), jnp.max(new, axis=1, keepdims=True))
            part = jnp.exp(total - top)
            new = jnp.exp(new - top)
            mass = jnp.sum(part, axis=1, keepdims=True) + jnp.sum(new, axis=1, keepdims=True)
            done.append((part, new, top, mass))
        both = stat[...]
        for k, (part, new, top, mass) in zip(ks, done):
            prob[k] = part
            pnew[k] = new
            both = jnp.where(lane == k, top, jnp.where(lane == ng + k, mass, both))
        stat[...] = both

    each(0, ng, 2, score_far)

    st_send[...] = jnp.transpose(stat[...])[0 : 2 * ng, :]
    st_moves = [
        pltpu.make_async_remote_copy(
            st_send, st_recv.at[o - 1], st_ssem.at[o - 1], st_rsem.at[o - 1],
            device_id={"tp": mate(t, o)}, device_id_type=MESH)
        for o in (1, 2, 3)
    ]
    for o in (2, 1, 0):
        st_moves[o].start()
    for move in value_moves[EARLY:]:
        move.start()
    for o in range(3):
        st_moves[o].wait_recv()
    tops = [st_send[0:ng, :]] + [st_recv[o, 0:ng, :] for o in range(3)]
    masses = [st_send[ng : 2 * ng, :]] + [st_recv[o, ng : 2 * ng, :] for o in range(3)]
    top = jnp.maximum(jnp.maximum(tops[0], tops[1]), jnp.maximum(tops[2], tops[3]))
    mass = sum(masses[o] * jnp.exp(tops[o] - top) for o in range(4))
    factor = jnp.exp(tops[0] - top) / mass
    fac[...] = jnp.transpose(jnp.concatenate([factor, jnp.zeros((128 - ng, 128), F32)], axis=0))

    def keep(out):
        kept = jnp.zeros((32, 128), F32)
        for c in range(CAP):
            kept = kept + jnp.where(lane[0:32] // 32 == c, out[32 * c : 32 * c + 32, :], 0.0)
        return kept

    def value(ks, mates, first):
        if first:
            for k in ks:
                column = jnp.sum(jnp.where(lane == k, fac[...], 0.0), axis=1, keepdims=True)
                pb[k] = (prob[k] * column).astype(BF16)
        kept = []
        for k in ks:
            there, ids = slots(k)
            p = pb[k].astype(F32)
            for o in mates:
                weighted = (p * scale_rows(block_of[o], 1, ids)).astype(BF16)
                held = [vn.at[core], vn.at[1 - core], vl, vo][o]
                values = jnp.concatenate([held[ids[c]] for c in range(CAP)], axis=0)
                kept.append((block_of[o], k, keep(nt(weighted, values))))
        for n, k, out in kept:
            acc[n, k] = acc[n, k] + out

    def value_new(j, _):
        k = lax.rem(first_new + 4 * j, ng)
        there, _ = slots(k)
        pn = pnew[k].astype(BF16)
        for n in range(4):
            both = qx[n, there, 32:48, :].astype(F32)
            new_values = pltpu.roll(both, 12, 0).astype(BF16)
            acc[n, k] = keep(nn(pn, new_values))
        return 0

    def scale_new(j, _):
        k = lax.rem(first_new + 4 * j, ng)
        column = jnp.sum(jnp.where(lane == k, fac[...], 0.0), axis=1, keepdims=True)
        pnew[k] = pnew[k] * column
        return 0

    near_sum = pltpu.make_async_remote_copy(
        acc.at[block_of[1]], ra.at[0], ha_ssem.at[0], ha_rsem.at[0],
        device_id={"tp": mate(t, 1)}, device_id_type=MESH)

    def far_sum(q):
        at = pl.ds(q * per, per)
        return pltpu.make_async_remote_copy(
            acc.at[block_of[3], at], ra.at[1, at], ha_ssem.at[1 + q], ha_rsem.at[1 + q],
            device_id={"tp": mate(t, 1)}, device_id_type=MESH)

    def chip_sum(q):
        at = pl.ds(q * per, per)
        return pltpu.make_async_remote_copy(
            sb.at[at], rb.at[at], hb_ssem.at[q], hb_rsem.at[q],
            device_id={"tp": mate(t, 2)}, device_id_type=MESH)

    def back_copy(k):
        there = lax.rem(g - k + ng, ng)
        return pltpu.make_async_remote_copy(
            mix.at[k], back.at[g], bk_ssem.at[k], bk_rsem.at[k],
            device_id={"grp": there}, device_id_type=MESH)

    def back_start(k, _):
        back_copy(k).start()
        return 0

    def back_wait(k, _):
        back_copy(k).wait()
        return 0

    def send_chip_sum(q):
        at = pl.ds(q * per, per)
        far_sum(q).wait()
        sb[at] = (acc[block_of[2], at] + ra[1, at]).astype(BF16)
        chip_sum(q).start()

    def send_back(q):
        at = pl.ds(q * per, per)
        chip_sum(q).wait()
        mix[at] = (acc[i, at] + ra[0, at] + rb[at].astype(F32)).astype(BF16)
        lax.fori_loop(max(q * per, 1), (q + 1) * per, back_start, 0)

    acc[...] = jnp.zeros_like(acc)
    lax.fori_loop(0, share, scale_new, 0)
    lax.fori_loop(0, share, value_new, 0)
    own_cache[2].wait()
    for move in near_values:
        move.wait_recv()
    each(0, ng, 2, lambda ks: value(ks, (0, 1), True))
    near_sum.start()
    for move in value_moves[:PIECES]:
        move.wait_recv()
    for q in range(chunks):
        each(q * per, (q + 1) * per, 4, lambda ks: value(ks, (3,), False))
        far_sum(q).start()
    for move in value_moves[PIECES:]:
        move.wait_recv()
    for q in range(chunks):
        each(q * per, (q + 1) * per, 4, lambda ks: value(ks, (2,), False))
        send_chip_sum(q)
    near_sum.wait()
    for q in range(chunks):
        send_back(q)
    back[g] = mix[0]
    lax.fori_loop(1, ng, back_wait, 0)

    wide = 32 * ng
    row_w = iota((128, wide), 0)
    lane_w = iota((128, wide), 1)
    hit = ((lane_w // 32).astype(F32) == src_col[:, 0:1]) & (lane_w % 4 == row_w // 32)
    chosen = rank_col[...] == (lane // 32).astype(F32)
    slots_all = back[...].reshape(wide, 128)
    mixed = jnp.zeros((128, 256), F32)
    for b in range(8):
        pick = ones(hit & ((lane_w // 4) % 8 == b))
        rows_b = jnp.where(chosen, nn(pick, slots_all), 0.0).astype(BF16)
        mixed = mixed + nn(rows_b, fold[128 * b : 128 * b + 128, :])
    mixed = mixed.astype(BF16)

    loads[3].wait()

    def columns(h, e, c):
        part, dy = BLOCKS[e]
        block = part * 8 + lax.rem(y + dy, 4) * 2 + c
        return pl.ds(pl.multiple_of((block * 2 + h) * half, 128), half)

    def ta_copy(h, e):
        return pltpu.make_async_remote_copy(
            ta_send.at[h, e], ta_recv.at[h, e], ta_ssem.at[h, e], ta_rsem.at[h, e],
            device_id={"tp": mate(t, 1)}, device_id_type=MESH)

    before = t + 2 * ((y + 3) % 4 - y)
    after = t + 2 * ((y + 1) % 4 - y)
    targets = (before, after, after, before, before, after)

    def tb_copy(u, e):
        return pltpu.make_async_remote_copy(
            tb_send.at[u, e], tb_recv.at[u, e], tb_ssem.at[u, e], tb_rsem.at[u, e],
            device_id={"tp": targets[e]}, device_id_type=MESH)

    def tc_copy(u):
        return pltpu.make_async_remote_copy(
            tc_send.at[u], tc_recv.at[u], tc_ssem.at[u], tc_rsem.at[u],
            device_id={"tp": flip(t, 8)}, device_id_type=MESH)

    quarter = half // 2

    def first_step(h, pair):
        for e in pair:
            ta_send[h, e] = nn(mixed, wov[:, columns(h, e, 1 - core)]).astype(BF16)
            ta_copy(h, e).start()
        for e in pair:
            own[h, e] = nn(mixed, wov[:, columns(h, e, core)])

    def second_step(u, pair):
        h, at = u // 2, pl.ds((u % 2) * quarter, quarter)
        for e in pair:
            if u % 2 == 0:
                ta_copy(h, e).wait()
            summed = own[h, e, :, at] + ta_recv[h, e, :, at].astype(F32)
            if e in (4, 5):
                tb_copy(u, e - 4).wait()
                summed = summed + tb_recv[u, e - 4].astype(F32)
            if e < 6:
                tb_send[u, e] = summed.astype(BF16)
                tb_copy(u, e).start()
            else:
                fin[u, e - 6] = summed

    def last_step(u):
        second_step(u, kept)
        for e in (2, 3, 4, 5):
            tb_copy(u, e).wait()
        fin[u, 0] = fin[u, 0] + tb_recv[u, 2].astype(F32) + tb_recv[u, 4].astype(F32)
        fin[u, 1] = fin[u, 1] + tb_recv[u, 3].astype(F32) + tb_recv[u, 5].astype(F32)
        tc_send[u] = fin[u, 1 - zh].astype(BF16)
        tc_copy(u).start()

    opposite, direct, joined, kept = (0, 1), (2, 3), (4, 5), (6, 7)
    first_step(0, opposite)
    first_step(0, direct)
    second_step(0, opposite)
    second_step(1, opposite)
    first_step(0, joined)
    second_step(0, direct)
    first_step(1, opposite)
    second_step(0, joined)
    second_step(1, direct)
    second_step(1, joined)
    first_step(1, direct)
    second_step(2, opposite)
    second_step(3, opposite)
    first_step(1, joined)
    second_step(2, direct)
    first_step(0, kept)
    second_step(2, joined)
    second_step(3, direct)
    last_step(0)
    first_step(1, kept)
    second_step(3, joined)
    last_step(1)
    last_step(2)
    last_step(3)
    for u in range(4):
        tc_copy(u).wait()
        out_ref[:, u * quarter : (u + 1) * quarter] = (fin[u, zh] + tc_recv[u].astype(F32)).astype(BF16)

    def q_sent(k, _):
        q_copy(k).wait_send()
        return 0

    def q_shared(k, _):
        for o in (1, 2):
            q_share(o, k).wait_send()
        q_relay(k).wait_send()
        return 0

    lax.fori_loop(1, ng, q_sent, 0)
    lax.fori_loop(0, ng, q_shared, 0)
    for o in (1, 2, 3):
        key_moves[o][0].wait_send()
        key_moves[o][1].wait_send()
        st_moves[o - 1].wait_send()
    for move in near_values + value_moves:
        move.wait_send()


def rope_tables(step_count, cached, particles):
    pair = np.arange(64, dtype=np.float32).reshape(4, 16)
    frequency = np.exp(-(pair / np.float32(64)) * np.log(np.float32(500000.0))).astype(np.float32)
    positions = (cached + np.arange(step_count)).astype(np.float32)
    angles = (positions[None, None, :] * frequency[:, :, None]).astype(np.float32)
    tables = np.stack([np.cos(angles), np.sin(angles)]).astype(np.float32)
    return np.repeat(tables, particles, axis=-1)


def shards(ng, inputs, norm_gain, w_query, w_keyval, w_out, kv_cache, kv_scales, ancestors):
    step_count, particles, width = inputs.shape
    cached = kv_cache.shape[3]
    rope = jnp.asarray(rope_tables(step_count, cached, particles))
    missing = -ancestors.shape[0] % 128
    if missing:
        ancestors = jnp.pad(ancestors, (0, missing), constant_values=-1)
    rows = step_count * particles
    cb = width // lax.axis_size("tp")
    half = cb // 2
    vmem = pl.BlockSpec(memory_space=pltpu.VMEM)
    hbm = pl.BlockSpec(memory_space=pltpu.HBM)
    dma = pltpu.SemaphoreType.DMA
    scratch = [
        pltpu.VMEM((rows, width), BF16),
        pltpu.VMEM((320, width), BF16),
        pltpu.VMEM((256, width), BF16),
        pltpu.VMEM((width // 128, 128), BF16),
        pltpu.VMEM((width // 128, 128), F32),
        pltpu.VMEM((2, 16, 128), F32),
        pltpu.VMEM((8, 128), jnp.int32),
        pltpu.VMEM((8, 128), jnp.int32),
        pltpu.SMEM((8, 128), jnp.int32),
        pltpu.VMEM((128, 128), F32),
        pltpu.VMEM((128, 128), F32),
        pltpu.VMEM((320, 128), F32),
        pltpu.VMEM((320, 128), BF16),
        pltpu.VMEM((ng * 16, 2048), BF16),
        pltpu.VMEM((128, 2048), BF16),
        pltpu.VMEM((ng, 48, 128), BF16),
        pltpu.VMEM((4, ng, 48, 128), BF16),
        pltpu.VMEM((2, particles, 32, 128), BF16),
        pltpu.VMEM((2, particles, 32, 128), BF16),
        pltpu.VMEM((2, particles, 32, 128), BF16),
        pltpu.VMEM((particles, 32, 128), BF16),
        pltpu.VMEM((particles, 32, 128), BF16),
        pltpu.VMEM((4, 2, particles, 128), BF16),
        pltpu.VMEM((4, 2, particles, 128), F32),
        pltpu.VMEM((ng, 128, 128), F32),
        pltpu.VMEM((ng, 128, 128), BF16),
        pltpu.VMEM((ng, 128, 16), F32),
        pltpu.VMEM((128, 128), F32),
        pltpu.VMEM((2 * ng, 128), F32),
        pltpu.VMEM((3, 2 * ng, 128), F32),
        pltpu.VMEM((128, 128), F32),
        pltpu.VMEM((4, ng, 32, 128), F32),
        pltpu.VMEM((2, ng, 32, 128), F32),
        pltpu.VMEM((ng, 32, 128), BF16),
        pltpu.VMEM((ng, 32, 128), BF16),
        pltpu.VMEM((ng, 32, 128), BF16),
        pltpu.VMEM((ng, 32, 128), BF16),
        pltpu.VMEM((1024, 256), BF16),
        pltpu.VMEM((2, 8, rows, half), BF16),
        pltpu.VMEM((2, 8, rows, half), BF16),
        pltpu.VMEM((2, 8, rows, half), F32),
        pltpu.VMEM((4, 6, rows, half // 2), BF16),
        pltpu.VMEM((4, 6, rows, half // 2), BF16),
        pltpu.VMEM((4, 2, rows, half // 2), F32),
        pltpu.VMEM((4, rows, half // 2), BF16),
        pltpu.VMEM((4, rows, half // 2), BF16),
        dma((11,)),
        dma((3, 2)), dma((3, 2)),
        dma((3, PIECES)), dma((3, PIECES)),
        dma((ng,)), dma((ng,)),
        dma((3, ng)), dma((3, ng)),
        dma((3,)), dma((3,)),
        dma((1 + MAX_CHUNKS,)), dma((1 + MAX_CHUNKS,)),
        dma((MAX_CHUNKS,)), dma((MAX_CHUNKS,)),
        dma((ng,)), dma((ng,)),
        dma((2, 8)), dma((2, 8)),
        dma((4, 6)), dma((4, 6)),
        dma((4,)), dma((4,)),
    ]
    out = pl.pallas_call(
        functools.partial(kernel, ng),
        out_shape=jax.ShapeDtypeStruct((rows, cb), BF16),
        in_specs=[hbm] * 9,
        out_specs=vmem,
        scratch_shapes=scratch,
        compiler_params=pltpu.CompilerParams(
            collective_id=0, has_side_effects=True, vmem_limit_bytes=60 * 1024 * 1024),
    )(
        inputs.reshape(rows, width),
        norm_gain.reshape(width // 128, 128),
        jnp.transpose(w_query, (1, 2, 0)).reshape(256, width),
        jnp.transpose(w_keyval, (1, 2, 0)).reshape(64, width),
        w_out.reshape(256, width),
        kv_cache,
        kv_scales.reshape(2, particles, cached),
        rope,
        ancestors.reshape(-1, 128),
    )
    return out.reshape(step_count, particles, cb)


def solution(mesh):
    in_specs = (
        P(None, "grp", None),
        P(),
        P(None, None, "tp"),
        P(None, None, "tp"),
        P(None, "tp", None),
        P(None, "grp", "tp", None),
        P(None, "grp", "tp", None),
        P(),
    )
    out_specs = P(None, "grp", "tp")
    return jax.shard_map(
        functools.partial(shards, mesh.shape["grp"]), mesh=mesh, in_specs=in_specs, out_specs=out_specs,
        check_vma=False)
```

```python
import functools

import jax
import jax.numpy as jnp
import numpy as np
from jax import lax
from jax.experimental import pallas as pl
from jax.experimental.pallas import tpu as pltpu
from jax.sharding import PartitionSpec as P

HD = 128
CAP = 4
MESH = pl.DeviceIdType.MESH
F32 = jnp.float32
BF16 = jnp.bfloat16
MAX_CHUNKS = 4
PIECES = 4
BLOCKS = ((0, 2), (1, 2), (0, 1), (1, 3), (0, 3), (1, 1), (0, 0), (1, 0))


def flip(t, bit):
    return t + bit - 2 * bit * ((t // bit) % 2)


def mate(t, offset):
    if offset & 1:
        t = flip(t, 1)
    if offset & 2:
        t = flip(t, 2)
    return t


def nt(a, b):
    return lax.dot_general(a, b, (((1,), (1,)), ((), ())), preferred_element_type=F32)


def nn(a, b):
    return jnp.dot(a, b, preferred_element_type=F32)


def iota(shape, axis):
    return lax.broadcasted_iota(jnp.int32, shape, axis)


def kernel(
    ng, x_hbm, gain_hbm, wq_hbm, wkv_hbm, wo_hbm, kv_hbm, sc_hbm, rope_hbm, anc_hbm,
    out_ref,
    xv, wv, wov, gain_v, gain_f, rope, anc, ids_v, ids_s, src_col, rank_col,
    accq, qt, onehot, spread, sendq, qx, kn, kf, vown, sv, svf, scx, scf, prob, px, pnp, pnew, stat, st_send, st_recv,
    facn, fac, mix, back, picks, fold, ta_send, ta_recv, own, tb_send, tb_recv, fin, tc_send, tc_recv,
    loc_sem, k_ssem, k_rsem, p_ssem, p_rsem, pn_ssem, pn_rsem, qa_ssem, qa_rsem, qg_ssem, qg_rsem, st_ssem, st_rsem,
    bk_ssem, bk_rsem, ta_ssem, ta_rsem, tb_ssem, tb_rsem, tc_ssem, tc_rsem,
):
    g = lax.axis_index("grp")
    t = lax.axis_index("tp")
    i = t % 4
    core = t % 2
    y = (t // 2) % 4
    zh = t // 8
    width = x_hbm.shape[1]
    half = out_ref.shape[1] // 2
    chunks = min(MAX_CHUNKS, ng)
    per = ng // chunks
    block_of = [mate(t, o) % 4 for o in range(4)]
    core_of = [core, 1 - core, core, 1 - core]

    loads = [
        pltpu.make_async_copy(x_hbm, xv, loc_sem.at[0]),
        pltpu.make_async_copy(wq_hbm, wv.at[pl.ds(0, 256)], loc_sem.at[1]),
        pltpu.make_async_copy(wkv_hbm, wv.at[pl.ds(256, 64)], loc_sem.at[2]),
        pltpu.make_async_copy(wo_hbm, wov, loc_sem.at[3]),
        pltpu.make_async_copy(anc_hbm, anc.at[pl.ds(0, anc_hbm.shape[0])], loc_sem.at[4]),
        pltpu.make_async_copy(gain_hbm, gain_v, loc_sem.at[5]),
        pltpu.make_async_copy(rope_hbm.at[:, i], rope, loc_sem.at[6]),
    ]
    anc[...] = jnp.full(anc.shape, -1, jnp.int32)
    for n in (4, 0, 5, 6, 1, 2):
        loads[n].start()

    barrier = pltpu.get_barrier_semaphore()
    tp_peers = [mate(t, 1), mate(t, 2), mate(t, 3), t + 2 * ((y + 3 - 2 * (y % 2)) % 4 - y), flip(t, 8)]

    def greet(k, _):
        pl.semaphore_signal(barrier, inc=1, device_id={"grp": lax.rem(g + k, ng)}, device_id_type=MESH)
        return 0

    for peer in tp_peers:
        pl.semaphore_signal(barrier, inc=1, device_id={"tp": peer}, device_id_type=MESH)
    lax.fori_loop(1, ng, greet, 0)
    pl.semaphore_wait(barrier, len(tp_peers) + ng - 1)

    def lanes_of(block):
        return pl.ds(pl.multiple_of(128 * block, 128), 128)

    def key_copies(o):
        args = dict(device_id={"tp": mate(t, o)}, device_id_type=MESH)
        lanes = lanes_of(block_of[o])
        piece = kv_hbm.shape[1] // PIECES
        pieces = [pl.ds(j * piece, piece) for j in range(PIECES)]
        held = kn if o == 1 else kf
        return [
            pltpu.make_async_remote_copy(
                kv_hbm.at[0, at, :, lanes], held.at[core, at], k_ssem.at[o - 1, j], k_rsem.at[o - 1, j], **args)
            for j, at in enumerate(pieces)
        ] + [
            pltpu.make_async_remote_copy(
                sc_hbm.at[:, :, lanes], scx.at[i], k_ssem.at[o - 1, PIECES], k_rsem.at[o - 1, PIECES], **args),
        ]

    key_moves = {o: key_copies(o) for o in (1, 2, 3)}
    for o in (2, 3, 1):
        key_moves[o][PIECES].start()
    for j in range(PIECES - 1):
        for o in (2, 3, 1):
            key_moves[o][j].start()
    key_moves[1][PIECES - 1].start()
    own_cache = [
        pltpu.make_async_copy(kv_hbm.at[0, :, :, lanes_of(i)], kn.at[core], loc_sem.at[7]),
        pltpu.make_async_copy(sc_hbm.at[:, :, lanes_of(i)], scx.at[i], loc_sem.at[8]),
    ]
    for b in range(4):
        at = pl.ds(128 * b, 128)
        own_cache.append(pltpu.make_async_copy(kv_hbm.at[1, :, :, at], vown.at[b], loc_sem.at[11 + b]))
        own_cache.append(pltpu.make_async_copy(sc_hbm.at[1, :, at], sv.at[b], loc_sem.at[15 + b]))
    for copy in own_cache:
        copy.start()
    loads[3].start()

    row = iota((128, 128), 0)
    lane = iota((128, 128), 1)

    def ones(where):
        return jnp.where(where, 1.0, 0.0).astype(BF16)

    loads[4].wait()
    parents = anc[...]
    source = parents >> 5
    wanted = source == g
    within = iota((8, 128), 1) % 32

    def running(v):
        for shift in (1, 2, 4, 8, 16):
            v = v + jnp.where(within >= shift, pltpu.roll(v, shift, 1), 0)
        return v

    place = running(wanted.astype(jnp.int32))
    ids = jnp.zeros((8, 128), jnp.int32)
    for c in range(CAP):
        at_slot = running(jnp.where(wanted & (place == c + 1), parents & 31, 0))
        ids = jnp.where(within == 32 - CAP + c, pltpu.roll(at_slot, (c + 1 - CAP) % 128, 1), ids)
    ids_v[...] = ids
    to_scalars = pltpu.make_async_copy(ids_v, ids_s, loc_sem.at[10])
    to_scalars.start()
    mine = jnp.sum(jnp.where(iota((8, 128), 0) == g // 4, source.astype(F32), 0.0), axis=0, keepdims=True)
    mine = nn(jnp.broadcast_to(mine, (8, 128)).astype(BF16), ones(row == (g % 4) * 32 + lane % 32))[0:1]
    mine = jnp.broadcast_to(mine, (128, 128))
    mine_col = jnp.transpose(mine)
    src_col[...] = mine_col
    rank = jnp.sum(jnp.where((mine == mine_col) & (row < lane % 32), 1.0, 0.0), axis=0, keepdims=True)
    rank_col[...] = jnp.transpose(jnp.broadcast_to(rank, (128, 128)))

    slot_row = iota((ng * 16, 128), 0)
    slot_lane = iota((ng * 16, 128), 1)
    hit = (mine[0:1] == (slot_row // 16).astype(F32)) & (slot_row % 4 == slot_lane // 32)
    for c in range(CAP):
        hit_c = hit & (rank == c)
        for gl in range(4):
            onehot[:, (c * 4 + gl) * 128 : (c * 4 + gl + 1) * 128] = ones(hit_c & ((slot_row // 4) % 4 == gl))
    spread[...] = jnp.zeros_like(spread)

    loads[5].wait()
    gain_f[...] = gain_v[...].astype(F32)
    loads[0].wait()
    step = min(1024, width)

    def squares(k, total):
        part = xv[:, pl.ds(pl.multiple_of(k * step, step), step)].astype(F32)
        return total + jnp.sum(part * part, axis=1, keepdims=True)

    total = lax.fori_loop(0, width // step, squares, jnp.zeros((128, 1), F32))
    inv = lax.rsqrt(total / width + 1e-05)
    loads[1].wait()
    loads[2].wait()
    accq[...] = jnp.zeros_like(accq)

    def project(k, _):
        part = pl.ds(pl.multiple_of(k * step, step), step)
        gains = gain_f[pl.ds(pl.multiple_of(k * (step // 128), 8), step // 128), :]
        gains = jnp.concatenate([gains[r : r + 1] for r in range(step // 128)], axis=1)
        normed = (xv[:, part].astype(F32) * inv * gains).astype(BF16)
        accq[...] += nt(wv[:, part], normed)
        return 0

    lax.fori_loop(0, width // step, project, 0)
    loads[6].wait()
    cosine = rope[0]
    sine = rope[1]
    for b in range(9):
        front = accq[32 * b : 32 * b + 16, :]
        rear = accq[32 * b + 16 : 32 * b + 32, :]
        new_front = front * cosine - rear * sine
        new_rear = rear * cosine + front * sine
        if b < 8:
            new_front = new_front * HD ** (-0.5)
            new_rear = new_rear * HD ** (-0.5)
        qt[32 * b : 32 * b + 16, :] = new_front.astype(BF16)
        qt[32 * b + 16 : 32 * b + 32, :] = new_rear.astype(BF16)
    qt[288:320, :] = accq[288:320, :].astype(BF16)

    for third in range(3):
        for c in range(CAP):
            for gl in range(4):
                at = pl.ds((c * 4 + gl) * 128, 128)
                b = third * 4 + gl
                if b < 10:
                    spread[32 * c : 32 * c + 32, at] = qt[32 * b : 32 * b + 32, :]
                else:
                    spread[32 * c : 32 * c + 32, at] = jnp.zeros((32, 128), BF16)
        packed = nt(onehot[...], spread[...]).astype(BF16)
        sendq[:, 16 * third : 16 * third + 16, :] = packed.reshape(ng, 16, 128)

    def q_copy(k):
        there = lax.rem(g + k, ng)
        return pltpu.make_async_remote_copy(
            sendq.at[there], qx.at[i, g], qa_ssem.at[k], qa_rsem.at[k],
            device_id={"grp": there}, device_id_type=MESH)

    def q_share(o, k):
        here = lax.rem(g - k + ng, ng)
        return pltpu.make_async_remote_copy(
            qx.at[i, here], qx.at[i, here], qg_ssem.at[o - 1, k], qg_rsem.at[o - 1, k],
            device_id={"tp": mate(t, o)}, device_id_type=MESH)

    def q_arrival(o, k):
        here = lax.rem(g - k + ng, ng)
        return pltpu.make_async_remote_copy(
            qx.at[i, here], qx.at[block_of[o], here], qg_ssem.at[o - 1, k], qg_rsem.at[o - 1, k],
            device_id={"tp": mate(t, o)}, device_id_type=MESH)

    def q_start(k, _):
        q_copy(k).start()
        return 0

    def q_forward(k, _):
        q_copy(k).wait_recv()
        for o in (2, 1):
            q_share(o, k).start()
        return 0

    def q_relay(k):
        here = lax.rem(g - k + ng, ng)
        return pltpu.make_async_remote_copy(
            qx.at[block_of[2], here], qx.at[block_of[2], here], qg_ssem.at[2, k], qg_rsem.at[2, k],
            device_id={"tp": mate(t, 1)}, device_id_type=MESH)

    def hand_on(k):
        q_arrival(2, k).wait_recv()
        q_relay(k).start()

    lax.fori_loop(1, ng, q_start, 0)
    qx[i, g] = sendq[g]
    for o in (2, 1):
        q_share(o, 0).start()
    lax.fori_loop(1, ng, q_forward, 0)
    for o in (2, 3):
        key_moves[o][PIECES - 1].start()

    fold_row = iota(fold.shape, 0)
    fold_lane = iota(fold.shape, 1)
    fold[...] = ones((fold_row // 128 == fold_lane // 32) & (fold_row % 32 == fold_lane % 32))
    wide = 32 * ng
    row_w = iota((128, wide), 0)
    lane_w = iota((128, wide), 1)
    hit = ((lane_w // 32).astype(F32) == src_col[:, 0:1]) & (lane_w % 4 == row_w // 32)
    for b in range(8):
        picks[b] = ones(hit & ((lane_w // 4) % 8 == b))
    diagonal = ones(row // 32 == lane // 32)
    stat[...] = jnp.zeros_like(stat)
    to_scalars.wait()

    def slots(k):
        there = lax.rem(g - k + ng, ng)
        return there, [ids_s[there // 4, (there % 4) * 32 + 32 - CAP + c] & 31 for c in range(CAP)]

    def scale_rows(n, kind, ids):
        return jnp.concatenate(
            [jnp.broadcast_to(scf[n, kind, pl.ds(ids[c], 1), :], (32, 128)) for c in range(CAP)], axis=0)

    def queries(n, there):
        return jnp.concatenate([qx[n, there, 0:32, :]] * CAP, axis=0) * diagonal

    def block_scores(o, there, ids):
        n = block_of[o]
        held = kn if o < 2 else kf
        keys = jnp.concatenate([held[core_of[o], ids[c]] for c in range(CAP)], axis=0)
        return nn(queries(n, there), keys) * scale_rows(n, 0, ids)

    own_cache[0].wait()
    own_cache[1].wait()
    for move in key_moves[1]:
        move.wait_recv()
    key_moves[2][PIECES].wait_recv()
    key_moves[3][PIECES].wait_recv()
    scf[...] = scx[...].astype(F32)

    def each(first, last, width, body):
        width = min(width, last - first)

        def run(j, _):
            body([first + j * width + d for d in range(width)])
            return 0

        lax.fori_loop(0, (last - first) // width, run, 0)

    def score_near(ks):
        for k in ks:
            q_arrival(1, k).wait_recv()
        totals = []
        for k in ks:
            there, ids = slots(k)
            totals.append(block_scores(0, there, ids) + block_scores(1, there, ids))
        for k, total in zip(ks, totals):
            prob[k] = total

    each(0, ng, 2, score_near)

    def hand_all(k, _):
        hand_on(k)
        return 0

    lax.fori_loop(0, ng, hand_all, 0)
    pnew[...] = jnp.full(pnew.shape, -jnp.inf, F32)

    def far_arrival(k, _):
        q_arrival(3, k).wait_recv()
        return 0

    lax.fori_loop(0, ng, far_arrival, 0)
    first_new = (g - i + 4 * ng) % 4
    share = max(ng // 4, 1)

    column = iota((128, 16), 1)
    seen = (column <= iota((128, 16), 0) % 4) & (column < 4)
    news = []
    for j in range(share):
        k = lax.rem(first_new + 4 * j, ng)
        there, _ = slots(k)
        new = jnp.zeros((128, 16), F32)
        for n in range(4):
            new = new + nt(queries(n, there), qx[n, there, 32:48, :])
        mine_too = seen & (there == i) if ng < 4 else seen
        news.append((k, jnp.where(mine_too, new, -jnp.inf)))
    for k, new in news:
        pnew[k] = new

    def score_far(ks):
        done = []
        for k in ks:
            there, ids = slots(k)
            total = prob[k] + block_scores(2, there, ids) + block_scores(3, there, ids)
            new = pnew[k]
            top = jnp.maximum(jnp.max(total, axis=1, keepdims=True), jnp.max(new, axis=1, keepdims=True))
            part = jnp.exp(total - top)
            new = jnp.exp(new - top)
            mass = jnp.sum(part, axis=1, keepdims=True) + jnp.sum(new, axis=1, keepdims=True)
            done.append((part, new, top, mass))
        both = stat[...]
        for k, (part, new, top, mass) in zip(ks, done):
            px[i, k] = part.astype(BF16)
            pnew[k] = new
            both = jnp.where(lane == k, top, jnp.where(lane == ng + k, mass, both))
        stat[...] = both

    for o in (2, 3):
        for move in key_moves[o][:PIECES]:
            move.wait_recv()

    def p_at(q):
        return pl.ds(q * per, per)

    def p_copy(o, q):
        return pltpu.make_async_remote_copy(
            px.at[i, p_at(q)], px.at[i, p_at(q)], p_ssem.at[o - 1, q], p_rsem.at[o - 1, q],
            device_id={"tp": mate(t, o)}, device_id_type=MESH)

    def p_arrival(o, q):
        return pltpu.make_async_remote_copy(
            px.at[i, p_at(q)], px.at[block_of[o], p_at(q)], p_ssem.at[o - 1, q], p_rsem.at[o - 1, q],
            device_id={"tp": mate(t, o)}, device_id_type=MESH)

    def p_relay(q):
        return pltpu.make_async_remote_copy(
            px.at[block_of[2], p_at(q)], px.at[block_of[2], p_at(q)], p_ssem.at[2, q], p_rsem.at[2, q],
            device_id={"tp": mate(t, 1)}, device_id_type=MESH)

    for q in range(chunks):
        each(q * per, (q + 1) * per, 2, score_far)
        if q < chunks - 1:
            p_copy(2, q).start()
            p_copy(1, q).start()
    packed = jnp.zeros((128, 128), F32)
    for j in range(share):
        new = pnew[lax.rem(first_new + 4 * j, ng)]
        packed = jnp.where(lane // 16 == j, jnp.concatenate([new] * 8, axis=1), packed)
    pnp[i] = packed.astype(BF16)
    pn_moves = [
        pltpu.make_async_remote_copy(
            pnp.at[i], pnp.at[i], pn_ssem.at[o - 1], pn_rsem.at[o - 1],
            device_id={"tp": mate(t, o)}, device_id_type=MESH)
        for o in (1, 2, 3)
    ]
    pn_arrivals = [
        pltpu.make_async_remote_copy(
            pnp.at[i], pnp.at[block_of[o]], pn_ssem.at[o - 1], pn_rsem.at[o - 1],
            device_id={"tp": mate(t, o)}, device_id_type=MESH)
        for o in (1, 2, 3)
    ]

    st_send[...] = jnp.transpose(stat[...])[0 : 2 * ng, :]
    st_moves = [
        pltpu.make_async_remote_copy(
            st_send, st_recv.at[o - 1], st_ssem.at[o - 1], st_rsem.at[o - 1],
            device_id={"tp": mate(t, o)}, device_id_type=MESH)
        for o in (1, 2, 3)
    ]
    for o in (2, 1, 0):
        st_moves[o].start()
    for o in (2, 1, 0):
        pn_moves[o].start()
    p_copy(2, chunks - 1).start()
    p_copy(1, chunks - 1).start()
    for copy in own_cache[2:]:
        copy.wait()
    svf[...] = sv[...].astype(F32)
    for o in range(3):
        st_moves[o].wait_recv()
        pn_arrivals[o].wait_recv()
    tops = [st_send[0:ng, :]] + [st_recv[o, 0:ng, :] for o in range(3)]
    masses = [st_send[ng : 2 * ng, :]] + [st_recv[o, ng : 2 * ng, :] for o in range(3)]
    top = jnp.maximum(jnp.maximum(tops[0], tops[1]), jnp.maximum(tops[2], tops[3]))
    mass = sum(masses[o] * jnp.exp(tops[o] - top) for o in range(4))
    for o in range(4):
        facn[block_of[o]] = jnp.exp(tops[o] - top) / mass
    factors = [facn[n] for n in range(4)]
    if 4 * ng < 128:
        factors.append(jnp.zeros((128 - 4 * ng, 128), F32))
    fac[...] = jnp.transpose(jnp.concatenate(factors, axis=0))

    def keep(out):
        kept = jnp.zeros((32, 128), F32)
        for c in range(CAP):
            kept = kept + jnp.where(lane[0:32] // 32 == c, out[32 * c : 32 * c + 32, :], 0.0)
        return kept

    def factor_of(n, k):
        return jnp.sum(jnp.where(lane == n * ng + k, fac[...], 0.0), axis=1, keepdims=True)

    def value(ks):
        kept = []
        for k in ks:
            there, ids = slots(k)
            out = jnp.zeros((128, 128), F32)
            for n in range(4):
                scales = jnp.concatenate(
                    [jnp.broadcast_to(svf[n, pl.ds(ids[c], 1), :], (32, 128)) for c in range(CAP)], axis=0)
                weighted = (px[n, k].astype(F32) * factor_of(n, k) * scales).astype(BF16)
                values = jnp.concatenate([vown[n, ids[c]] for c in range(CAP)], axis=0)
                out = out + nt(weighted, values)
            n = there % 4
            new_probs = (pnp[n].astype(F32) * factor_of(n, k)).astype(BF16)
            both = pltpu.roll(qx[i, there, 32:48, :].astype(F32), 12, 0)
            new_values = jnp.where(row // 16 == k // 4, jnp.concatenate([both] * 8, axis=0), 0.0).astype(BF16)
            kept.append(keep(out + nn(new_probs, new_values)).astype(BF16))
        for k, out in zip(ks, kept):
            mix[k] = out

    def back_copy(k):
        there = lax.rem(g - k + ng, ng)
        return pltpu.make_async_remote_copy(
            mix.at[k], back.at[g], bk_ssem.at[k], bk_rsem.at[k],
            device_id={"grp": there}, device_id_type=MESH)

    def back_start(k, _):
        back_copy(k).start()
        return 0

    def back_wait(k, _):
        back_copy(k).wait()
        return 0

    def hand_on_p(q):
        p_arrival(2, q).wait_recv()
        p_relay(q).start()

    hand_on_p(0)
    for q in range(chunks):
        if q + 1 < chunks:
            hand_on_p(q + 1)
        p_arrival(1, q).wait_recv()
        p_arrival(3, q).wait_recv()
        each(q * per, (q + 1) * per, 2, value)
        lax.fori_loop(max(q * per, 1), (q + 1) * per, back_start, 0)
    back[g] = mix[0]
    lax.fori_loop(1, ng, back_wait, 0)

    chosen = rank_col[...] == (lane // 32).astype(F32)
    slots_all = back[...].reshape(wide, 128)
    mixed = jnp.zeros((128, 256), F32)
    for b in range(8):
        rows_b = jnp.where(chosen, nn(picks[b], slots_all), 0.0).astype(BF16)
        mixed = mixed + nn(rows_b, fold[128 * b : 128 * b + 128, :])
    mixed = mixed.astype(BF16)

    loads[3].wait()

    def columns(h, e, c):
        part, dy = BLOCKS[e]
        block = part * 8 + lax.rem(y + dy, 4) * 2 + c
        return pl.ds(pl.multiple_of((block * 2 + h) * half, 128), half)

    def ta_copy(h, e):
        return pltpu.make_async_remote_copy(
            ta_send.at[h, e], ta_recv.at[h, e], ta_ssem.at[h, e], ta_rsem.at[h, e],
            device_id={"tp": mate(t, 1)}, device_id_type=MESH)

    before = t + 2 * ((y + 3) % 4 - y)
    after = t + 2 * ((y + 1) % 4 - y)
    targets = (before, after, after, before, before, after)

    def tb_copy(u, e):
        return pltpu.make_async_remote_copy(
            tb_send.at[u, e], tb_recv.at[u, e], tb_ssem.at[u, e], tb_rsem.at[u, e],
            device_id={"tp": targets[e]}, device_id_type=MESH)

    def tc_copy(u):
        return pltpu.make_async_remote_copy(
            tc_send.at[u], tc_recv.at[u], tc_ssem.at[u], tc_rsem.at[u],
            device_id={"tp": flip(t, 8)}, device_id_type=MESH)

    quarter = half // 2

    def first_step(h, pair):
        for e in pair:
            ta_send[h, e] = nn(mixed, wov[:, columns(h, e, 1 - core)]).astype(BF16)
            ta_copy(h, e).start()
        for e in pair:
            own[h, e] = nn(mixed, wov[:, columns(h, e, core)])

    def second_step(u, pair):
        h, at = u // 2, pl.ds((u % 2) * quarter, quarter)
        for e in pair:
            if u % 2 == 0:
                ta_copy(h, e).wait()
            summed = own[h, e, :, at] + ta_recv[h, e, :, at].astype(F32)
            if e in (4, 5):
                tb_copy(u, e - 4).wait()
                summed = summed + tb_recv[u, e - 4].astype(F32)
            if e < 6:
                tb_send[u, e] = summed.astype(BF16)
                tb_copy(u, e).start()
            else:
                fin[u, e - 6] = summed

    def last_step(u):
        second_step(u, kept)
        for e in (2, 3, 4, 5):
            tb_copy(u, e).wait()
        fin[u, 0] = fin[u, 0] + tb_recv[u, 2].astype(F32) + tb_recv[u, 4].astype(F32)
        fin[u, 1] = fin[u, 1] + tb_recv[u, 3].astype(F32) + tb_recv[u, 5].astype(F32)
        tc_send[u] = fin[u, 1 - zh].astype(BF16)
        tc_copy(u).start()

    opposite, direct, joined, kept = (0, 1), (2, 3), (4, 5), (6, 7)
    first_step(0, opposite)
    first_step(0, direct)
    second_step(0, opposite)
    second_step(1, opposite)
    first_step(0, joined)
    second_step(0, direct)
    first_step(1, opposite)
    second_step(0, joined)
    second_step(1, direct)
    second_step(1, joined)
    first_step(1, direct)
    second_step(2, opposite)
    second_step(3, opposite)
    first_step(1, joined)
    second_step(2, direct)
    first_step(0, kept)
    second_step(2, joined)
    second_step(3, direct)
    last_step(0)
    first_step(1, kept)
    second_step(3, joined)
    last_step(1)
    last_step(2)
    last_step(3)
    for u in range(4):
        tc_copy(u).wait()
        out_ref[:, u * quarter : (u + 1) * quarter] = (fin[u, zh] + tc_recv[u].astype(F32)).astype(BF16)

    def q_sent(k, _):
        q_copy(k).wait_send()
        return 0

    def q_shared(k, _):
        for o in (1, 2):
            q_share(o, k).wait_send()
        q_relay(k).wait_send()
        return 0

    lax.fori_loop(1, ng, q_sent, 0)
    lax.fori_loop(0, ng, q_shared, 0)
    for o in (1, 2, 3):
        for move in key_moves[o]:
            move.wait_send()
        st_moves[o - 1].wait_send()
    for q in range(chunks):
        p_copy(1, q).wait_send()
        p_copy(2, q).wait_send()
        p_relay(q).wait_send()
    for move in pn_moves:
        move.wait_send()


def rope_tables(step_count, cached, particles):
    pair = np.arange(64, dtype=np.float32).reshape(4, 16)
    frequency = np.exp(-(pair / np.float32(64)) * np.log(np.float32(500000.0))).astype(np.float32)
    positions = (cached + np.arange(step_count)).astype(np.float32)
    angles = (positions[None, None, :] * frequency[:, :, None]).astype(np.float32)
    tables = np.stack([np.cos(angles), np.sin(angles)]).astype(np.float32)
    return np.repeat(tables, particles, axis=-1)


def shards(ng, inputs, norm_gain, w_query, w_keyval, w_out, kv_cache, kv_scales, ancestors):
    step_count, particles, width = inputs.shape
    cached = kv_cache.shape[3]
    rope = jnp.asarray(rope_tables(step_count, cached, particles))
    missing = -ancestors.shape[0] % 128
    if missing:
        ancestors = jnp.pad(ancestors, (0, missing), constant_values=-1)
    rows = step_count * particles
    cb = width // lax.axis_size("tp")
    half = cb // 2
    vmem = pl.BlockSpec(memory_space=pltpu.VMEM)
    hbm = pl.BlockSpec(memory_space=pltpu.HBM)
    dma = pltpu.SemaphoreType.DMA
    scratch = [
        pltpu.VMEM((rows, width), BF16),
        pltpu.VMEM((320, width), BF16),
        pltpu.VMEM((256, width), BF16),
        pltpu.VMEM((width // 128, 128), BF16),
        pltpu.VMEM((width // 128, 128), F32),
        pltpu.VMEM((2, 16, 128), F32),
        pltpu.VMEM((8, 128), jnp.int32),
        pltpu.VMEM((8, 128), jnp.int32),
        pltpu.SMEM((8, 128), jnp.int32),
        pltpu.VMEM((128, 128), F32),
        pltpu.VMEM((128, 128), F32),
        pltpu.VMEM((320, 128), F32),
        pltpu.VMEM((320, 128), BF16),
        pltpu.VMEM((ng * 16, 2048), BF16),
        pltpu.VMEM((128, 2048), BF16),
        pltpu.VMEM((ng, 48, 128), BF16),
        pltpu.VMEM((4, ng, 48, 128), BF16),
        pltpu.VMEM((2, particles, 32, 128), BF16),
        pltpu.VMEM((2, particles, 32, 128), BF16),
        pltpu.VMEM((4, particles, 32, 128), BF16),
        pltpu.VMEM((4, particles, 128), BF16),
        pltpu.VMEM((4, particles, 128), F32),
        pltpu.VMEM((4, 2, particles, 128), BF16),
        pltpu.VMEM((4, 2, particles, 128), F32),
        pltpu.VMEM((ng, 128, 128), F32),
        pltpu.VMEM((4, ng, 128, 128), BF16),
        pltpu.VMEM((4, 128, 128), BF16),
        pltpu.VMEM((ng, 128, 16), F32),
        pltpu.VMEM((128, 128), F32),
        pltpu.VMEM((2 * ng, 128), F32),
        pltpu.VMEM((3, 2 * ng, 128), F32),
        pltpu.VMEM((4, ng, 128), F32),
        pltpu.VMEM((128, 128), F32),
        pltpu.VMEM((ng, 32, 128), BF16),
        pltpu.VMEM((ng, 32, 128), BF16),
        pltpu.VMEM((8, 128, 32 * ng), BF16),
        pltpu.VMEM((1024, 256), BF16),
        pltpu.VMEM((2, 8, rows, half), BF16),
        pltpu.VMEM((2, 8, rows, half), BF16),
        pltpu.VMEM((2, 8, rows, half), F32),
        pltpu.VMEM((4, 6, rows, half // 2), BF16),
        pltpu.VMEM((4, 6, rows, half // 2), BF16),
        pltpu.VMEM((4, 2, rows, half // 2), F32),
        pltpu.VMEM((4, rows, half // 2), BF16),
        pltpu.VMEM((4, rows, half // 2), BF16),
        dma((19,)),
        dma((3, PIECES + 1)), dma((3, PIECES + 1)),
        dma((3, MAX_CHUNKS)), dma((3, MAX_CHUNKS)),
        dma((3,)), dma((3,)),
        dma((ng,)), dma((ng,)),
        dma((3, ng)), dma((3, ng)),
        dma((3,)), dma((3,)),
        dma((ng,)), dma((ng,)),
        dma((2, 8)), dma((2, 8)),
        dma((4, 6)), dma((4, 6)),
        dma((4,)), dma((4,)),
    ]
    out = pl.pallas_call(
        functools.partial(kernel, ng),
        out_shape=pltpu.VMEM((rows, cb), BF16),
        in_specs=[hbm] * 9,
        out_specs=vmem,
        scratch_shapes=scratch,
        compiler_params=pltpu.CompilerParams(
            collective_id=0, has_side_effects=True, vmem_limit_bytes=60 * 1024 * 1024),
    )(
        inputs.reshape(rows, width),
        norm_gain.reshape(width // 128, 128),
        jnp.transpose(w_query, (1, 2, 0)).reshape(256, width),
        jnp.transpose(w_keyval, (1, 2, 0)).reshape(64, width),
        w_out.reshape(256, width),
        kv_cache,
        kv_scales.reshape(2, particles, cached),
        rope,
        ancestors.reshape(-1, 128),
    )
    return out.reshape(step_count, particles, cb)


def solution(mesh):
    in_specs = (
        P(None, "grp", None),
        P(),
        P(None, None, "tp"),
        P(None, None, "tp"),
        P(None, "tp", None),
        P(None, "grp", "tp", None),
        P(None, "grp", "tp", None),
        P(),
    )
    out_specs = P(None, "grp", "tp")
    return jax.shard_map(
        functools.partial(shards, mesh.shape["grp"]), mesh=mesh, in_specs=in_specs, out_specs=out_specs,
        check_vma=False)
```

```python
import functools

import jax
import jax.numpy as jnp
import numpy as np
from jax import lax
from jax.experimental import pallas as pl
from jax.experimental.pallas import tpu as pltpu
from jax.sharding import PartitionSpec as P

HD = 128
CAP = 4
MESH = pl.DeviceIdType.MESH
F32 = jnp.float32
BF16 = jnp.bfloat16
MAX_CHUNKS = 4
PIECES = 4
BLOCKS = ((0, 2), (1, 2), (0, 1), (1, 3), (0, 3), (1, 1), (0, 0), (1, 0))


def flip(t, bit):
    return t + bit - 2 * bit * ((t // bit) % 2)


def mate(t, offset):
    if offset & 1:
        t = flip(t, 1)
    if offset & 2:
        t = flip(t, 2)
    return t


def nt(a, b):
    return lax.dot_general(a, b, (((1,), (1,)), ((), ())), preferred_element_type=F32)


def nn(a, b):
    return jnp.dot(a, b, preferred_element_type=F32)


def iota(shape, axis):
    return lax.broadcasted_iota(jnp.int32, shape, axis)


def kernel(
    ng, x_hbm, gain_hbm, wq_hbm, wkv_hbm, wo_hbm, kv_hbm, sc_hbm, rope_hbm, anc_hbm,
    out_ref,
    xv, wv, wov, gain_v, gain_f, rope, anc, ids_v, ids_s, src_col, rank_col,
    accq, qt, onehot, spread, sendq, qx, kn, kf, vown, sv, svf, scx, scf, prob, px, pnp, pnew, stat, st_send, st_recv,
    facn, fac, mix, back, picks, fold, ta_send, ta_recv, own, tb_send, tb_recv, fin, tc_send, tc_recv,
    loc_sem, k_ssem, k_rsem, p_ssem, p_rsem, pn_ssem, pn_rsem, qa_ssem, qa_rsem, qg_ssem, qg_rsem, st_ssem, st_rsem,
    bk_ssem, bk_rsem, ta_ssem, ta_rsem, tb_ssem, tb_rsem, tc_ssem, tc_rsem,
):
    g = lax.axis_index("grp")
    t = lax.axis_index("tp")
    i = t % 4
    core = t % 2
    y = (t // 2) % 4
    zh = t // 8
    width = x_hbm.shape[1]
    half = out_ref.shape[1] // 2
    chunks = min(MAX_CHUNKS, ng)
    per = ng // chunks
    block_of = [mate(t, o) % 4 for o in range(4)]
    core_of = [core, 1 - core, core, 1 - core]

    loads = [
        pltpu.make_async_copy(x_hbm, xv, loc_sem.at[0]),
        pltpu.make_async_copy(wq_hbm, wv.at[pl.ds(0, 256)], loc_sem.at[1]),
        pltpu.make_async_copy(wkv_hbm, wv.at[pl.ds(256, 64)], loc_sem.at[2]),
        pltpu.make_async_copy(wo_hbm, wov, loc_sem.at[3]),
        pltpu.make_async_copy(anc_hbm, anc.at[pl.ds(0, anc_hbm.shape[0])], loc_sem.at[4]),
        pltpu.make_async_copy(gain_hbm, gain_v, loc_sem.at[5]),
        pltpu.make_async_copy(rope_hbm.at[:, i], rope, loc_sem.at[6]),
    ]
    anc[...] = jnp.full(anc.shape, -1, jnp.int32)
    for n in (4, 0, 5, 6, 1, 2):
        loads[n].start()

    barrier = pltpu.get_barrier_semaphore()
    tp_peers = [mate(t, 1), mate(t, 2), mate(t, 3), t + 2 * ((y + 3 - 2 * (y % 2)) % 4 - y), flip(t, 8)]

    def greet(k, _):
        pl.semaphore_signal(barrier, inc=1, device_id={"grp": lax.rem(g + k, ng)}, device_id_type=MESH)
        return 0

    for peer in tp_peers:
        pl.semaphore_signal(barrier, inc=1, device_id={"tp": peer}, device_id_type=MESH)
    lax.fori_loop(1, ng, greet, 0)
    pl.semaphore_wait(barrier, len(tp_peers) + ng - 1)

    def lanes_of(block):
        return pl.ds(pl.multiple_of(128 * block, 128), 128)

    def key_copies(o):
        args = dict(device_id={"tp": mate(t, o)}, device_id_type=MESH)
        lanes = lanes_of(block_of[o])
        piece = kv_hbm.shape[1] // PIECES
        pieces = [pl.ds(j * piece, piece) for j in range(PIECES)]
        held = kn if o == 1 else kf
        return [
            pltpu.make_async_remote_copy(
                kv_hbm.at[0, at, :, lanes], held.at[core, at], k_ssem.at[o - 1, j], k_rsem.at[o - 1, j], **args)
            for j, at in enumerate(pieces)
        ] + [
            pltpu.make_async_remote_copy(
                sc_hbm.at[:, :, lanes], scx.at[i], k_ssem.at[o - 1, PIECES], k_rsem.at[o - 1, PIECES], **args),
        ]

    key_moves = {o: key_copies(o) for o in (1, 2, 3)}
    for o in (2, 3, 1):
        key_moves[o][PIECES].start()
    for j in range(PIECES - 1):
        for o in (2, 3, 1):
            key_moves[o][j].start()
    key_moves[1][PIECES - 1].start()
    own_cache = [
        pltpu.make_async_copy(kv_hbm.at[0, :, :, lanes_of(i)], kn.at[core], loc_sem.at[7]),
        pltpu.make_async_copy(sc_hbm.at[:, :, lanes_of(i)], scx.at[i], loc_sem.at[8]),
    ]
    for b in range(4):
        at = pl.ds(128 * b, 128)
        own_cache.append(pltpu.make_async_copy(kv_hbm.at[1, :, :, at], vown.at[b], loc_sem.at[11 + b]))
        own_cache.append(pltpu.make_async_copy(sc_hbm.at[1, :, at], sv.at[b], loc_sem.at[15 + b]))
    for copy in own_cache:
        copy.start()
    loads[3].start()

    row = iota((128, 128), 0)
    lane = iota((128, 128), 1)

    def ones(where):
        return jnp.where(where, 1.0, 0.0).astype(BF16)

    loads[4].wait()
    parents = anc[...]
    source = parents >> 5
    wanted = source == g
    within = iota((8, 128), 1) % 32

    def running(v):
        for shift in (1, 2, 4, 8, 16):
            v = v + jnp.where(within >= shift, pltpu.roll(v, shift, 1), 0)
        return v

    place = running(wanted.astype(jnp.int32))
    ids = jnp.zeros((8, 128), jnp.int32)
    for c in range(CAP):
        at_slot = running(jnp.where(wanted & (place == c + 1), parents & 31, 0))
        ids = jnp.where(within == 32 - CAP + c, pltpu.roll(at_slot, (c + 1 - CAP) % 128, 1), ids)
    ids_v[...] = ids
    to_scalars = pltpu.make_async_copy(ids_v, ids_s, loc_sem.at[10])
    to_scalars.start()
    mine = jnp.sum(jnp.where(iota((8, 128), 0) == g // 4, source.astype(F32), 0.0), axis=0, keepdims=True)
    mine = nn(jnp.broadcast_to(mine, (8, 128)).astype(BF16), ones(row == (g % 4) * 32 + lane % 32))[0:1]
    mine = jnp.broadcast_to(mine, (128, 128))
    mine_col = jnp.transpose(mine)
    src_col[...] = mine_col
    rank = jnp.sum(jnp.where((mine == mine_col) & (row < lane % 32), 1.0, 0.0), axis=0, keepdims=True)
    rank_col[...] = jnp.transpose(jnp.broadcast_to(rank, (128, 128)))

    slot_row = iota((ng * 16, 128), 0)
    slot_lane = iota((ng * 16, 128), 1)
    hit = (mine[0:1] == (slot_row // 16).astype(F32)) & (slot_row % 4 == slot_lane // 32)
    for c in range(CAP):
        hit_c = hit & (rank == c)
        for gl in range(4):
            onehot[:, (c * 4 + gl) * 128 : (c * 4 + gl + 1) * 128] = ones(hit_c & ((slot_row // 4) % 4 == gl))
    spread[...] = jnp.zeros_like(spread)

    loads[5].wait()
    gain_f[...] = gain_v[...].astype(F32)
    loads[0].wait()
    step = min(1024, width)

    def squares(k, total):
        part = xv[:, pl.ds(pl.multiple_of(k * step, step), step)].astype(F32)
        return total + jnp.sum(part * part, axis=1, keepdims=True)

    total = lax.fori_loop(0, width // step, squares, jnp.zeros((128, 1), F32))
    inv = lax.rsqrt(total / width + 1e-05)
    loads[1].wait()
    loads[2].wait()
    accq[...] = jnp.zeros_like(accq)

    def project(k, _):
        part = pl.ds(pl.multiple_of(k * step, step), step)
        gains = gain_f[pl.ds(pl.multiple_of(k * (step // 128), 8), step // 128), :]
        gains = jnp.concatenate([gains[r : r + 1] for r in range(step // 128)], axis=1)
        normed = (xv[:, part].astype(F32) * inv * gains).astype(BF16)
        accq[...] += nt(wv[:, part], normed)
        return 0

    lax.fori_loop(0, width // step, project, 0)
    loads[6].wait()
    cosine = rope[0]
    sine = rope[1]
    for b in range(9):
        front = accq[32 * b : 32 * b + 16, :]
        rear = accq[32 * b + 16 : 32 * b + 32, :]
        new_front = front * cosine - rear * sine
        new_rear = rear * cosine + front * sine
        if b < 8:
            new_front = new_front * HD ** (-0.5)
            new_rear = new_rear * HD ** (-0.5)
        qt[32 * b : 32 * b + 16, :] = new_front.astype(BF16)
        qt[32 * b + 16 : 32 * b + 32, :] = new_rear.astype(BF16)
    qt[288:320, :] = accq[288:320, :].astype(BF16)

    for third in range(3):
        for c in range(CAP):
            for gl in range(4):
                at = pl.ds((c * 4 + gl) * 128, 128)
                b = third * 4 + gl
                if b < 10:
                    spread[32 * c : 32 * c + 32, at] = qt[32 * b : 32 * b + 32, :]
                else:
                    spread[32 * c : 32 * c + 32, at] = jnp.zeros((32, 128), BF16)
        packed = nt(onehot[...], spread[...]).astype(BF16)
        sendq[:, 16 * third : 16 * third + 16, :] = packed.reshape(ng, 16, 128)

    def q_copy(k):
        there = lax.rem(g + k, ng)
        return pltpu.make_async_remote_copy(
            sendq.at[there], qx.at[i, g], qa_ssem.at[k], qa_rsem.at[k],
            device_id={"grp": there}, device_id_type=MESH)

    def q_share(o, k):
        here = lax.rem(g - k + ng, ng)
        return pltpu.make_async_remote_copy(
            qx.at[i, here], qx.at[i, here], qg_ssem.at[o - 1, k], qg_rsem.at[o - 1, k],
            device_id={"tp": mate(t, o)}, device_id_type=MESH)

    def q_arrival(o, k):
        here = lax.rem(g - k + ng, ng)
        return pltpu.make_async_remote_copy(
            qx.at[i, here], qx.at[block_of[o], here], qg_ssem.at[o - 1, k], qg_rsem.at[o - 1, k],
            device_id={"tp": mate(t, o)}, device_id_type=MESH)

    def q_start(k, _):
        q_copy(k).start()
        return 0

    def q_forward(k, _):
        q_copy(k).wait_recv()
        for o in (2, 1):
            q_share(o, k).start()
        return 0

    def q_relay(k):
        here = lax.rem(g - k + ng, ng)
        return pltpu.make_async_remote_copy(
            qx.at[block_of[2], here], qx.at[block_of[2], here], qg_ssem.at[2, k], qg_rsem.at[2, k],
            device_id={"tp": mate(t, 1)}, device_id_type=MESH)

    def hand_on(k):
        q_arrival(2, k).wait_recv()
        q_relay(k).start()

    lax.fori_loop(1, ng, q_start, 0)
    qx[i, g] = sendq[g]
    for o in (2, 1):
        q_share(o, 0).start()
    lax.fori_loop(1, ng, q_forward, 0)
    for o in (2, 3):
        key_moves[o][PIECES - 1].start()

    fold_row = iota(fold.shape, 0)
    fold_lane = iota(fold.shape, 1)
    fold[...] = ones((fold_row // 128 == fold_lane // 32) & (fold_row % 32 == fold_lane % 32))
    wide = 32 * ng
    row_w = iota((128, wide), 0)
    lane_w = iota((128, wide), 1)
    hit = ((lane_w // 32).astype(F32) == src_col[:, 0:1]) & (lane_w % 4 == row_w // 32)
    for b in range(8):
        picks[b] = ones(hit & ((lane_w // 4) % 8 == b))
    diagonal = ones(row // 32 == lane // 32)
    stat[...] = jnp.zeros_like(stat)
    to_scalars.wait()

    def slots(k):
        there = lax.rem(g - k + ng, ng)
        return there, [ids_s[there // 4, (there % 4) * 32 + 32 - CAP + c] & 31 for c in range(CAP)]

    def scale_rows(n, kind, ids):
        return jnp.concatenate(
            [jnp.broadcast_to(scf[n, kind, pl.ds(ids[c], 1), :], (32, 128)) for c in range(CAP)], axis=0)

    def queries(n, there):
        return jnp.concatenate([qx[n, there, 0:32, :]] * CAP, axis=0) * diagonal

    def block_scores(o, there, ids):
        n = block_of[o]
        held = kn if o < 2 else kf
        keys = jnp.concatenate([held[core_of[o], ids[c]] for c in range(CAP)], axis=0)
        return nn(queries(n, there), keys) * scale_rows(n, 0, ids)

    own_cache[0].wait()
    own_cache[1].wait()
    for move in key_moves[1]:
        move.wait_recv()
    key_moves[2][PIECES].wait_recv()
    key_moves[3][PIECES].wait_recv()
    scf[...] = scx[...].astype(F32)

    def each(first, last, width, body):
        width = min(width, last - first)

        def run(j, _):
            body([first + j * width + d for d in range(width)])
            return 0

        lax.fori_loop(0, (last - first) // width, run, 0)

    def score_near(ks):
        for k in ks:
            q_arrival(1, k).wait_recv()
        totals = []
        for k in ks:
            there, ids = slots(k)
            totals.append(block_scores(0, there, ids) + block_scores(1, there, ids))
        for k, total in zip(ks, totals):
            prob[k] = total

    each(0, ng, 4, score_near)

    def hand_all(k, _):
        hand_on(k)
        return 0

    lax.fori_loop(0, ng, hand_all, 0)
    pnew[...] = jnp.full(pnew.shape, -jnp.inf, F32)

    def far_arrival(k, _):
        q_arrival(3, k).wait_recv()
        return 0

    lax.fori_loop(0, ng, far_arrival, 0)
    first_new = (g - i + 4 * ng) % 4
    share = max(ng // 4, 1)

    column = iota((128, 16), 1)
    seen = (column <= iota((128, 16), 0) % 4) & (column < 4)
    news = []
    for j in range(share):
        k = lax.rem(first_new + 4 * j, ng)
        there, _ = slots(k)
        new = jnp.zeros((128, 16), F32)
        for n in range(4):
            new = new + nt(queries(n, there), qx[n, there, 32:48, :])
        mine_too = seen & (there == i) if ng < 4 else seen
        news.append((k, jnp.where(mine_too, new, -jnp.inf)))
    for k, new in news:
        pnew[k] = new

    def score_far(ks):
        done = []
        for k in ks:
            there, ids = slots(k)
            total = prob[k] + block_scores(2, there, ids) + block_scores(3, there, ids)
            new = pnew[k]
            top = jnp.maximum(jnp.max(total, axis=1, keepdims=True), jnp.max(new, axis=1, keepdims=True))
            part = jnp.exp(total - top)
            new = jnp.exp(new - top)
            mass = jnp.sum(part, axis=1, keepdims=True) + jnp.sum(new, axis=1, keepdims=True)
            done.append((part, new, top, mass))
        both = stat[...]
        for k, (part, new, top, mass) in zip(ks, done):
            px[i, k] = part.astype(BF16)
            pnew[k] = new
            both = jnp.where(lane == k, top, jnp.where(lane == ng + k, mass, both))
        stat[...] = both

    for o in (2, 3):
        for move in key_moves[o][:PIECES]:
            move.wait_recv()

    def p_at(q):
        return pl.ds(q * per, per)

    def p_copy(o, q):
        return pltpu.make_async_remote_copy(
            px.at[i, p_at(q)], px.at[i, p_at(q)], p_ssem.at[o - 1, q], p_rsem.at[o - 1, q],
            device_id={"tp": mate(t, o)}, device_id_type=MESH)

    def p_arrival(o, q):
        return pltpu.make_async_remote_copy(
            px.at[i, p_at(q)], px.at[block_of[o], p_at(q)], p_ssem.at[o - 1, q], p_rsem.at[o - 1, q],
            device_id={"tp": mate(t, o)}, device_id_type=MESH)

    def p_relay(q):
        return pltpu.make_async_remote_copy(
            px.at[block_of[2], p_at(q)], px.at[block_of[2], p_at(q)], p_ssem.at[2, q], p_rsem.at[2, q],
            device_id={"tp": mate(t, 1)}, device_id_type=MESH)

    for q in range(chunks):
        each(q * per, (q + 1) * per, 4, score_far)
        if q == 0:
            p_copy(2, q).start()
            p_copy(1, q).start()
    packed = jnp.zeros((128, 128), F32)
    for j in range(share):
        new = pnew[lax.rem(first_new + 4 * j, ng)]
        packed = jnp.where(lane // 16 == j, jnp.concatenate([new] * 8, axis=1), packed)
    pnp[i] = packed.astype(BF16)
    pn_moves = [
        pltpu.make_async_remote_copy(
            pnp.at[i], pnp.at[i], pn_ssem.at[o - 1], pn_rsem.at[o - 1],
            device_id={"tp": mate(t, o)}, device_id_type=MESH)
        for o in (1, 2, 3)
    ]
    pn_arrivals = [
        pltpu.make_async_remote_copy(
            pnp.at[i], pnp.at[block_of[o]], pn_ssem.at[o - 1], pn_rsem.at[o - 1],
            device_id={"tp": mate(t, o)}, device_id_type=MESH)
        for o in (1, 2, 3)
    ]

    st_send[...] = jnp.transpose(stat[...])[0 : 2 * ng, :]
    st_moves = [
        pltpu.make_async_remote_copy(
            st_send, st_recv.at[o - 1], st_ssem.at[o - 1], st_rsem.at[o - 1],
            device_id={"tp": mate(t, o)}, device_id_type=MESH)
        for o in (1, 2, 3)
    ]
    for o in (2, 1, 0):
        st_moves[o].start()
    for o in (2, 1, 0):
        pn_moves[o].start()
    for q in range(1, chunks):
        p_copy(2, q).start()
        p_copy(1, q).start()
    for copy in own_cache[2:]:
        copy.wait()
    svf[...] = sv[...].astype(F32)
    for o in range(3):
        st_moves[o].wait_recv()
        pn_arrivals[o].wait_recv()
    tops = [st_send[0:ng, :]] + [st_recv[o, 0:ng, :] for o in range(3)]
    masses = [st_send[ng : 2 * ng, :]] + [st_recv[o, ng : 2 * ng, :] for o in range(3)]
    top = jnp.maximum(jnp.maximum(tops[0], tops[1]), jnp.maximum(tops[2], tops[3]))
    mass = sum(masses[o] * jnp.exp(tops[o] - top) for o in range(4))
    for o in range(4):
        facn[block_of[o]] = jnp.exp(tops[o] - top) / mass
    factors = [facn[n] for n in range(4)]
    if 4 * ng < 128:
        factors.append(jnp.zeros((128 - 4 * ng, 128), F32))
    fac[...] = jnp.transpose(jnp.concatenate(factors, axis=0))

    def keep(out):
        kept = jnp.zeros((32, 128), F32)
        for c in range(CAP):
            kept = kept + jnp.where(lane[0:32] // 32 == c, out[32 * c : 32 * c + 32, :], 0.0)
        return kept

    def factor_of(n, k):
        return jnp.sum(jnp.where(lane == n * ng + k, fac[...], 0.0), axis=1, keepdims=True)

    def value(ks):
        kept = []
        for k in ks:
            there, ids = slots(k)
            out = jnp.zeros((128, 128), F32)
            for n in range(4):
                scales = jnp.concatenate(
                    [jnp.broadcast_to(svf[n, pl.ds(ids[c], 1), :], (32, 128)) for c in range(CAP)], axis=0)
                weighted = (px[n, k].astype(F32) * factor_of(n, k) * scales).astype(BF16)
                values = jnp.concatenate([vown[n, ids[c]] for c in range(CAP)], axis=0)
                out = out + nt(weighted, values)
            n = there % 4
            new_probs = (pnp[n].astype(F32) * factor_of(n, k)).astype(BF16)
            both = pltpu.roll(qx[i, there, 32:48, :].astype(F32), 12, 0)
            new_values = jnp.where(row // 16 == k // 4, jnp.concatenate([both] * 8, axis=0), 0.0).astype(BF16)
            kept.append(keep(out + nn(new_probs, new_values)).astype(BF16))
        for k, out in zip(ks, kept):
            mix[k] = out

    def back_copy(k):
        there = lax.rem(g - k + ng, ng)
        return pltpu.make_async_remote_copy(
            mix.at[k], back.at[g], bk_ssem.at[k], bk_rsem.at[k],
            device_id={"grp": there}, device_id_type=MESH)

    def back_start(k, _):
        back_copy(k).start()
        return 0

    def back_wait(k, _):
        back_copy(k).wait()
        return 0

    def hand_on_p(q):
        p_arrival(2, q).wait_recv()
        p_relay(q).start()

    hand_on_p(0)
    for q in range(chunks):
        if q + 1 < chunks:
            hand_on_p(q + 1)
        p_arrival(1, q).wait_recv()
        p_arrival(3, q).wait_recv()
        each(q * per, (q + 1) * per, 4, value)
        lax.fori_loop(max(q * per, 1), (q + 1) * per, back_start, 0)
    back[g] = mix[0]
    lax.fori_loop(1, ng, back_wait, 0)

    chosen = rank_col[...] == (lane // 32).astype(F32)
    slots_all = back[...].reshape(wide, 128)
    mixed = jnp.zeros((128, 256), F32)
    for b in range(8):
        rows_b = jnp.where(chosen, nn(picks[b], slots_all), 0.0).astype(BF16)
        mixed = mixed + nn(rows_b, fold[128 * b : 128 * b + 128, :])
    mixed = mixed.astype(BF16)

    loads[3].wait()

    def columns(h, e, c):
        part, dy = BLOCKS[e]
        block = part * 8 + lax.rem(y + dy, 4) * 2 + c
        return pl.ds(pl.multiple_of((block * 2 + h) * half, 128), half)

    def ta_copy(h, e):
        return pltpu.make_async_remote_copy(
            ta_send.at[h, e], ta_recv.at[h, e], ta_ssem.at[h, e], ta_rsem.at[h, e],
            device_id={"tp": mate(t, 1)}, device_id_type=MESH)

    before = t + 2 * ((y + 3) % 4 - y)
    after = t + 2 * ((y + 1) % 4 - y)
    targets = (before, after, after, before, before, after)

    def tb_copy(u, e):
        return pltpu.make_async_remote_copy(
            tb_send.at[u, e], tb_recv.at[u, e], tb_ssem.at[u, e], tb_rsem.at[u, e],
            device_id={"tp": targets[e]}, device_id_type=MESH)

    def tc_copy(u):
        return pltpu.make_async_remote_copy(
            tc_send.at[u], tc_recv.at[u], tc_ssem.at[u], tc_rsem.at[u],
            device_id={"tp": flip(t, 8)}, device_id_type=MESH)

    quarter = half // 2

    def first_step(h, pair):
        for e in pair:
            ta_send[h, e] = nn(mixed, wov[:, columns(h, e, 1 - core)]).astype(BF16)
            ta_copy(h, e).start()
        for e in pair:
            own[h, e] = nn(mixed, wov[:, columns(h, e, core)])

    def second_step(u, pair):
        h, at = u // 2, pl.ds((u % 2) * quarter, quarter)
        for e in pair:
            if u % 2 == 0:
                ta_copy(h, e).wait()
            summed = own[h, e, :, at] + ta_recv[h, e, :, at].astype(F32)
            if e in (4, 5):
                tb_copy(u, e - 4).wait()
                summed = summed + tb_recv[u, e - 4].astype(F32)
            if e < 6:
                tb_send[u, e] = summed.astype(BF16)
                tb_copy(u, e).start()
            else:
                fin[u, e - 6] = summed

    def last_step(u):
        second_step(u, kept)
        for e in (2, 3, 4, 5):
            tb_copy(u, e).wait()
        fin[u, 0] = fin[u, 0] + tb_recv[u, 2].astype(F32) + tb_recv[u, 4].astype(F32)
        fin[u, 1] = fin[u, 1] + tb_recv[u, 3].astype(F32) + tb_recv[u, 5].astype(F32)
        tc_send[u] = fin[u, 1 - zh].astype(BF16)
        tc_copy(u).start()

    opposite, direct, joined, kept = (0, 1), (2, 3), (4, 5), (6, 7)
    first_step(0, opposite)
    first_step(0, direct)
    second_step(0, opposite)
    second_step(1, opposite)
    first_step(0, joined)
    second_step(0, direct)
    first_step(1, opposite)
    second_step(0, joined)
    second_step(1, direct)
    second_step(1, joined)
    first_step(1, direct)
    second_step(2, opposite)
    second_step(3, opposite)
    first_step(1, joined)
    second_step(2, direct)
    first_step(0, kept)
    second_step(2, joined)
    second_step(3, direct)
    last_step(0)
    first_step(1, kept)
    second_step(3, joined)
    last_step(1)
    last_step(2)
    last_step(3)
    for u in range(4):
        tc_copy(u).wait()
        out_ref[:, u * quarter : (u + 1) * quarter] = (fin[u, zh] + tc_recv[u].astype(F32)).astype(BF16)

    def q_sent(k, _):
        q_copy(k).wait_send()
        return 0

    def q_shared(k, _):
        for o in (1, 2):
            q_share(o, k).wait_send()
        q_relay(k).wait_send()
        return 0

    lax.fori_loop(1, ng, q_sent, 0)
    lax.fori_loop(0, ng, q_shared, 0)
    for o in (1, 2, 3):
        for move in key_moves[o]:
            move.wait_send()
        st_moves[o - 1].wait_send()
    for q in range(chunks):
        p_copy(1, q).wait_send()
        p_copy(2, q).wait_send()
        p_relay(q).wait_send()
    for move in pn_moves:
        move.wait_send()


def rope_tables(step_count, cached, particles):
    pair = np.arange(64, dtype=np.float32).reshape(4, 16)
    frequency = np.exp(-(pair / np.float32(64)) * np.log(np.float32(500000.0))).astype(np.float32)
    positions = (cached + np.arange(step_count)).astype(np.float32)
    angles = (positions[None, None, :] * frequency[:, :, None]).astype(np.float32)
    tables = np.stack([np.cos(angles), np.sin(angles)]).astype(np.float32)
    return np.repeat(tables, particles, axis=-1)


def shards(ng, inputs, norm_gain, w_query, w_keyval, w_out, kv_cache, kv_scales, ancestors):
    step_count, particles, width = inputs.shape
    cached = kv_cache.shape[3]
    rope = jnp.asarray(rope_tables(step_count, cached, particles))
    missing = -ancestors.shape[0] % 128
    if missing:
        ancestors = jnp.pad(ancestors, (0, missing), constant_values=-1)
    rows = step_count * particles
    cb = width // lax.axis_size("tp")
    half = cb // 2
    vmem = pl.BlockSpec(memory_space=pltpu.VMEM)
    hbm = pl.BlockSpec(memory_space=pltpu.HBM)
    dma = pltpu.SemaphoreType.DMA
    scratch = [
        pltpu.VMEM((rows, width), BF16),
        pltpu.VMEM((320, width), BF16),
        pltpu.VMEM((256, width), BF16),
        pltpu.VMEM((width // 128, 128), BF16),
        pltpu.VMEM((width // 128, 128), F32),
        pltpu.VMEM((2, 16, 128), F32),
        pltpu.VMEM((8, 128), jnp.int32),
        pltpu.VMEM((8, 128), jnp.int32),
        pltpu.SMEM((8, 128), jnp.int32),
        pltpu.VMEM((128, 128), F32),
        pltpu.VMEM((128, 128), F32),
        pltpu.VMEM((320, 128), F32),
        pltpu.VMEM((320, 128), BF16),
        pltpu.VMEM((ng * 16, 2048), BF16),
        pltpu.VMEM((128, 2048), BF16),
        pltpu.VMEM((ng, 48, 128), BF16),
        pltpu.VMEM((4, ng, 48, 128), BF16),
        pltpu.VMEM((2, particles, 32, 128), BF16),
        pltpu.VMEM((2, particles, 32, 128), BF16),
        pltpu.VMEM((4, particles, 32, 128), BF16),
        pltpu.VMEM((4, particles, 128), BF16),
        pltpu.VMEM((4, particles, 128), F32),
        pltpu.VMEM((4, 2, particles, 128), BF16),
        pltpu.VMEM((4, 2, particles, 128), F32),
        pltpu.VMEM((ng, 128, 128), F32),
        pltpu.VMEM((4, ng, 128, 128), BF16),
        pltpu.VMEM((4, 128, 128), BF16),
        pltpu.VMEM((ng, 128, 16), F32),
        pltpu.VMEM((128, 128), F32),
        pltpu.VMEM((2 * ng, 128), F32),
        pltpu.VMEM((3, 2 * ng, 128), F32),
        pltpu.VMEM((4, ng, 128), F32),
        pltpu.VMEM((128, 128), F32),
        pltpu.VMEM((ng, 32, 128), BF16),
        pltpu.VMEM((ng, 32, 128), BF16),
        pltpu.VMEM((8, 128, 32 * ng), BF16),
        pltpu.VMEM((1024, 256), BF16),
        pltpu.VMEM((2, 8, rows, half), BF16),
        pltpu.VMEM((2, 8, rows, half), BF16),
        pltpu.VMEM((2, 8, rows, half), F32),
        pltpu.VMEM((4, 6, rows, half // 2), BF16),
        pltpu.VMEM((4, 6, rows, half // 2), BF16),
        pltpu.VMEM((4, 2, rows, half // 2), F32),
        pltpu.VMEM((4, rows, half // 2), BF16),
        pltpu.VMEM((4, rows, half // 2), BF16),
        dma((19,)),
        dma((3, PIECES + 1)), dma((3, PIECES + 1)),
        dma((3, MAX_CHUNKS)), dma((3, MAX_CHUNKS)),
        dma((3,)), dma((3,)),
        dma((ng,)), dma((ng,)),
        dma((3, ng)), dma((3, ng)),
        dma((3,)), dma((3,)),
        dma((ng,)), dma((ng,)),
        dma((2, 8)), dma((2, 8)),
        dma((4, 6)), dma((4, 6)),
        dma((4,)), dma((4,)),
    ]
    out = pl.pallas_call(
        functools.partial(kernel, ng),
        out_shape=pltpu.VMEM((rows, cb), BF16),
        in_specs=[hbm] * 9,
        out_specs=vmem,
        scratch_shapes=scratch,
        compiler_params=pltpu.CompilerParams(
            collective_id=0, has_side_effects=True, vmem_limit_bytes=60 * 1024 * 1024),
    )(
        inputs.reshape(rows, width),
        norm_gain.reshape(width // 128, 128),
        jnp.transpose(w_query, (1, 2, 0)).reshape(256, width),
        jnp.transpose(w_keyval, (1, 2, 0)).reshape(64, width),
        w_out.reshape(256, width),
        kv_cache,
        kv_scales.reshape(2, particles, cached),
        rope,
        ancestors.reshape(-1, 128),
    )
    return out.reshape(step_count, particles, cb)


def solution(mesh):
    in_specs = (
        P(None, "grp", None),
        P(),
        P(None, None, "tp"),
        P(None, None, "tp"),
        P(None, "tp", None),
        P(None, "grp", "tp", None),
        P(None, "grp", "tp", None),
        P(),
    )
    out_specs = P(None, "grp", "tp")
    return jax.shard_map(
        functools.partial(shards, mesh.shape["grp"]), mesh=mesh, in_specs=in_specs, out_specs=out_specs,
        check_vma=False)
```
